32 devices in a mesh: batch: 16 (over z, x, core), seq: 2 (over y).
Axes of the slice: x: 2, y: 2, z: 4, core: 2. Of those that a mesh axis runs over, the one named last changes fastest.
Arguments:
- inputs: bfloat16 [64, 128, 768], P('batch', 'seq'), may hold values from -6 to 6
- time_embed: bfloat16 [64, 768], P('batch'), may hold values from -3 to 3
- segment_ids: int32 [64, 128], P('batch'), may hold values from 0 to 3, never falling along the last dimension, each value on 1 to 64 neighbouring positions
- cotangent: bfloat16 [64, 128, 768], P('batch', 'seq'), may hold values from -6 to 6
- first_gain: bfloat16 [768], P(('batch', 'seq')), may hold values from 0.5 to 1.5
- first_shift: bfloat16 [768], P(('batch', 'seq')), may hold values from -1.5 to 1.5
- mix_weight: bfloat16 [768, 2304], P(('batch', 'seq')), may hold values from -0.21875 to 0.21875
- mix_bias: bfloat16 [1536], P(('batch', 'seq')), may hold values from -1.5 to 1.5
- out_weight: bfloat16 [768, 768], P(('batch', 'seq')), may hold values from -1.25 to 1.25
- out_bias: bfloat16 [768], P(('batch', 'seq')), may hold values from -1.5 to 1.5
- second_gain: bfloat16 [768], P(('batch', 'seq')), may hold values from 0.5 to 1.5
- second_shift: bfloat16 [768], P(('batch', 'seq')), may hold values from -1.5 to 1.5
- up_weight: bfloat16 [768, 3072], P(('batch', 'seq')), may hold values from -0.21875 to 0.21875
- up_bias: bfloat16 [3072], P(('batch', 'seq')), may hold values from -1.5 to 1.5
- down_weight: bfloat16 [3072, 768], P(('batch', 'seq')), may hold values from -0.109375 to 0.109375
- down_bias: bfloat16 [768], P(('batch', 'seq')), may hold values from -1.5 to 1.5
Outputs:
- layer_out: bfloat16 [64, 128, 768], P('batch', 'seq')
- inputs_grad: float32 [64, 128, 768], P('batch', 'seq')
- time_grad: float32 [64, 768], P('batch', 'seq')
- first_gain_grad: float32 [768], P(('batch', 'seq'))
- first_shift_grad: float32 [768], P(('batch', 'seq'))
- mix_weight_grad: float32 [768, 2304], P(('batch', 'seq'))
- mix_bias_grad: float32 [1536], P(('batch', 'seq'))
- out_weight_grad: float32 [768, 768], P(('batch', 'seq'))
- out_bias_grad: float32 [768], P(('batch', 'seq'))
- second_gain_grad: float32 [768], P(('batch', 'seq'))
- second_shift_grad: float32 [768], P(('batch', 'seq'))
- up_weight_grad: float32 [768, 3072], P(('batch', 'seq'))
- up_bias_grad: float32 [3072], P(('batch', 'seq'))
- down_weight_grad: float32 [3072, 768], P(('batch', 'seq'))
- down_bias_grad: float32 [768], P(('batch', 'seq'))
The draws below stay inside these ranges and needn't reach their ends.
Inputs may be any that keep to these rules, and one draw needn't show every extreme that they name: `segment_ids`: in each row of 128 positions the ids never fall, every id appears, and a document spans 1 to 64 positions.
All inputs are finite; a program needn't handle non-finite values.
Results may differ from the reference program's by a relative error of at most 0.0096.
Values may be sent and summed in bfloat16 or wider, within the bound.
A program may use at most 192 MiB of HBM per device.

```python
import math
from functools import partial
import jax
import jax.numpy as jnp
import numpy as np
from jax import lax

D = 768
HEADS = 12
HEAD_DIM = 64
FF = 3072
LEN = 128
SEGMENTS = 4
ROWS = 64


def raised(entries, own_key, source, target, parts, factor):
    def block_of(axis_at):
        return (jnp.arange(entries.shape[axis_at]) // (entries.shape[axis_at] // parts)).reshape((-1,) + (1,) * (entries.ndim - 1 - axis_at))

    one_side = jax.random.permutation(own_key, parts)[block_of(target)]
    far = (block_of(target) + parts // 2) % parts
    return jnp.where((block_of(source) == one_side) | (block_of(source) == far), factor * entries, entries)


def level_of(stream_key, extent, split, least, high):
    factor_of = 1.0
    for axis_at, shards_of in split:
        draws = jax.random.uniform(jax.random.fold_in(jax.random.fold_in(stream_key, 6), axis_at), (shards_of,), jnp.float32, least / len(split), high / len(split))
        factor_of = factor_of * jnp.repeat(jnp.exp(draws), extent[axis_at] // shards_of).reshape((-1,) + (1,) * (len(extent) - 1 - axis_at))
    return factor_of


def length_profile(number_of, total, bound, lean):
    loads = [(1 << 20) // math.isqrt(standing ** lean) + 1 for standing in range(2, number_of + 1)]
    rest, holding = total - bound - (number_of - 1), [1] * (number_of - 1)
    while rest > 0:
        movable = [i for i in range(number_of - 1) if holding[i] < bound]
        mass, remaining = sum([loads[i] for i in movable]), rest
        for i in movable:
            more = min(bound - holding[i], max(1, remaining * loads[i] // mass), rest)
            holding[i] = holding[i] + more
            rest = rest - more
    return np.array([bound] + holding)


def uneven(own_key, amount, total, bound, lean):
    if amount == 2:
        one = jax.random.randint(own_key, (), max(1, total - bound), min(bound, total - 1) + 1)
        return jnp.stack([one, total - one])
    tallies = jnp.asarray(length_profile(amount, total, bound, lean), jnp.int32)
    couples = (amount - 1) // 2
    donor, sink = tallies[1:1 + 2 * couples:2], tallies[2:2 + 2 * couples:2]
    room = jnp.minimum(donor - 1, bound - sink)
    moved = jax.random.randint(jax.random.fold_in(own_key, 1), (couples,), 0, 1 << 20) % (room + 1)
    tallies = tallies.at[1:1 + 2 * couples:2].set(donor - moved).at[2:2 + 2 * couples:2].set(sink + moved)
    return tallies[jax.random.permutation(jax.random.fold_in(own_key, 2), amount)]


def bell_draw(stream_key, dims, scale, limit, pieces=(), kind=jnp.bfloat16):
    gain = level_of(stream_key, dims, pieces, -0.22, 0.18) if pieces else 1.0
    result = jax.random.normal(stream_key, dims, jnp.float32) * scale * gain
    return jnp.minimum(jnp.maximum(result, -limit), limit).astype(kind)


def bell_draw_with(own_key, extent, scale, limit, pieces, heavy, dtype=jnp.bfloat16):
    result = scale * jax.random.normal(own_key, extent, jnp.float32)
    if pieces:
        result = result * level_of(own_key, extent, pieces, -0.22, 0.18)
    return jnp.clip(raised(result, jax.random.fold_in(own_key, 3), *heavy), -limit, limit).astype(dtype)


def setup_inputs(seed: int = 0) -> dict:
    streams_of = jax.random.split(jax.random.key(seed), 17)
    return {
        "inputs": bell_draw_with(streams_of[0], (ROWS, LEN, D), 1.0, 6.0, ((0, 16), (1, 2)), (0, 2, 16, 2.0)),
        "time_embed": bell_draw(streams_of[1], (ROWS, D), 0.5, 3.0, ((0, 16),)),
        "segment_ids": jax.vmap(lambda own: jnp.searchsorted(jnp.cumsum(uneven(own, SEGMENTS, LEN, LEN // 2, 0)), jnp.arange(LEN), side="right"))(jax.random.split(streams_of[2], ROWS)).reshape((ROWS, LEN)).astype(jnp.int32),
        "cotangent": bell_draw(streams_of[3], (ROWS, LEN, D), 1.0, 6.0, ((0, 16), (1, 2))),
        "first_gain": jnp.clip(1.0 + 0.1 * jax.random.normal(streams_of[4], (D,), jnp.float32), 0.5, 1.5).astype(jnp.bfloat16),
        "first_shift": bell_draw(streams_of[5], (D,), 0.3, 1.5, ((0, 32),)),
        "mix_weight": bell_draw(streams_of[6], (D, 3 * D), D ** -0.5, 0.21875, ((0, 32),)),
        "mix_bias": bell_draw(streams_of[7], (2 * D,), 0.3, 1.5, ((0, 32),)),
        "out_weight": bell_draw(streams_of[8], (D, D), (D // 32) ** -0.5, 1.25, ((0, 32),)),
        "out_bias": bell_draw(streams_of[9], (D,), 0.3, 1.5, ((0, 32),)),
        "second_gain": jnp.clip(1.0 + 0.1 * jax.random.normal(streams_of[10], (D,), jnp.float32), 0.5, 1.5).astype(jnp.bfloat16),
        "second_shift": bell_draw(streams_of[11], (D,), 0.3, 1.5, ((0, 32),)),
        "up_weight": bell_draw(streams_of[12], (D, FF), D ** -0.5, 0.21875, ((0, 32),)),
        "up_bias": bell_draw(streams_of[13], (FF,), 0.3, 1.5, ((0, 32),)),
        "down_weight": bell_draw(streams_of[14], (FF, D), FF ** -0.5, 0.109375, ((0, 32),)),
        "down_bias": bell_draw(streams_of[15], (D,), 0.3, 1.5, ((0, 32),)),
    }


@jax.custom_vjp
def low(v):
    return lax.optimization_barrier(v.astype(jnp.bfloat16)).astype(jnp.float32)

@jax.custom_vjp
def low_back(v):
    return v

def low_keep(v):
    return (low(v), None)

def low_pass(kept, grad):
    return (grad,)

def back_keep(v):
    return (v, None)

def back_low(kept, grad):
    return (low(grad),)
low.defvjp(low_keep, low_pass)
low_back.defvjp(back_keep, back_low)
EPSILON = 1e-05
HIGHEST = lax.Precision.HIGHEST

def layer_norm(hidden, norm_gain, norm_shift):
    average = lax.optimization_barrier(jnp.mean(hidden, axis=-1, keepdims=True))
    centred = hidden - average
    spread = lax.optimization_barrier(jnp.mean(centred * centred, axis=-1, keepdims=True))
    return centred * lax.rsqrt(spread + EPSILON) * norm_gain + norm_shift

def block_forward(params, row_group):
    group_inputs, group_time, group_ids = row_group
    first_gain, first_shift, mix_weight, mix_bias, out_weight, out_bias, second_gain, second_shift, up_weight, up_bias, down_weight, down_bias = params
    model_width = group_inputs.shape[-1]
    residual_in = group_inputs + group_time[:, None, :]
    normed_one = low(layer_norm(residual_in, first_gain, first_shift))
    projected = jnp.einsum('gtd,de->gte', normed_one, mix_weight, precision=HIGHEST)
    queries = low_back(low(projected[..., :model_width] + mix_bias[:model_width]))
    key_rows = low_back(low(projected[..., model_width:2 * model_width]))
    values = low_back(low(projected[..., 2 * model_width:] + mix_bias[model_width:]))
    shape_heads = (group_inputs.shape[0], group_inputs.shape[1], HEADS, HEAD_DIM)
    products_raw = jnp.einsum('gqhe,gkhe->ghqk', queries.reshape(shape_heads), key_rows.reshape(shape_heads), precision=HIGHEST)
    scores = low_back(products_raw * (1.0 / math.sqrt(HEAD_DIM)))
    same_segment = group_ids[:, None, :, None] == group_ids[:, None, None, :]
    masked = jnp.where(same_segment, scores, -1e+30)
    largest = lax.optimization_barrier(jnp.max(masked, axis=-1, keepdims=True))
    log_total = largest + jnp.log(lax.optimization_barrier(jnp.sum(jnp.exp(masked - largest), axis=-1, keepdims=True)))
    attention_weights = low(jnp.exp(masked - log_total))
    attended = jnp.einsum('ghqk,gkhe->gqhe', attention_weights, values.reshape(shape_heads), precision=HIGHEST)
    attended = low_back(low(attended.reshape(group_inputs.shape)))
    branch = low_back(jnp.einsum('gtc,cd->gtd', attended, out_weight, precision=HIGHEST) + out_bias)
    residual_mid = residual_in + branch
    normed_two = low(layer_norm(residual_mid, second_gain, second_shift))
    hidden_up = low_back(jnp.einsum('gtd,df->gtf', normed_two, up_weight, precision=HIGHEST) + up_bias)
    activation = low(jax.nn.gelu(hidden_up, approximate=False))
    return residual_mid + jnp.einsum('gtf,fd->gtd', activation, down_weight, precision=HIGHEST) + down_bias

def reference(inputs, time_embed, segment_ids, cotangent, first_gain, first_shift, mix_weight, mix_bias, out_weight, out_bias, second_gain, second_shift, up_weight, up_bias, down_weight, down_bias):
    params = tuple((weight.astype(jnp.float32) for weight in (first_gain, first_shift, mix_weight, mix_bias, out_weight, out_bias, second_gain, second_shift, up_weight, up_bias, down_weight, down_bias)))
    row_count = inputs.shape[0]
    group_rows = math.gcd(row_count, 32)
    groups = row_count // group_rows

    def whole_layer(inputs_full, time_full, param_list):
        packed = (inputs_full.reshape(groups, group_rows, LEN, D), time_full.reshape(groups, group_rows, D), segment_ids.reshape(groups, group_rows, LEN))
        outputs = lax.map(jax.checkpoint(partial(block_forward, param_list)), packed)
        return outputs.reshape(row_count, LEN, D)
    layer_out, pullback = jax.vjp(whole_layer, inputs.astype(jnp.float32), time_embed.astype(jnp.float32), params)
    inputs_grad, time_grad, param_grads = pullback(cotangent.astype(jnp.float32))
    return (layer_out.astype(jnp.bfloat16), inputs_grad, time_grad, param_grads[0], param_grads[1], param_grads[2], param_grads[3], param_grads[4], param_grads[5], param_grads[6], param_grads[7], param_grads[8], param_grads[9], param_grads[10], param_grads[11])
```

```python
from functools import partial
import math

import jax
import jax.numpy as jnp
from jax import lax
from jax.experimental import pallas as pl
from jax.experimental.pallas import tpu as pltpu
from jax.sharding import PartitionSpec as P

HEAD_DIM = 64
EPSILON = 1e-05
NEG_FILL = -1e30
BATCH, SEQ = "batch", "seq"
AXES = (BATCH, SEQ)
F32, BF16 = jnp.float32, jnp.bfloat16


def norm_back(d_out, normal, inv, gain):
    g = d_out * gain
    return inv * (g - jnp.mean(g, -1, keepdims=True) - normal * jnp.mean(g * normal, -1, keepdims=True))


def normal_part(hidden):
    centred = hidden - jnp.mean(hidden, -1, keepdims=True)
    inv = lax.rsqrt(jnp.mean(centred * centred, -1, keepdims=True) + EPSILON)
    return centred * inv, inv


def contract(a, b, over_a, over_b, batch=((), ())):
    return lax.dot_general(a, b, ((over_a, over_b), batch), preferred_element_type=F32)


def layer(inputs, time, ids, cot, params):
    (gain1, shift1, mix, mbias, out, obias, gain2, shift2, up, ubias, down, dbias) = params
    gain1, shift1, mbias, obias, gain2, shift2, ubias, dbias = (
        v.astype(F32) for v in (gain1, shift1, mbias, obias, gain2, shift2, ubias, dbias))
    rows, length, width = inputs.shape
    heads = width // HEAD_DIM
    scale = 1.0 / math.sqrt(HEAD_DIM)
    flat = lambda t: t.reshape(rows * length, -1)
    by_head = lambda t: t.reshape(rows, length, heads, HEAD_DIM).transpose(0, 2, 1, 3).reshape(rows * heads, length, HEAD_DIM)
    unhead = lambda t: flat(t.reshape(rows, heads, length, HEAD_DIM).transpose(0, 2, 1, 3))
    each = ((0,), (0,))
    cot = flat(cot)
    res_in = flat(inputs.astype(F32) + time.astype(F32)[:, None, :])
    norm1, inv1 = normal_part(res_in)
    normed1 = (norm1 * gain1 + shift1).astype(BF16)
    proj = contract(normed1, mix, (1,), (0,))
    q = by_head((proj[:, :width] + mbias[:width]).astype(BF16))
    k = by_head(proj[:, width:2 * width].astype(BF16))
    v = by_head((proj[:, 2 * width:] + mbias[width:]).astype(BF16))
    scores = contract(q, k, (2,), (2,), each) * scale
    same = jnp.repeat(ids[:, :, None] == ids[:, None, :], heads, axis=0)
    masked = jnp.where(same, scores, NEG_FILL)
    top = jnp.max(masked, -1, keepdims=True)
    log_total = top + jnp.log(jnp.sum(jnp.exp(masked - top), -1, keepdims=True))
    probs = jnp.exp(masked - log_total)
    probs16 = probs.astype(BF16)
    att = unhead(contract(probs16, v, (2,), (1,), each).astype(BF16))
    res_mid = res_in + (contract(att, out, (1,), (0,)) + obias)
    norm2, inv2 = normal_part(res_mid)
    normed2 = (norm2 * gain2 + shift2).astype(BF16)
    hid = contract(normed2, up, (1,), (0,)) + ubias
    cdf = 0.5 * (1.0 + lax.erf(hid * math.sqrt(0.5)))
    act = (hid * cdf).astype(BF16)
    layer_out = (res_mid + contract(act, down, (1,), (0,)) + dbias).astype(BF16)

    cot32 = cot.astype(F32)
    slope = cdf + hid * jnp.exp(-0.5 * hid * hid) * (1.0 / math.sqrt(2 * math.pi))
    d_hid = (contract(cot, down, (1,), (1,)) * slope).astype(BF16)
    d_n2 = contract(d_hid, up, (1,), (1,))
    d_mid = cot32 + norm_back(d_n2, norm2, inv2, gain2)
    d_br = d_mid.astype(BF16)
    d_att = by_head(contract(d_br, out, (1,), (1,)).astype(BF16))
    d_pr = contract(d_att, v, (2,), (2,), each)
    d_sc = (probs * (d_pr - jnp.sum(probs * d_pr, -1, keepdims=True))).astype(BF16)
    d_q = unhead((contract(d_sc, k, (2,), (1,), each) * scale).astype(BF16))
    d_k = unhead((contract(d_sc, q, (1,), (1,), each) * scale).astype(BF16))
    d_v = unhead(contract(probs16, d_att, (1,), (1,), each).astype(BF16))
    d_proj = jnp.concatenate([d_q, d_k, d_v], -1)
    d_n1 = contract(d_proj, mix, (1,), (1,))
    x_grad = d_mid + norm_back(d_n1, norm1, inv1, gain1)

    def col(t):
        return jnp.sum(t.astype(F32), axis=0)

    weigh = lambda a, b: contract(a, b, (0,), (0,))
    grads = (col(d_n1 * norm1), col(d_n1), weigh(normed1, d_proj), jnp.concatenate([col(d_q), col(d_v)]),
             weigh(att, d_br), col(d_br), col(d_n2 * norm2), col(d_n2), weigh(normed2, d_hid), col(d_hid),
             weigh(act, cot), col(cot32))
    return layer_out.reshape(inputs.shape), x_grad.reshape(inputs.shape), grads


def gather_all(shard):
    return lax.all_gather(shard, AXES, axis=0, tiled=True)


def scatter_sum(grad):
    return lax.psum_scatter(grad, AXES, scatter_dimension=0, tiled=True)


def rows_whole(tensor):
    return lax.all_to_all(tensor, SEQ, split_axis=0, concat_axis=1, tiled=True)


def rows_split(tensor):
    return lax.all_to_all(tensor, SEQ, split_axis=1, concat_axis=0, tiled=True)


def any_mesh(inputs, time_embed, segment_ids, cotangent, *shards):
    y, count = lax.axis_index(SEQ), inputs.shape[0] // lax.axis_size(SEQ)
    mine = [lax.dynamic_slice_in_dim(t, y * count, count, 0) for t in (time_embed, segment_ids)]
    layer_out, x_grad, grads = layer(
        rows_whole(inputs), mine[0], mine[1], rows_whole(cotangent), [gather_all(w) for w in shards])
    time_grad = lax.all_to_all(jnp.sum(x_grad, 1), SEQ, split_axis=1, concat_axis=0, tiled=True)
    return (rows_split(layer_out), rows_split(x_grad), time_grad) + tuple(scatter_sum(g) for g in grads)


MESH = pl.DeviceIdType.MESH
Z_CHIPS = 4


class Place:
    def __init__(self):
        b, self.y = lax.axis_index(BATCH), lax.axis_index(SEQ)
        self.z, self.x, self.c = b // 4, (b // 2) % 2, b % 2
        z, x, c, y = self.z, self.x, self.c, self.y
        self.x2, self.y2 = x + (1 - 2 * x) * (1 - c), y + (1 - 2 * y) * c
        self.x3, self.y3 = x + (1 - 2 * x) * c, y + (1 - 2 * y) * (1 - c)
        self.near = self.at(z, self.x2, c, self.y2)
        self.far = self.at(z, self.x3, c, self.y3)
        self.twin = self.at(z, x, 1 - c, y)
        self.x_peer = self.at(z, 1 - x, c, y)
        self.y_peer = self.at(z, x, c, 1 - y)
        self.z_slots = [lax.rem(z + d, Z_CHIPS) for d in (1, 2, 3)]
        self.z_from = [lax.rem(z + Z_CHIPS - d, Z_CHIPS) for d in (1, 2, 3)]
        self.z_peers = [self.at(q, x, c, y) for q in self.z_slots]

    @staticmethod
    def at(z, x, c, y):
        return ((z * 2 + x) * 2 + c, y)

    def greet(self):
        barrier = pltpu.get_barrier_semaphore()
        partners = self.z_peers + [self.near, self.far, self.twin]
        for partner in partners:
            pl.semaphore_signal(barrier, inc=1, device_id=partner, device_id_type=MESH)
        pl.semaphore_wait(barrier, len(partners))


class Wires:
    def __init__(self, send_sem, recv_sem, place):
        self.send_sem, self.recv_sem, self.place, self.sent = send_sem, recv_sem, place, []

    def start(self, src, dst, slot, device):
        copy = pltpu.make_async_remote_copy(
            src_ref=src, dst_ref=dst, send_sem=self.send_sem.at[slot], recv_sem=self.recv_sem.at[slot],
            device_id=device, device_id_type=MESH,
        )
        copy.start()
        self.sent.append(copy)

    def arrived(self, dst, slot):
        pltpu.make_async_remote_copy(
            src_ref=dst, dst_ref=dst, send_sem=self.send_sem.at[slot], recv_sem=self.recv_sem.at[slot],
            device_id=self.place.twin, device_id_type=MESH,
        ).wait_recv()

    def finish(self):
        for copy in self.sent:
            copy.wait_send()


class Gather:
    SLOTS = 10

    def __init__(self, wires, place, own, buf, at, wide, base):
        self.w, self.p, self.own, self.buf, self.cols, self.base = wires, place, own, buf, pl.ds(at, wide), base

    def mine(self):
        p = self.p
        return self.buf.at[p.z, p.x, p.c, p.y, :, self.cols]

    def block(self, x, y, c):
        return self.buf.at[:, x, c, y, :, self.cols]

    def begin(self):
        for j, peer in enumerate(self.p.z_peers):
            self.w.start(self.own.at[:, self.cols], self.mine(), self.base + j, peer)

    def after_z(self):
        p, w, base = self.p, self.w, self.base
        for j in range(3):
            w.arrived(self.mine(), base + j)
        b = self.block(p.x, p.y, p.c)
        w.start(b, b, base + 3, p.near)
        w.start(b, b, base + 4, p.far)
        w.start(b, b, base + 6, p.twin)

    def after_near(self):
        p, w, base = self.p, self.w, self.base
        b = self.block(p.x2, p.y2, p.c)
        w.arrived(b, base + 3)
        w.start(b, b, base + 5, p.far)
        w.start(b, b, base + 7, p.twin)

    def after_far(self):
        p, w, base = self.p, self.w, self.base
        b = self.block(p.x3, p.y3, p.c)
        w.arrived(b, base + 4)
        w.start(b, b, base + 8, p.twin)
        b = self.block(1 - p.x, 1 - p.y, p.c)
        w.arrived(b, base + 5)
        w.start(b, b, base + 9, p.twin)

    def complete(self):
        p = self.p
        for j in range(6, 10):
            self.w.arrived(self.block(p.x, p.y, 1 - p.c), self.base + j)


def butterfly(wires, place, value, send, recv, base):
    peers = [place.twin, place.y_peer, place.x_peer]
    peers.append(place.at(place.z + 1 - 2 * (place.z % 2), place.x, place.c, place.y))
    peers.append(place.at(lax.rem(place.z + 2, Z_CHIPS), place.x, place.c, place.y))
    for step, peer in enumerate(peers):
        send[step] = value.astype(send.dtype)
        wires.start(send.at[step], recv.at[step], base + step, peer)
        wires.arrived(recv.at[step], base + step)
        value = value + recv[step].astype(F32)
    return value


def gather_kernel(chunks, w1, w2, w3, small, xin, cot, b1, b2, b3, total, xfull, cfull,
                  sm_send, sm_recv, send_sem, recv_sem, local_sem):
    p = Place()
    p.greet()
    wires = Wires(send_sem, recv_sem, p)
    own, bufs = (w1, w2, w3), (b1, b2, b3)
    locs = []
    for w in range(3):
        locs.append(pltpu.make_async_copy(own[w], bufs[w].at[p.z, p.x, p.c, p.y], local_sem.at[w]))
    for i, (src, dst) in enumerate(((xin, xfull), (cot, cfull))):
        locs.append(pltpu.make_async_copy(src.at[pl.ds(2 * p.y, 2)], dst.at[:, p.y], local_sem.at[3 + i]))
    for copy in locs:
        copy.start()
    base = len(chunks) * Gather.SLOTS
    for i, (src, dst) in enumerate(((xin, xfull), (cot, cfull))):
        wires.start(src.at[pl.ds(2 - 2 * p.y, 2)], dst.at[:, p.y], base + i, p.y_peer)
    gathers = [Gather(wires, p, own[w], bufs[w], at, wide, Gather.SLOTS * k) for k, (w, at, wide) in enumerate(chunks)]
    gathers[0].begin()
    gathers[1].begin()
    total[...] = butterfly(wires, p, small[...].astype(F32), sm_send, sm_recv, base + 2)
    for copy in locs:
        copy.wait()
    count = len(gathers)
    for k in range(count + 2):
        if k < count:
            gathers[k].after_z()
        if k + 2 < count:
            gathers[k + 2].begin()
        if 0 <= k - 1 < count:
            gathers[k - 1].after_near()
        if 0 <= k - 2 < count:
            gathers[k - 2].after_far()
            gathers[k - 2].complete()
    for i, dst in enumerate((xfull, cfull)):
        wires.arrived(dst.at[:, p.y], base + i)
    wires.finish()


class Scatter:
    SLOTS = 6

    def __init__(self, wires, place, grads, out, bufs, at, wide, base):
        self.w, self.p, self.grads, self.out, self.base = wires, place, grads, out, base
        self.cols = pl.ds(at, wide)
        self.s1, self.r1, self.s2, self.r2, self.sz, self.rz = bufs

    def part(self, ref, *index):
        return ref.at[index + (slice(None), slice(None), self.cols)]

    def value(self, ref, *index):
        return ref[index + (slice(None), slice(None), self.cols)].astype(F32)

    def begin(self):
        p = self.p
        for j, (x, y) in enumerate(((p.x3, p.y3), (1 - p.x, 1 - p.y))):
            self.s1[j, :, :, self.cols] = self.value(self.grads, x, y).astype(BF16)
            self.w.start(self.part(self.s1, j), self.part(self.r1, j), self.base + j, p.far)

    def after_far(self):
        p = self.p
        self.w.arrived(self.part(self.r1, 1), self.base + 1)
        self.s2[:, :, self.cols] = (self.value(self.grads, p.x2, p.y2) + self.value(self.r1, 1)).astype(BF16)
        self.w.start(self.part(self.s2), self.part(self.r2), self.base + 2, p.near)
        self.w.arrived(self.part(self.r1, 0), self.base)

    def after_near(self):
        p = self.p
        self.w.arrived(self.part(self.r2), self.base + 2)
        for q in range(Z_CHIPS):
            total = (self.grads[p.x, p.y, q, :, self.cols] + self.r1[0, q, :, self.cols].astype(F32)
                     + self.r2[q, :, self.cols].astype(F32))
            self.sz[q, :, self.cols] = total.astype(BF16)

            @pl.when(q == p.z)
            def _():
                self.out[:, self.cols] = total
        for j, (q, peer) in enumerate(zip(p.z_slots, p.z_peers)):
            self.w.start(self.sz.at[q, :, self.cols], self.rz.at[j, :, self.cols], self.base + 3 + j, peer)

    def after_z(self):
        total = self.out[:, self.cols]
        for j in range(3):
            self.w.arrived(self.rz.at[j, :, self.cols], self.base + 3 + j)
            total = total + self.rz[j, :, self.cols].astype(F32)
        self.out[:, self.cols] = total


def scatter_kernel(chunks, g1, g2, g3, small, lout, igrad, tgrad, o1, o2, o3, total, lo_out, ig_out, tg_out, *scratch):
    bufs = [scratch[i * 6:(i + 1) * 6] for i in range(3)]
    sm_send, sm_recv, send_sem, recv_sem, local_sem = scratch[18:]
    p = Place()
    p.greet()
    wires = Wires(send_sem, recv_sem, p)
    grads, outs = (g1, g2, g3), (o1, o2, o3)
    base = len(chunks) * Scatter.SLOTS
    locs = []
    for i, (src, dst) in enumerate(((lout, lo_out), (igrad, ig_out))):
        locs.append(pltpu.make_async_copy(src.at[:, p.y], dst.at[pl.ds(2 * p.y, 2)], local_sem.at[i]))
        wires.start(src.at[:, 1 - p.y], dst.at[pl.ds(2 * p.y, 2)], base + i, p.y_peer)
    locs.append(pltpu.make_async_copy(tgrad.at[p.y], tg_out.at[p.y], local_sem.at[2]))
    wires.start(tgrad.at[1 - p.y], tg_out.at[p.y], base + 2, p.y_peer)
    for copy in locs:
        copy.start()
    scatters = [Scatter(wires, p, grads[w], outs[w], bufs[w], at, wide, Scatter.SLOTS * k)
                for k, (w, at, wide) in enumerate(chunks)]
    count = len(scatters)
    scatters[0].begin()
    scatters[1].begin()
    total[...] = butterfly(wires, p, small[...], sm_send, sm_recv, base + 3)
    for k in range(count + 2):
        if k < count:
            scatters[k].after_far()
        if k + 2 < count:
            scatters[k + 2].begin()
        if 0 <= k - 1 < count:
            scatters[k - 1].after_near()
        if 0 <= k - 2 < count:
            scatters[k - 2].after_z()
    for i, dst in enumerate((lo_out, ig_out)):
        wires.arrived(dst.at[pl.ds(2 * p.y, 2)], base + i)
    wires.arrived(tg_out.at[p.y], base + 2)
    for copy in locs:
        copy.wait()
    wires.finish()


def chunked(widths):
    chunks = []
    for w, pieces in enumerate(widths):
        at = 0
        for wide in pieces:
            chunks.append((w, at, wide))
            at += wide
    return chunks


ANY, VMEM = pl.BlockSpec(memory_space=pl.ANY), pl.BlockSpec(memory_space=pltpu.VMEM)
SMALL = (16, 768)


def run_gather(w1, w2, w3, small, xin, cot):
    chunks = chunked(((384,) * 4, (384,) * 4, (256,) * 3))
    slots = len(chunks) * Gather.SLOTS + 7
    shapes = [jax.ShapeDtypeStruct((4, 2, 2, 2) + w.shape, BF16) for w in (w1, w2, w3)]
    half = jax.ShapeDtypeStruct((2, 2) + xin.shape[1:], BF16)
    return pl.pallas_call(
        partial(gather_kernel, chunks),
        out_shape=shapes + [jax.ShapeDtypeStruct(small.shape, F32), half, half],
        in_specs=[ANY] * 3 + [VMEM] + [ANY] * 2,
        out_specs=[ANY] * 3 + [VMEM] + [ANY] * 2,
        scratch_shapes=[pltpu.VMEM((5,) + small.shape, BF16)] * 2
        + [pltpu.SemaphoreType.DMA((slots,))] * 2 + [pltpu.SemaphoreType.DMA((5,))],
        compiler_params=pltpu.CompilerParams(collective_id=0, has_side_effects=True),
    )(w1, w2, w3, small, xin, cot)


def run_scatter(grads, small, lout, igrad, tgrad):
    wide = [g.shape[-1] for g in grads]
    rows = [g.shape[-2] for g in grads]
    chunks = chunked([(n // 3,) * 3 if n % 384 == 0 and n < 1000 else (384,) * (n // 384) for n in wide])
    slots = len(chunks) * Scatter.SLOTS + 8
    scratch = []
    for r, n in zip(rows, wide):
        scratch += [pltpu.VMEM(s, BF16) for s in (
            (2, 4, r, n), (2, 4, r, n), (4, r, n), (4, r, n), (4, r, n), (3, r, n))]
    scratch += [pltpu.VMEM((5,) + SMALL, F32)] * 2
    scratch += [pltpu.SemaphoreType.DMA((slots,))] * 2 + [pltpu.SemaphoreType.DMA((3,))]
    out_shape = [jax.ShapeDtypeStruct((r, n), F32) for r, n in zip(rows, wide)]
    out_shape += [jax.ShapeDtypeStruct(SMALL, F32)]
    out_shape += [jax.ShapeDtypeStruct((4,) + lout.shape[2:], BF16), jax.ShapeDtypeStruct((4,) + lout.shape[2:], F32),
                  jax.ShapeDtypeStruct(tgrad.shape, F32)]
    return pl.pallas_call(
        partial(scatter_kernel, chunks),
        out_shape=out_shape,
        in_specs=[VMEM] * 4 + [ANY] * 3,
        out_specs=[VMEM] * 4 + [ANY] * 3,
        scratch_shapes=scratch,
        compiler_params=pltpu.CompilerParams(collective_id=1, has_side_effects=True, vmem_limit_bytes=56 * 2**20),
    )(*grads, small, lout, igrad, tgrad)


def pack_halves(shard):
    r, n = shard.shape
    return shard.reshape(r, 2, n // 2).transpose(1, 0, 2).reshape(2 * r, n // 2)


def unpack_halves(packed):
    r, n = packed.shape
    return packed.reshape(2, r // 2, n).transpose(1, 0, 2).reshape(r // 2, 2 * n)


def unpack_gathered(buf, at, wide):
    part = buf[..., at:at + wide].reshape(32, 2, 24, wide)
    return part.transpose(0, 2, 1, 3).reshape(768, 2 * wide)


def place_in_zeros(shard, index):
    n = shard.shape[0]
    return lax.dynamic_update_slice(jnp.zeros((32 * n,), shard.dtype), shard, (index * n,))


def split_grad(grad, c, packed):
    k, n = grad.shape
    g = grad.reshape(4, 2, 2, 2, k // 32, n)
    mine = lax.dynamic_index_in_dim(g, c, 2, keepdims=False)
    other = lax.dynamic_index_in_dim(g, 1 - c, 2, keepdims=False).astype(BF16)
    pairs = [(i, i ^ 1) for i in range(16)]
    total = mine + lax.ppermute(other, BATCH, pairs).astype(F32)
    total = total.transpose(1, 2, 0, 3, 4)
    if packed:
        r = k // 32
        total = total.reshape(2, 2, 4, r, 2, n // 2).transpose(0, 1, 2, 4, 3, 5).reshape(2, 2, 4, 2 * r, n // 2)
    return total


def whole_rows(inputs, time_embed, segment_ids, cotangent, first_gain, first_shift, mix_weight, mix_bias, out_weight,
               out_bias, second_gain, second_shift, up_weight, up_bias, down_weight, down_bias):
    b, y = lax.axis_index(BATCH), lax.axis_index(SEQ)
    c, index = b % 2, b * 2 + y
    smalls = [first_gain, first_shift, mix_bias, out_bias, second_gain, second_shift, up_bias, down_bias]
    flat = jnp.concatenate([place_in_zeros(v, index) for v in smalls] + [jnp.zeros((4 * 768,), BF16)]).reshape(SMALL)
    w1 = jnp.concatenate([pack_halves(mix_weight), pack_halves(out_weight)], axis=1)
    b1, b2, b3, total, xfull, cfull = run_gather(w1, pack_halves(up_weight), down_weight, flat, inputs, cotangent)
    mix, out, up = unpack_gathered(b1, 0, 1152), unpack_gathered(b1, 1152, 384), unpack_gathered(b2, 0, 1536)
    down = b3.reshape(3072, 768)
    gain1, shift1, mbias, obias = total[0], total[1], total[2:4].reshape(-1), total[4]
    gain2, shift2, ubias, dbias = total[5], total[6], total[7:11].reshape(-1), total[11]
    x = xfull.reshape(2, 128, 768)
    cot = cfull.reshape(2, 128, 768)
    time = lax.dynamic_slice_in_dim(time_embed, 2 * y, 2, 0)
    ids = lax.dynamic_slice_in_dim(segment_ids, 2 * y, 2, 0)
    params = (gain1, shift1, mix, mbias, out, obias, gain2, shift2, up, ubias, down, dbias)
    layer_out, x_grad, g = layer(x, time, ids, cot, params)
    g_mix, g_out, g_up, g_down = g[2], g[4], g[8], g[10]
    small_grads = jnp.concatenate([g[0], g[1], g[3], g[5], g[6], g[7], g[9], g[11], jnp.zeros((4 * 768,), F32)]).reshape(SMALL)
    grads = [split_grad(g_down, c, False), split_grad(g_up, c, True),
             jnp.concatenate([split_grad(g_out, c, True), split_grad(g_mix, c, True)], -1)]
    tg = jnp.sum(x_grad, 1).reshape(2, 2, 384).transpose(1, 0, 2)
    tg = jnp.pad(tg, ((0, 0), (0, 6), (0, 0)))
    o3, o2, o1, total, lo, ig, tg = run_scatter(
        grads, small_grads, layer_out.reshape(2, 2, 64, 768), x_grad.reshape(2, 2, 64, 768), tg)
    parts, at = [], 0
    flat = total.reshape(-1)
    for v in smalls:
        n = v.shape[0]
        parts.append(lax.dynamic_slice(flat, (at + index * n,), (n,)))
        at += 32 * n
    time_grad = tg[:, :2].reshape(4, 384)
    return (lo, ig, time_grad, parts[0], parts[1], unpack_halves(o1[:, 384:]), parts[2], unpack_halves(o1[:, :384]), parts[3],
            parts[4], parts[5], unpack_halves(o2), parts[6], o3, parts[7])


def solution(mesh):
    fits = mesh.shape[BATCH] == 16 and mesh.shape[SEQ] == 2
    tokens, rows, vector, matrix = P(BATCH, SEQ, None), P(BATCH, None), P(AXES), P(AXES, None)
    params = (vector, vector, matrix, vector, matrix, vector, vector, vector, matrix, vector, matrix, vector)
    return jax.shard_map(
        whole_rows if fits else any_mesh,
        mesh=mesh,
        in_specs=(tokens, rows, rows, tokens) + params,
        out_specs=(tokens, tokens, P(BATCH, SEQ)) + params,
        check_vma=False,
    )
```

```python
from functools import partial
import math
from types import SimpleNamespace

import jax
import jax.numpy as jnp
from jax import lax
from jax.experimental import pallas as pl
from jax.experimental.pallas import tpu as pltpu
from jax.sharding import PartitionSpec as P

HEAD_DIM = 64
EPSILON = 1e-05
NEG_FILL = -1e30
BATCH, SEQ = "batch", "seq"
AXES = (BATCH, SEQ)
F32, BF16 = jnp.float32, jnp.bfloat16


def norm_back(d_out, normal, inv, gain):
    g = d_out * gain
    return inv * (g - jnp.mean(g, -1, keepdims=True) - normal * jnp.mean(g * normal, -1, keepdims=True))


def normal_part(hidden):
    centred = hidden - jnp.mean(hidden, -1, keepdims=True)
    inv = lax.rsqrt(jnp.mean(centred * centred, -1, keepdims=True) + EPSILON)
    return centred * inv, inv


def contract(a, b, over_a, over_b, batch=((), ())):
    return lax.dot_general(a, b, ((over_a, over_b), batch), preferred_element_type=F32)


def layer(inputs, time, ids, cot, params):
    (gain1, shift1, mix, mbias, out, obias, gain2, shift2, up, ubias, down, dbias) = params
    gain1, shift1, mbias, obias, gain2, shift2, ubias, dbias = (
        v.astype(F32) for v in (gain1, shift1, mbias, obias, gain2, shift2, ubias, dbias))
    rows, length, width = inputs.shape
    heads = width // HEAD_DIM
    scale = 1.0 / math.sqrt(HEAD_DIM)
    flat = lambda t: t.reshape(rows * length, -1)
    by_head = lambda t: t.reshape(rows, length, heads, HEAD_DIM).transpose(0, 2, 1, 3).reshape(rows * heads, length, HEAD_DIM)
    unhead = lambda t: flat(t.reshape(rows, heads, length, HEAD_DIM).transpose(0, 2, 1, 3))
    each = ((0,), (0,))
    cot = flat(cot)
    res_in = flat(inputs.astype(F32) + time.astype(F32)[:, None, :])
    norm1, inv1 = normal_part(res_in)
    normed1 = (norm1 * gain1 + shift1).astype(BF16)
    proj = contract(normed1, mix, (1,), (0,))
    q = by_head((proj[:, :width] + mbias[:width]).astype(BF16))
    k = by_head(proj[:, width:2 * width].astype(BF16))
    v = by_head((proj[:, 2 * width:] + mbias[width:]).astype(BF16))
    scores = contract(q, k, (2,), (2,), each) * scale
    same = jnp.repeat(ids[:, :, None] == ids[:, None, :], heads, axis=0)
    masked = jnp.where(same, scores, NEG_FILL)
    top = jnp.max(masked, -1, keepdims=True)
    log_total = top + jnp.log(jnp.sum(jnp.exp(masked - top), -1, keepdims=True))
    probs = jnp.exp(masked - log_total)
    probs16 = probs.astype(BF16)
    att = unhead(contract(probs16, v, (2,), (1,), each).astype(BF16))
    res_mid = res_in + (contract(att, out, (1,), (0,)) + obias)
    norm2, inv2 = normal_part(res_mid)
    normed2 = (norm2 * gain2 + shift2).astype(BF16)
    hid = contract(normed2, up, (1,), (0,)) + ubias
    cdf = 0.5 * (1.0 + lax.erf(hid * math.sqrt(0.5)))
    act = (hid * cdf).astype(BF16)
    layer_out = (res_mid + contract(act, down, (1,), (0,)) + dbias).astype(BF16)

    cot32 = cot.astype(F32)
    slope = cdf + hid * jnp.exp(-0.5 * hid * hid) * (1.0 / math.sqrt(2 * math.pi))
    d_hid = (contract(cot, down, (1,), (1,)) * slope).astype(BF16)
    d_n2 = contract(d_hid, up, (1,), (1,))
    d_mid = cot32 + norm_back(d_n2, norm2, inv2, gain2)
    d_br = d_mid.astype(BF16)
    d_att = by_head(contract(d_br, out, (1,), (1,)).astype(BF16))
    d_pr = contract(d_att, v, (2,), (2,), each)
    d_sc = (probs * (d_pr - jnp.sum(probs * d_pr, -1, keepdims=True))).astype(BF16)
    d_q = unhead((contract(d_sc, k, (2,), (1,), each) * scale).astype(BF16))
    d_k = unhead((contract(d_sc, q, (1,), (1,), each) * scale).astype(BF16))
    d_v = unhead(contract(probs16, d_att, (1,), (1,), each).astype(BF16))
    d_proj = jnp.concatenate([d_q, d_k, d_v], -1)
    d_n1 = contract(d_proj, mix, (1,), (1,))
    x_grad = d_mid + norm_back(d_n1, norm1, inv1, gain1)

    def col(t):
        return jnp.sum(t.astype(F32), axis=0)

    weigh = lambda a, b: contract(a, b, (0,), (0,))
    grads = (col(d_n1 * norm1), col(d_n1), weigh(normed1, d_proj), jnp.concatenate([col(d_q), col(d_v)]),
             weigh(att, d_br), col(d_br), col(d_n2 * norm2), col(d_n2), weigh(normed2, d_hid), col(d_hid),
             weigh(act, cot), col(cot32))
    return layer_out.reshape(inputs.shape), x_grad.reshape(inputs.shape), grads


def gather_all(shard):
    return lax.all_gather(shard, AXES, axis=0, tiled=True)


def scatter_sum(grad):
    return lax.psum_scatter(grad, AXES, scatter_dimension=0, tiled=True)


def rows_whole(tensor):
    return lax.all_to_all(tensor, SEQ, split_axis=0, concat_axis=1, tiled=True)


def rows_split(tensor):
    return lax.all_to_all(tensor, SEQ, split_axis=1, concat_axis=0, tiled=True)


def any_mesh(inputs, time_embed, segment_ids, cotangent, *shards):
    y, count = lax.axis_index(SEQ), inputs.shape[0] // lax.axis_size(SEQ)
    mine = [lax.dynamic_slice_in_dim(t, y * count, count, 0) for t in (time_embed, segment_ids)]
    layer_out, x_grad, grads = layer(
        rows_whole(inputs), mine[0], mine[1], rows_whole(cotangent), [gather_all(w) for w in shards])
    time_grad = lax.all_to_all(jnp.sum(x_grad, 1), SEQ, split_axis=1, concat_axis=0, tiled=True)
    return (rows_split(layer_out), rows_split(x_grad), time_grad) + tuple(scatter_sum(g) for g in grads)


MESH = pl.DeviceIdType.MESH
Z_CHIPS = 4
TOKENS, WIDTH, HIDDEN, PART = 256, 768, 3072, 384
SMALL = (16, WIDTH)
TRANSPOSED = ((1,), (1,))
TOKEN_SUM = ((0,), (0,))


class Place:
    def __init__(self):
        b, self.y = lax.axis_index(BATCH), lax.axis_index(SEQ)
        self.z, self.x, self.c = b // 4, (b // 2) % 2, b % 2
        z, x, c, y = self.z, self.x, self.c, self.y
        self.x2, self.y2 = x + (1 - 2 * x) * (1 - c), y + (1 - 2 * y) * c
        self.x3, self.y3 = x + (1 - 2 * x) * c, y + (1 - 2 * y) * (1 - c)
        self.near = self.at(z, self.x2, c, self.y2)
        self.far = self.at(z, self.x3, c, self.y3)
        self.twin = self.at(z, x, 1 - c, y)
        self.x_peer = self.at(z, 1 - x, c, y)
        self.y_peer = self.at(z, x, c, 1 - y)
        self.z_slots = [lax.rem(z + d, Z_CHIPS) for d in (1, 2, 3)]
        self.z_peers = [self.at(q, x, c, y) for q in self.z_slots]

    @staticmethod
    def at(z, x, c, y):
        return ((z * 2 + x) * 2 + c, y)

    def role(self, c, x, y):
        dx, dy = (x + self.x) % 2, (y + self.y) % 2
        return (dx + 2 * dy) * (1 - c) + (dy + 2 * dx) * c

    def of_role(self, c, role):
        low, high = role % 2, role // 2
        dx, dy = low * (1 - c) + high * c, high * (1 - c) + low * c
        return (self.x + dx) % 2, (self.y + dy) % 2

    def greet(self):
        barrier = pltpu.get_barrier_semaphore()
        partners = self.z_peers + [self.near, self.far, self.twin]
        for partner in partners:
            pl.semaphore_signal(barrier, inc=1, device_id=partner, device_id_type=MESH)
        pl.semaphore_wait(barrier, len(partners))


class Wires:
    def __init__(self, send_sem, recv_sem, place):
        self.send_sem, self.recv_sem, self.place = send_sem, recv_sem, place
        self.sent, self.used = [], 0

    def slots(self, count):
        self.used += count
        return self.used - count

    def start(self, src, dst, slot, device):
        copy = pltpu.make_async_remote_copy(
            src_ref=src, dst_ref=dst, send_sem=self.send_sem.at[slot], recv_sem=self.recv_sem.at[slot],
            device_id=device, device_id_type=MESH,
        )
        copy.start()
        self.sent.append(copy)
        return copy

    def arrived(self, dst, slot):
        pltpu.make_async_remote_copy(
            src_ref=dst, dst_ref=dst, send_sem=self.send_sem.at[slot], recv_sem=self.recv_sem.at[slot],
            device_id=self.place.twin, device_id_type=MESH,
        ).wait_recv()

    def left(self, copies):
        for copy in copies:
            copy.wait_send()
        self.sent = [kept for kept in self.sent if all(kept is not copy for copy in copies)]

    def finish(self):
        for copy in self.sent:
            copy.wait_send()
        self.sent = []


class Gather:
    def __init__(self, wires, place, own, buf, at, wide):
        self.w, self.p, self.own, self.buf, self.cols = wires, place, own, buf, pl.ds(at, wide)
        self.base, self.copies = wires.slots(10), []

    def send(self, src, dst, slot, device):
        self.copies.append(self.w.start(src, dst, self.base + slot, device))

    def mine(self):
        p = self.p
        return self.buf.at[p.z, p.x, p.c, p.y, :, self.cols]

    def block(self, x, y, c):
        return self.buf.at[:, x, c, y, :, self.cols]

    def begin(self):
        for j, peer in enumerate(self.p.z_peers):
            self.send(self.own.at[:, self.cols], self.mine(), j, peer)

    def after_z(self):
        p = self.p
        for j in range(3):
            self.w.arrived(self.mine(), self.base + j)
        b = self.block(p.x, p.y, p.c)
        self.send(b, b, 3, p.near)
        self.send(b, b, 4, p.far)
        self.send(b, b, 6, p.twin)

    def after_near(self):
        p = self.p
        b = self.block(p.x2, p.y2, p.c)
        self.w.arrived(b, self.base + 3)
        self.send(b, b, 5, p.far)
        self.send(b, b, 7, p.twin)

    def after_far(self):
        p = self.p
        b = self.block(p.x3, p.y3, p.c)
        self.w.arrived(b, self.base + 4)
        self.send(b, b, 8, p.twin)
        b = self.block(1 - p.x, 1 - p.y, p.c)
        self.w.arrived(b, self.base + 5)
        self.send(b, b, 9, p.twin)
        for j in range(6, 10):
            self.w.arrived(self.block(p.x, p.y, 1 - p.c), self.base + j)

    def halves_in_place(self):
        self.w.left(self.copies)
        rows = self.buf.shape[-2] // 2

        @pl.loop(0, 16)
        def _(pair):
            z, x, c = pair // 4, (pair // 2) % 2, pair % 2
            v = [self.buf[z, x, c, y, :, self.cols].astype(F32) for y in (0, 1)]
            for h in (0, 1):
                part = slice(h * rows, h * rows + rows)
                self.buf[z, x, c, h, :, self.cols] = jnp.concatenate([v[0][part], v[1][part]], 0).astype(BF16)


class Scatter:
    def __init__(self, wires, place, rows, cols, keep, s1, r1, s2, r2, sz, rz, out, out_cols):
        self.w, self.p, self.rows, self.cols, self.out_cols = wires, place, rows, cols, out_cols
        self.keep, self.s1, self.r1, self.s2, self.r2, self.sz, self.rz, self.out = keep, s1, r1, s2, r2, sz, rz, out
        self.base, self.quarter, self.packed = wires.slots(5), Z_CHIPS * rows, rows % 16 != 0
        wide = cols.size // 2 if self.packed else cols.size
        self.z_cols = pl.ds(cols.start // 2 if self.packed else cols.start, wide)

    def begin(self, left, right):
        q = self.quarter
        for role in range(4):
            rows = slice(role * q, role * q + q)
            total = contract(left[0][rows], right[0], (1,), (0,)) + contract(left[1][rows], right[1], (1,), (0,))
            at = pl.ds((role % 2) * q, q)
            if role < 2:
                self.keep[at, self.cols] = total
            else:
                self.s1[at, self.cols] = total.astype(BF16)
        both = pl.ds(0, 2 * q)
        self.w.start(self.s1.at[both, self.cols], self.r1.at[both, self.cols], self.base, self.p.far)

    def after_far(self):
        q = self.quarter
        self.w.arrived(self.r1.at[pl.ds(0, 2 * q), self.cols], self.base)
        at = pl.ds(q, q)
        self.s2[:, self.cols] = (self.keep[at, self.cols] + self.r1[at, self.cols].astype(F32)).astype(BF16)
        self.w.start(self.s2.at[:, self.cols], self.r2.at[:, self.cols], self.base + 1, self.p.near)

    def after_near(self):
        q, n = self.quarter, self.rows
        self.w.arrived(self.r2.at[:, self.cols], self.base + 1)
        at = pl.ds(0, q)
        total = self.keep[at, self.cols] + self.r1[at, self.cols].astype(F32) + self.r2[:, self.cols].astype(F32)
        for z in range(Z_CHIPS):
            piece = total[z * n:z * n + n]

            @pl.when(z == self.p.z)
            def _():
                self.out[:, self.out_cols] = piece

            if self.packed:
                half = self.z_cols.size
                piece = jnp.concatenate([piece[:, :half], piece[:, half:]], 0)
            self.sz[z, :, self.z_cols] = piece.astype(BF16)
        for j, (z, peer) in enumerate(zip(self.p.z_slots, self.p.z_peers)):
            self.w.start(self.sz.at[z, :, self.z_cols], self.rz.at[j, :, self.z_cols], self.base + 2 + j, peer)

    def after_z(self):
        total = 0.0
        for j in range(3):
            self.w.arrived(self.rz.at[j, :, self.z_cols], self.base + 2 + j)
            total = total + self.rz[j, :, self.z_cols].astype(F32)
        if self.packed:
            total = jnp.concatenate([total[:self.rows], total[self.rows:]], 1)
        self.out[:, self.out_cols] = self.out[:, self.out_cols] + total


class Butterfly:
    def __init__(self, wires, place, send, recv):
        self.w, self.send, self.recv, self.base = wires, send, recv, wires.slots(5)
        self.peers = [place.twin, place.y_peer, place.x_peer]
        self.peers.append(place.at(place.z + 1 - 2 * (place.z % 2), place.x, place.c, place.y))
        self.peers.append(place.at(lax.rem(place.z + 2, Z_CHIPS), place.x, place.c, place.y))
        self.step = 0

    def begin(self, value):
        i = self.step
        self.send[i] = value.astype(self.send.dtype)
        self.w.start(self.send.at[i], self.recv.at[i], self.base + i, self.peers[i])

    def next(self):
        i = self.step
        self.w.arrived(self.recv.at[i], self.base + i)
        value = self.send[i].astype(F32) + self.recv[i].astype(F32)
        self.step += 1
        if self.step < 5:
            self.begin(value)
        return value


def merged(value):
    return value.reshape(-1, value.shape[-1])


def by_rows(step, body, *carry):
    return lax.fori_loop(0, TOKENS // step, lambda i, kept: body(i, pl.ds(pl.multiple_of(i * step, step), step), *kept), carry)


def folded(value):
    return jnp.sum(value.reshape(value.shape[0] // 8, 8, value.shape[1]), 0)


def column_sums(value):
    return contract(jnp.ones((8, value.shape[0]), BF16), value, (1,), (0,))[0:1]


def token_block(i):
    return i // 4, (i // 2) % 2, pl.ds(pl.multiple_of((i % 2) * 32, 32), 32)


def scratch_table(slots):
    k, w = WIDTH // 2, WIDTH
    return [
        ("par_send", (5,) + SMALL, BF16), ("par_recv", (5,) + SMALL, BF16), ("par", SMALL, F32),
        ("sum_send", (5,) + SMALL, F32), ("sum_recv", (5,) + SMALL, F32), ("sums", SMALL, F32),
        ("b1", (4, 2, 2, 2, 48, 1536), BF16), ("b2", (4, 2, 2, 2, 48, 1536), BF16), ("b3", (4, 2, 2, 2, 96, w), BF16),
        ("x0", (2, 2, 64, w), BF16), ("cot", (2, 2, 2, 64, w), BF16),
        ("res_in", (TOKENS, w), F32), ("normed1", (TOKENS, w), BF16), ("qkv", (TOKENS, 3 * w), BF16),
        ("probs", (12, TOKENS, 128), F32), ("att", (TOKENS, w), BF16), ("res_mid", (TOKENS, w), F32),
        ("normed2", (TOKENS, w), BF16), ("slope", (TOKENS, HIDDEN), F32), ("act", (TOKENS, HIDDEN), BF16),
        ("pick", (2, k, w), BF16), ("pick_act", (2, 192, PART), BF16),
        ("t1", (2, k, TOKENS), BF16), ("t1_send", (k, TOKENS), BF16),
        ("to", (2, k, TOKENS), BF16), ("to_send", (k, TOKENS), BF16),
        ("t2", (2, k, TOKENS), BF16), ("t2_send", (k, TOKENS), BF16),
        ("ta", (2, 4, 4, 96, TOKENS), BF16), ("ta_send", (4, 4, 96, TOKENS), BF16),
        ("d_hid", (2, TOKENS, HIDDEN), BF16), ("d_norm", (TOKENS, w), F32), ("d_mid", (TOKENS, w), F32),
        ("d_branch", (2, TOKENS, w), BF16), ("d_att", (TOKENS, w), BF16), ("d_proj", (2, TOKENS, 3 * w), BF16),
        ("lo", (2, 2, 64, w), BF16), ("ig", (2, 2, 64, w), F32), ("tg", (2, 8, PART), F32),
        ("keep_d", (768, w), F32), ("s1_d", (768, w), BF16), ("r1_d", (768, w), BF16), ("s2_d", (PART, w), BF16),
        ("r2_d", (PART, w), BF16), ("sz_d", (4, 96, w), BF16), ("rz_d", (3, 96, w), BF16),
        ("keep_u", (192, HIDDEN), F32), ("s1_u", (192, HIDDEN), BF16), ("r1_u", (192, HIDDEN), BF16),
        ("s2_u", (96, HIDDEN), BF16), ("r2_u", (96, HIDDEN), BF16), ("sz_u", (4, 48, 1536), BF16), ("rz_u", (3, 48, 1536), BF16),
        ("r1_m", (192, HIDDEN), BF16),
        ("s2_m", (96, HIDDEN), BF16), ("r2_m", (96, HIDDEN), BF16), ("sz_m", (4, 48, 1536), BF16), ("rz_m", (3, 48, 1536), BF16),
        ("send_sem", (slots,), None), ("recv_sem", (slots,), None), ("local_sem", (10,), None),
    ]


SLOTS = 240


def layer_kernel(names, w1, w2, w3, small, time, ids_down, ids_along, xin, cin,
                 o_mix, o_out, o_up, o_down, o_small, lo_out, ig_out, tg_out, *scratch):
    m = SimpleNamespace(**dict(zip(names, scratch)))
    p = Place()
    p.greet()
    wires = Wires(m.send_sem, m.recv_sem, p)
    me, twin = p.c, 1 - p.c
    scale = 1.0 / math.sqrt(HEAD_DIM)

    own, bufs = (w1, w2, w3), (m.b1, m.b2, m.b3)
    locs = [pltpu.make_async_copy(own[i], bufs[i].at[p.z, p.x, p.c, p.y], m.local_sem.at[i]) for i in range(3)]
    rows_own, rows_other = pl.ds(2 * p.y, 2), pl.ds(2 - 2 * p.y, 2)
    locs.append(pltpu.make_async_copy(xin.at[rows_own], m.x0.at[:, p.y], m.local_sem.at[3]))
    locs.append(pltpu.make_async_copy(cin.at[rows_own], m.cot.at[me, :, p.y], m.local_sem.at[4]))
    for copy in locs:
        copy.start()
    swap = wires.slots(3)
    wires.start(xin.at[rows_other], m.x0.at[:, p.y], swap, p.y_peer)
    params = Butterfly(wires, p, m.par_send, m.par_recv)
    params.begin(small[...].astype(F32))

    plan = [(0, PART * i, PART) for i in range(4)] + [(1, PART * i, PART) for i in range(4)] + [(2, 256 * i, 256) for i in range(3)]
    gathers = [Gather(wires, p, own[w], bufs[w], at, wide) for w, at, wide in plan]
    ahead = 3
    for g in gathers[:ahead]:
        g.begin()
    wires.start(cin.at[rows_other], m.cot.at[me, :, p.y], swap + 1, p.y_peer)

    def z_step(k):
        gathers[k].after_z()
        if k + ahead < len(gathers):
            gathers[k + ahead].begin()

    def near_step(k):
        gathers[k].after_near()

    def far_step(k):
        gathers[k].after_far()
        if plan[k][0] < 2:
            gathers[k].halves_in_place()

    lane, row = lax.broadcasted_iota(jnp.int32, (24, WIDTH), 1), lax.broadcasted_iota(jnp.int32, (24, WIDTH), 0)
    lane_a, row_a = lax.broadcasted_iota(jnp.int32, (192, PART), 1), lax.broadcasted_iota(jnp.int32, (192, PART), 0)
    for side, c in ((0, me), (1, twin)):
        pieces = []
        for role in range(4):
            x, y = p.of_role(c, role)
            for z in range(Z_CHIPS):
                first = (((z * 2 + x) * 2 + c) * 2 + y) * 24
                pieces.append((lane == row + first).astype(F32))
        m.pick[side] = jnp.concatenate(pieces, 0).astype(BF16)
        m.pick_act[side] = (lane_a == row_a + c * 192).astype(F32).astype(BF16)

    twin_base = wires.slots(16)

    def transposed(value, ref, send, slot):
        ref[me] = contract(m.pick[0], value, *TRANSPOSED).astype(BF16)
        send[...] = contract(m.pick[1], value, *TRANSPOSED).astype(BF16)
        wires.start(send, ref.at[me], twin_base + slot, p.twin)

    def left_of(ref):
        return [merged(ref[core]) for core in (0, 1)]

    def normal(h):
        centred = h - jnp.mean(h, -1, keepdims=True)
        inv = lax.rsqrt(jnp.mean(centred * centred, -1, keepdims=True) + EPSILON)
        return centred * inv, inv

    def first_norm():
        m.par[...] = params.next()
        for copy in locs[3:]:
            copy.wait()
        wires.arrived(m.x0.at[:, p.y], swap)

        def body(i, at):
            r, half, pos = token_block(i)
            h = m.x0[r, half, pos, :].astype(F32) + time[r]
            m.res_in[at, :] = h
            m.normed1[at, :] = (normal(h)[0] * m.par[0:1, :] + m.par[1:2, :]).astype(BF16)
            return ()

        by_rows(32, body)
        transposed(m.normed1[...], m.t1, m.t1_send, 0)

    def projected(k):
        for h in (0, 1):
            weight = merged(m.b1[:, :, :, h, :, pl.ds(PART * k, PART)])
            group, lanes = (3 * h + k) // 2, PART * ((3 * h + k) % 2)
            total = contract(m.normed1[...], weight, (1,), (0,))
            if group != 1:
                total = total + m.par[2 + group // 2:3 + group // 2, lanes:lanes + PART]
            m.qkv[:, WIDTH * group + lanes:WIDTH * group + lanes + PART] = total.astype(BF16)

    low = (lax.broadcasted_iota(jnp.int32, (1, 128), 1) < HEAD_DIM).astype(F32)
    heads_of = [low.astype(BF16), (1.0 - low).astype(BF16)]

    def two_heads(value):
        return jnp.concatenate([value * h for h in heads_of], 0)

    def side_by_side(value):
        return jnp.concatenate([value[:128], value[128:]], 1)

    def at_pair(i):
        return pl.ds(pl.multiple_of((i // 6) * 128, 128), 128), [
            pl.ds(pl.multiple_of((i % 6) * 128 + WIDTH * part, 128), 128) for part in range(3)]

    def attention(first, last):
        def body(i, _):
            rows, (cq, ck, cv) = at_pair(i)
            q2, k, v = two_heads(m.qkv[rows, cq]), m.qkv[rows, ck], m.qkv[rows, cv]
            scores = contract(q2, k, *TRANSPOSED) * scale
            same = ids_down[rows, :] == ids_along[i // 6]
            masked = jnp.where(jnp.concatenate([same, same], 0), scores, NEG_FILL)
            e = jnp.exp(masked - jnp.max(masked, -1, keepdims=True))
            probs = e / jnp.sum(e, -1, keepdims=True)
            m.probs[i] = probs
            m.att[rows, cq] = contract(side_by_side(probs.astype(BF16)), two_heads(v), (1,), (0,)).astype(BF16)
            return 0

        lax.fori_loop(first, last, body, 0)

    def out_half(h):
        return merged(m.b1[:, :, :, h, :, pl.ds(3 * PART, PART)])

    def branch():
        transposed(m.att[...], m.to, m.to_send, 1)
        for h in (0, 1):
            at = slice(PART * h, PART * h + PART)
            total = contract(m.att[...], out_half(h), (1,), (0,)) + m.par[4:5, at]
            m.res_mid[:, at] = m.res_in[:, at] + total

        def body(i, at):
            m.normed2[at, :] = (normal(m.res_mid[at, :])[0] * m.par[5:6, :] + m.par[6:7, :]).astype(BF16)
            return ()

        by_rows(32, body)
        transposed(m.normed2[...], m.t2, m.t2_send, 2)

    def up_part(k):
        for h in (0, 1):
            first = 1536 * h + PART * k
            cols, lanes = slice(first, first + PART), first % WIDTH
            weight = merged(m.b2[:, :, :, h, :, pl.ds(PART * k, PART)])
            bias = m.par[7 + first // WIDTH:8 + first // WIDTH, lanes:lanes + PART]
            m.slope[:, cols] = contract(m.normed2[...], weight, (1,), (0,)) + bias

            def body(i, at):
                v = m.slope[at, cols]
                cdf = 0.5 + 0.5 * lax.erf(v * math.sqrt(0.5))
                m.act[at, cols] = (v * cdf).astype(BF16)
                m.slope[at, cols] = cdf + v * jnp.exp(-0.5 * v * v) * (1.0 / math.sqrt(2 * math.pi))
                return ()

            by_rows(32, body)
            z, x = (first // PART) // 2, (first // PART) % 2
            act = m.act[:, cols]
            for side, c in ((0, me), (1, twin)):
                picked = contract(m.pick_act[side], act, *TRANSPOSED).astype(BF16)
                for y in (0, 1):
                    role = p.role(c, x, y)
                    piece = picked[96 * y:96 * y + 96]
                    if side == 0:
                        m.ta[me, role, z] = piece
                    else:
                        m.ta_send[role, z] = piece

    def cot_whole():
        wires.arrived(m.cot.at[me, :, p.y], swap + 1)
        wires.start(m.cot.at[me], m.cot.at[me], twin_base + 3, p.twin)

    def act_out():
        wires.start(m.ta_send, m.ta.at[me], twin_base + 4, p.twin)

    def scatter_of(kind, first, wide, out, out_first):
        cols, out_cols = pl.ds(first, wide), pl.ds(out_first, wide)
        if kind == 0:
            return Scatter(wires, p, 96, cols, m.keep_d, m.s1_d, m.r1_d, m.s2_d, m.r2_d, m.sz_d, m.rz_d, out, out_cols)
        if kind == 1:
            return Scatter(wires, p, 24, cols, m.keep_u, m.s1_u, m.r1_u, m.s2_u, m.r2_u, m.sz_u, m.rz_u, out, out_cols)
        return Scatter(wires, p, 24, cols, m.slope, m.act, m.r1_m, m.s2_m, m.r2_m, m.sz_m, m.rz_m, out, out_cols)

    down = [scatter_of(0, 256 * i, 256, o_down, 256 * i) for i in range(3)]
    ups = [scatter_of(1, WIDTH * i, WIDTH, o_up, WIDTH * i) for i in range(4)]
    mixes = [scatter_of(2, WIDTH * i, WIDTH, o_mix, WIDTH * i) for i in range(3)]
    outs = scatter_of(2, 3 * WIDTH, WIDTH, o_out, 0)

    def down_grad(i):
        if i == 0:
            wires.arrived(m.cot.at[twin], twin_base + 3)
            wires.arrived(m.ta.at[twin], twin_base + 4)
            m.sums[...] = jnp.zeros(SMALL, F32)
            m.sums[11:12, :] = column_sums(merged(m.cot[me]))
        cols = pl.ds(256 * i, 256)
        down[i].begin(left_of(m.ta), [merged(m.cot[core, :, :, :, cols]) for core in (0, 1)])

    def hidden_grad(i):
        cot = merged(m.cot[me])
        for part in (2 * i, 2 * i + 1):
            cols = slice(PART * part, PART * part + PART)
            d_act = contract(cot, merged(m.b3[part // 2, part % 2]), *TRANSPOSED)
            grad = (d_act * m.slope[:, cols]).astype(BF16)
            m.d_hid[me, :, cols] = grad
            lanes = PART * (part % 2)
            m.sums[7 + i:8 + i, lanes:lanes + PART] = column_sums(grad)
        at = m.d_hid.at[me, :, pl.ds(WIDTH * i, WIDTH)]
        wires.start(at, at, twin_base + 5 + i, p.twin)

    def up_grad(i):
        if i == 0:
            wires.arrived(m.t2.at[twin], twin_base + 2)
        cols = pl.ds(WIDTH * i, WIDTH)
        wires.arrived(m.d_hid.at[twin, :, cols], twin_base + 5 + i)
        ups[i].begin(left_of(m.t2), [m.d_hid[core, :, cols] for core in (0, 1)])

    def layer_result():
        for i in range(3):
            cols = slice(256 * i, 256 * i + 256)
            total = contract(m.act[...], merged(m.b3[:, :, :, :, :, cols]), (1,), (0,)) + m.par[11:12, cols]
            total = (m.res_mid[:, cols] + total).astype(BF16)
            for r in (0, 1):
                for half in (0, 1):
                    first = r * 128 + half * 64
                    m.lo[r, half, :, cols] = total[first:first + 64]

    back = wires.slots(3)
    lo_copy = pltpu.make_async_copy(m.lo.at[:, p.y], lo_out.at[rows_own], m.local_sem.at[5])
    ig_copy = pltpu.make_async_copy(m.ig.at[:, p.y], ig_out.at[rows_own], m.local_sem.at[6])
    tg_copy = pltpu.make_async_copy(m.tg.at[p.y], tg_out.at[p.y], m.local_sem.at[7])

    def result_out():
        lo_copy.start()
        wires.start(m.lo.at[:, 1 - p.y], lo_out.at[rows_own], back, p.y_peer)

    def second_norm_back():
        halves = [merged(m.b2[:, :, :, h]) for h in (0, 1)]
        m.d_norm[...] = contract(m.d_hid[me, :, 0:1536], halves[0], *TRANSPOSED)
        m.d_norm[...] += contract(m.d_hid[me, :, 1536:3072], halves[1], *TRANSPOSED)

        def body(i, at, gain_sum, shift_sum):
            r, half, pos = token_block(i)
            norm, inv = normal(m.res_mid[at, :])
            dn = m.d_norm[at, :]
            dn_norm = dn * norm
            g, gn = dn * m.par[5:6, :], dn_norm * m.par[5:6, :]
            back_in = inv * (g - jnp.mean(g, -1, keepdims=True) - norm * jnp.mean(gn, -1, keepdims=True))
            d_mid = m.cot[me, r, half, pos, :].astype(F32) + back_in
            m.d_mid[at, :] = d_mid
            m.d_branch[me, at, :] = d_mid.astype(BF16)
            return gain_sum + folded(dn_norm), shift_sum + folded(dn)

        zero = jnp.zeros((8, WIDTH), F32)
        gain_sum, shift_sum = by_rows(32, body, zero, zero)
        m.sums[5:6, :] = jnp.sum(gain_sum, 0, keepdims=True)
        m.sums[6:7, :] = jnp.sum(shift_sum, 0, keepdims=True)
        wires.start(m.d_branch.at[me], m.d_branch.at[me], twin_base + 9, p.twin)
        d_branch = m.d_branch[me]
        m.sums[4:5, :] = column_sums(d_branch)
        d_att = contract(d_branch[:, 0:PART], out_half(0), *TRANSPOSED) + contract(d_branch[:, PART:], out_half(1), *TRANSPOSED)
        m.d_att[...] = d_att.astype(BF16)

    def out_grad():
        wires.arrived(m.to.at[twin], twin_base + 1)
        wires.arrived(m.d_branch.at[twin], twin_base + 9)
        outs.begin(left_of(m.to), [m.d_branch[core] for core in (0, 1)])

    def attention_back(first, last):
        def body(i, _):
            rows, (cq, ck, cv) = at_pair(i)
            q2, k, v = two_heads(m.qkv[rows, cq]), m.qkv[rows, ck], m.qkv[rows, cv]
            da2 = two_heads(m.d_att[rows, cq])
            probs = m.probs[i]
            d_probs = contract(da2, v, *TRANSPOSED)
            delta = jnp.sum(probs * d_probs, -1, keepdims=True)
            d_scores = (probs * (d_probs - delta)).astype(BF16)
            m.d_proj[me, rows, cq] = (contract(side_by_side(d_scores), two_heads(k), (1,), (0,)) * scale).astype(BF16)
            m.d_proj[me, rows, ck] = (contract(d_scores, q2, *TOKEN_SUM) * scale).astype(BF16)
            m.d_proj[me, rows, cv] = contract(probs.astype(BF16), da2, *TOKEN_SUM).astype(BF16)
            return 0

        lax.fori_loop(first, last, body, 0)

    def proj_out():
        for i in range(3):
            at = m.d_proj.at[me, :, pl.ds(WIDTH * i, WIDTH)]
            wires.start(at, at, twin_base + 10 + i, p.twin)

    def mix_grad(i):
        if i == 0:
            wires.arrived(m.t1.at[twin], twin_base)
        cols = pl.ds(WIDTH * i, WIDTH)
        if i != 1:
            m.sums[2 + i // 2:3 + i // 2, :] = column_sums(m.d_proj[me, :, cols])
        wires.arrived(m.d_proj.at[twin, :, cols], twin_base + 10 + i)
        mixes[i].begin(left_of(m.t1), [m.d_proj[core, :, cols] for core in (0, 1)])

    def first_norm_back():
        halves = [merged(m.b1[:, :, :, h, :, 0:3 * PART]) for h in (0, 1)]
        m.d_norm[...] = contract(m.d_proj[me, :, 0:3 * PART], halves[0], *TRANSPOSED)
        m.d_norm[...] += contract(m.d_proj[me, :, 3 * PART:], halves[1], *TRANSPOSED)

        def body(i, at, gain_sum, shift_sum, row_sum):
            r, half, pos = token_block(i)
            norm, inv = normal(m.res_in[at, :])
            dn = m.d_norm[at, :]
            dn_norm = dn * norm
            g, gn = dn * m.par[0:1, :], dn_norm * m.par[0:1, :]
            grad = m.d_mid[at, :] + inv * (g - jnp.mean(g, -1, keepdims=True) - norm * jnp.mean(gn, -1, keepdims=True))
            m.ig[r, half, pos, :] = grad
            sums = folded(grad)
            first = (r == 0).astype(F32)
            return (gain_sum + folded(dn_norm), shift_sum + folded(dn),
                    row_sum + jnp.concatenate([sums * first, sums * (1.0 - first)], 0))

        zero = jnp.zeros((8, WIDTH), F32)
        gain_sum, shift_sum, row_sum = by_rows(32, body, zero, zero, jnp.zeros((16, WIDTH), F32))
        m.sums[0:1, :] = jnp.sum(gain_sum, 0, keepdims=True)
        m.sums[1:2, :] = jnp.sum(shift_sum, 0, keepdims=True)
        for r in (0, 1):
            total = jnp.sum(row_sum[8 * r:8 * r + 8], 0, keepdims=True)
            for half in (0, 1):
                m.tg[half, r:r + 1, :] = total[:, PART * half:PART * half + PART]
        ig_copy.start()
        wires.start(m.ig.at[:, 1 - p.y], ig_out.at[rows_own], back + 1, p.y_peer)
        tg_copy.start()
        wires.start(m.tg.at[1 - p.y], tg_out.at[p.y], back + 2, p.y_peer)

    totals = Butterfly(wires, p, m.sum_send, m.sum_recv)

    for copy in locs[:3]:
        copy.wait()
    z_step(0)
    params.next()
    z_step(1)
    near_step(0)
    params.next()
    z_step(2)
    near_step(1)
    params.next()
    params.next()
    first_norm()
    far_step(0)
    projected(0)
    z_step(3)
    near_step(2)
    far_step(1)
    projected(1)
    cot_whole()
    z_step(4)
    near_step(3)
    far_step(2)
    projected(2)
    attention(0, 4)
    z_step(5)
    near_step(4)
    attention(4, 8)
    far_step(3)
    attention(8, 12)
    z_step(6)
    near_step(5)
    branch()
    far_step(4)
    up_part(0)
    z_step(7)
    near_step(6)
    far_step(5)
    up_part(1)
    z_step(8)
    near_step(7)
    far_step(6)
    up_part(2)
    z_step(9)
    near_step(8)
    far_step(7)
    up_part(3)
    act_out()
    z_step(10)
    near_step(9)
    down_grad(0)
    far_step(8)
    near_step(10)
    down_grad(1)
    far_step(9)
    down_grad(2)
    down[0].after_far()
    far_step(10)
    hidden_grad(0)
    hidden_grad(1)
    down[1].after_far()
    down[0].after_near()
    up_grad(0)
    hidden_grad(2)
    up_grad(1)
    hidden_grad(3)
    up_grad(2)
    down[2].after_far()
    down[1].after_near()
    up_grad(3)
    layer_result()
    result_out()
    second_norm_back()
    ups[0].after_far()
    down[2].after_near()
    down[0].after_z()
    attention_back(0, 4)
    out_grad()
    ups[1].after_far()
    ups[0].after_near()
    attention_back(4, 8)
    ups[2].after_far()
    ups[1].after_near()
    attention_back(8, 12)
    proj_out()
    for i in range(3):
        mix_grad(i)
    first_norm_back()
    ups[3].after_far()
    ups[2].after_near()
    down[1].after_z()
    totals.begin(m.sums[...])
    outs.after_far()
    ups[3].after_near()
    down[2].after_z()
    totals.next()
    mixes[0].after_far()
    outs.after_near()
    ups[0].after_z()
    totals.next()
    mixes[1].after_far()
    mixes[0].after_near()
    ups[1].after_z()
    totals.next()
    mixes[2].after_far()
    mixes[1].after_near()
    ups[2].after_z()
    totals.next()
    ups[3].after_z()
    outs.after_z()
    mixes[2].after_near()
    o_small[...] = totals.next()
    for s in mixes:
        s.after_z()
    wires.arrived(lo_out.at[rows_own], back)
    wires.arrived(ig_out.at[rows_own], back + 1)
    wires.arrived(tg_out.at[p.y], back + 2)
    for copy in (lo_copy, ig_copy, tg_copy):
        copy.wait()
    wires.finish()


def pack_halves(shard):
    r, n = shard.shape
    return shard.reshape(r, 2, n // 2).transpose(1, 0, 2).reshape(2 * r, n // 2)


def place_in_zeros(shard, index):
    n = shard.shape[0]
    return lax.dynamic_update_slice(jnp.zeros((32 * n,), shard.dtype), shard, (index * n,))


def in_one_kernel(inputs, time_embed, segment_ids, cotangent, gain1, shift1, mix, mbias, out, obias, gain2, shift2, up, ubias,
                  down, dbias):
    y = lax.axis_index(SEQ)
    index = lax.axis_index(BATCH) * 2 + y
    smalls = (gain1, shift1, mbias, obias, gain2, shift2, ubias, dbias)
    flat = jnp.concatenate([place_in_zeros(v, index) for v in smalls] + [jnp.zeros((4 * WIDTH,), BF16)]).reshape(SMALL)
    w1 = jnp.concatenate([pack_halves(mix), pack_halves(out)], axis=1)
    time = lax.dynamic_slice_in_dim(time_embed, 2 * y, 2, 0).astype(F32).reshape(2, 1, WIDTH)
    ids = lax.dynamic_slice_in_dim(segment_ids, 2 * y, 2, 0)
    ids_down = jnp.broadcast_to(ids.reshape(TOKENS, 1), (TOKENS, 128))
    table = scratch_table(SLOTS)
    anywhere, vmem = pl.BlockSpec(memory_space=pl.ANY), pl.BlockSpec(memory_space=pltpu.VMEM)
    tokens = inputs.shape
    o_mix, o_out, o_up, o_down, sums, lo, ig, tg = pl.pallas_call(
        partial(layer_kernel, [name for name, _, _ in table]),
        out_shape=[jax.ShapeDtypeStruct(w.shape, F32) for w in (mix, out, up, down)]
        + [jax.ShapeDtypeStruct(SMALL, F32), jax.ShapeDtypeStruct(tokens, BF16), jax.ShapeDtypeStruct(tokens, F32),
           jax.ShapeDtypeStruct((2, 8, PART), F32)],
        in_specs=[vmem] * 7 + [anywhere] * 2,
        out_specs=[vmem] * 5 + [anywhere] * 3,
        scratch_shapes=[pltpu.SemaphoreType.DMA(shape) if kind is None else pltpu.VMEM(shape, kind) for _, shape, kind in table],
        compiler_params=pltpu.CompilerParams(collective_id=0, has_side_effects=True, vmem_limit_bytes=60 * 2**20),
    )(w1, pack_halves(up), down, flat, time, ids_down, ids.reshape(2, 1, 128), inputs, cotangent)
    parts, at = [], 0
    flat = sums.reshape(-1)
    for v in smalls:
        n = v.shape[0]
        parts.append(lax.dynamic_slice(flat, (at + index * n,), (n,)))
        at += 32 * n
    time_grad = tg[:, :2].reshape(4, PART)
    return (lo, ig, time_grad, parts[0], parts[1], o_mix, parts[2], o_out, parts[3], parts[4], parts[5], o_up, parts[6], o_down,
            parts[7])


def solution(mesh):
    fits = mesh.shape[BATCH] == 16 and mesh.shape[SEQ] == 2
    tokens, rows, vector, matrix = P(BATCH, SEQ, None), P(BATCH, None), P(AXES), P(AXES, None)
    params = (vector, vector, matrix, vector, matrix, vector, vector, vector, matrix, vector, matrix, vector)
    return jax.shard_map(
        in_one_kernel if fits else any_mesh,
        mesh=mesh,
        in_specs=(tokens, rows, rows, tokens) + params,
        out_specs=(tokens, tokens, P(BATCH, SEQ)) + params,
        check_vma=False,
    )
```

```python
from functools import partial
import math
from types import SimpleNamespace

import jax
import jax.numpy as jnp
from jax import lax
from jax.experimental import pallas as pl
from jax.experimental.pallas import tpu as pltpu
from jax.sharding import PartitionSpec as P

HEAD_DIM = 64
EPSILON = 1e-05
NEG_FILL = -1e30
BATCH, SEQ = "batch", "seq"
AXES = (BATCH, SEQ)
F32, BF16 = jnp.float32, jnp.bfloat16


def norm_back(d_out, normal, inv, gain):
    g = d_out * gain
    return inv * (g - jnp.mean(g, -1, keepdims=True) - normal * jnp.mean(g * normal, -1, keepdims=True))


def normal_part(hidden):
    centred = hidden - jnp.mean(hidden, -1, keepdims=True)
    inv = lax.rsqrt(jnp.mean(centred * centred, -1, keepdims=True) + EPSILON)
    return centred * inv, inv


def contract(a, b, over_a, over_b, batch=((), ())):
    return lax.dot_general(a, b, ((over_a, over_b), batch), preferred_element_type=F32)


def layer(inputs, time, ids, cot, params):
    (gain1, shift1, mix, mbias, out, obias, gain2, shift2, up, ubias, down, dbias) = params
    gain1, shift1, mbias, obias, gain2, shift2, ubias, dbias = (
        v.astype(F32) for v in (gain1, shift1, mbias, obias, gain2, shift2, ubias, dbias))
    rows, length, width = inputs.shape
    heads = width // HEAD_DIM
    scale = 1.0 / math.sqrt(HEAD_DIM)
    flat = lambda t: t.reshape(rows * length, -1)
    by_head = lambda t: t.reshape(rows, length, heads, HEAD_DIM).transpose(0, 2, 1, 3).reshape(rows * heads, length, HEAD_DIM)
    unhead = lambda t: flat(t.reshape(rows, heads, length, HEAD_DIM).transpose(0, 2, 1, 3))
    each = ((0,), (0,))
    cot = flat(cot)
    res_in = flat(inputs.astype(F32) + time.astype(F32)[:, None, :])
    norm1, inv1 = normal_part(res_in)
    normed1 = (norm1 * gain1 + shift1).astype(BF16)
    proj = contract(normed1, mix, (1,), (0,))
    q = by_head((proj[:, :width] + mbias[:width]).astype(BF16))
    k = by_head(proj[:, width:2 * width].astype(BF16))
    v = by_head((proj[:, 2 * width:] + mbias[width:]).astype(BF16))
    scores = contract(q, k, (2,), (2,), each) * scale
    same = jnp.repeat(ids[:, :, None] == ids[:, None, :], heads, axis=0)
    masked = jnp.where(same, scores, NEG_FILL)
    top = jnp.max(masked, -1, keepdims=True)
    log_total = top + jnp.log(jnp.sum(jnp.exp(masked - top), -1, keepdims=True))
    probs = jnp.exp(masked - log_total)
    probs16 = probs.astype(BF16)
    att = unhead(contract(probs16, v, (2,), (1,), each).astype(BF16))
    res_mid = res_in + (contract(att, out, (1,), (0,)) + obias)
    norm2, inv2 = normal_part(res_mid)
    normed2 = (norm2 * gain2 + shift2).astype(BF16)
    hid = contract(normed2, up, (1,), (0,)) + ubias
    cdf = 0.5 * (1.0 + lax.erf(hid * math.sqrt(0.5)))
    act = (hid * cdf).astype(BF16)
    layer_out = (res_mid + contract(act, down, (1,), (0,)) + dbias).astype(BF16)

    cot32 = cot.astype(F32)
    slope = cdf + hid * jnp.exp(-0.5 * hid * hid) * (1.0 / math.sqrt(2 * math.pi))
    d_hid = (contract(cot, down, (1,), (1,)) * slope).astype(BF16)
    d_n2 = contract(d_hid, up, (1,), (1,))
    d_mid = cot32 + norm_back(d_n2, norm2, inv2, gain2)
    d_br = d_mid.astype(BF16)
    d_att = by_head(contract(d_br, out, (1,), (1,)).astype(BF16))
    d_pr = contract(d_att, v, (2,), (2,), each)
    d_sc = (probs * (d_pr - jnp.sum(probs * d_pr, -1, keepdims=True))).astype(BF16)
    d_q = unhead((contract(d_sc, k, (2,), (1,), each) * scale).astype(BF16))
    d_k = unhead((contract(d_sc, q, (1,), (1,), each) * scale).astype(BF16))
    d_v = unhead(contract(probs16, d_att, (1,), (1,), each).astype(BF16))
    d_proj = jnp.concatenate([d_q, d_k, d_v], -1)
    d_n1 = contract(d_proj, mix, (1,), (1,))
    x_grad = d_mid + norm_back(d_n1, norm1, inv1, gain1)

    def col(t):
        return jnp.sum(t.astype(F32), axis=0)

    weigh = lambda a, b: contract(a, b, (0,), (0,))
    grads = (col(d_n1 * norm1), col(d_n1), weigh(normed1, d_proj), jnp.concatenate([col(d_q), col(d_v)]),
             weigh(att, d_br), col(d_br), col(d_n2 * norm2), col(d_n2), weigh(normed2, d_hid), col(d_hid),
             weigh(act, cot), col(cot32))
    return layer_out.reshape(inputs.shape), x_grad.reshape(inputs.shape), grads


def gather_all(shard):
    return lax.all_gather(shard, AXES, axis=0, tiled=True)


def scatter_sum(grad):
    return lax.psum_scatter(grad, AXES, scatter_dimension=0, tiled=True)


def rows_whole(tensor):
    return lax.all_to_all(tensor, SEQ, split_axis=0, concat_axis=1, tiled=True)


def rows_split(tensor):
    return lax.all_to_all(tensor, SEQ, split_axis=1, concat_axis=0, tiled=True)


def any_mesh(inputs, time_embed, segment_ids, cotangent, *shards):
    y, count = lax.axis_index(SEQ), inputs.shape[0] // lax.axis_size(SEQ)
    mine = [lax.dynamic_slice_in_dim(t, y * count, count, 0) for t in (time_embed, segment_ids)]
    layer_out, x_grad, grads = layer(
        rows_whole(inputs), mine[0], mine[1], rows_whole(cotangent), [gather_all(w) for w in shards])
    time_grad = lax.all_to_all(jnp.sum(x_grad, 1), SEQ, split_axis=1, concat_axis=0, tiled=True)
    return (rows_split(layer_out), rows_split(x_grad), time_grad) + tuple(scatter_sum(g) for g in grads)


MESH = pl.DeviceIdType.MESH
Z_CHIPS = 4
TOKENS, WIDTH, HIDDEN, PART = 256, 768, 3072, 384
SMALL = (16, WIDTH)
PIECE = 24
TRANSPOSED = ((1,), (1,))
TOKEN_SUM = ((0,), (0,))


class Place:
    def __init__(self):
        b, self.y = lax.axis_index(BATCH), lax.axis_index(SEQ)
        self.z, self.x, self.c = b // 4, (b // 2) % 2, b % 2
        z, x, c, y = self.z, self.x, self.c, self.y
        self.twin = self.at(z, x, 1 - c, y)
        self.x_peer = self.at(z, 1 - x, c, y)
        self.y_peer = self.at(z, x, c, 1 - y)
        self.z_slots = [lax.rem(z + d, Z_CHIPS) for d in (1, 2, 3)]
        self.z_peers = [self.at(q, x, c, y) for q in self.z_slots]

    @staticmethod
    def at(z, x, c, y):
        return ((z * 2 + x) * 2 + c, y)

    def routes(self, turn):
        c = 1 if turn else self.c
        x, y = self.x, self.y
        return (x + (1 - 2 * x) * (1 - c), y + (1 - 2 * y) * c), (x + (1 - 2 * x) * c, y + (1 - 2 * y) * (1 - c))

    def on_chip(self, chip):
        return self.at(self.z, chip[0], self.c, chip[1])

    def role(self, c, x, y):
        dx, dy = (x + self.x) % 2, (y + self.y) % 2
        return (dx + 2 * dy) * (1 - c) + (dy + 2 * dx) * c

    def of_role(self, c, role):
        low, high = role % 2, role // 2
        dx, dy = low * (1 - c) + high * c, high * (1 - c) + low * c
        return (self.x + dx) % 2, (self.y + dy) % 2

    def greet(self):
        barrier = pltpu.get_barrier_semaphore()
        partners = self.z_peers + [self.x_peer, self.y_peer, self.twin]
        for partner in partners:
            pl.semaphore_signal(barrier, inc=1, device_id=partner, device_id_type=MESH)
        pl.semaphore_wait(barrier, len(partners))


class Wires:
    def __init__(self, send_sem, recv_sem, place):
        self.send_sem, self.recv_sem, self.place = send_sem, recv_sem, place
        self.sent, self.used = [], 0

    def slots(self, count):
        self.used += count
        return self.used - count

    def start(self, src, dst, slot, device):
        copy = pltpu.make_async_remote_copy(
            src_ref=src, dst_ref=dst, send_sem=self.send_sem.at[slot], recv_sem=self.recv_sem.at[slot],
            device_id=device, device_id_type=MESH,
        )
        copy.start()
        self.sent.append(copy)
        return copy

    def arrived(self, dst, slot):
        pltpu.make_async_remote_copy(
            src_ref=dst, dst_ref=dst, send_sem=self.send_sem.at[slot], recv_sem=self.recv_sem.at[slot],
            device_id=self.place.twin, device_id_type=MESH,
        ).wait_recv()

    def left(self, copies):
        for copy in copies:
            copy.wait_send()
        self.sent = [kept for kept in self.sent if all(kept is not copy for copy in copies)]

    def finish(self):
        for copy in self.sent:
            copy.wait_send()
        self.sent = []


class Gather:
    def __init__(self, wires, place, own, buf, at, wide, turn=False):
        self.w, self.p, self.own, self.buf, self.cols = wires, place, own, buf, pl.ds(at, wide)
        self.base, self.copies = wires.slots(10), []
        self.near, self.far = place.routes(turn)

    def send(self, src, dst, slot, device):
        self.copies.append(self.w.start(src, dst, self.base + slot, device))

    def mine(self):
        p = self.p
        return self.buf.at[p.z, p.x, p.c, p.y, :, self.cols]

    def block(self, x, y, c):
        return self.buf.at[:, x, c, y, :, self.cols]

    def begin(self):
        for j, peer in enumerate(self.p.z_peers):
            self.send(self.own.at[:, self.cols], self.mine(), j, peer)

    def after_z(self):
        p = self.p
        for j in range(3):
            self.w.arrived(self.mine(), self.base + j)
        b = self.block(p.x, p.y, p.c)
        self.send(b, b, 3, p.on_chip(self.near))
        self.send(b, b, 4, p.on_chip(self.far))
        self.send(b, b, 6, p.twin)

    def after_near(self):
        p = self.p
        b = self.block(*self.near, p.c)
        self.w.arrived(b, self.base + 3)
        self.send(b, b, 5, p.on_chip(self.far))
        self.send(b, b, 7, p.twin)

    def after_far(self):
        p = self.p
        b = self.block(*self.far, p.c)
        self.w.arrived(b, self.base + 4)
        self.send(b, b, 8, p.twin)
        b = self.block(1 - p.x, 1 - p.y, p.c)
        self.w.arrived(b, self.base + 5)
        self.send(b, b, 9, p.twin)
        for j in range(6, 10):
            self.w.arrived(self.block(p.x, p.y, 1 - p.c), self.base + j)

    def halves_in_place(self):
        self.w.left(self.copies)
        rows = self.buf.shape[-2] // 2

        @pl.loop(0, 16)
        def _(pair):
            z, x, c = pair // 4, (pair // 2) % 2, pair % 2
            v = [self.buf[z, x, c, y, :, self.cols].astype(F32) for y in (0, 1)]
            for h in (0, 1):
                part = slice(h * rows, h * rows + rows)
                self.buf[z, x, c, h, :, self.cols] = jnp.concatenate([v[0][part], v[1][part]], 0).astype(BF16)


class LayerFirst(Gather):
    def begin(self):
        for j, chip in enumerate((self.near, self.far)):
            self.send(self.own.at[:, self.cols], self.mine(), j, self.p.on_chip(chip))

    def shard(self, chip):
        return self.buf.at[self.p.z, chip[0], self.p.c, chip[1], :, self.cols]

    def layer(self, z, c):
        return self.buf.at[z, :, c, :, :, self.cols]

    def forward(self):
        b = self.shard(self.near)
        self.w.arrived(b, self.base)
        self.send(b, b, 2, self.p.on_chip(self.far))

    def along_z(self):
        p = self.p
        self.w.arrived(self.shard(self.far), self.base + 1)
        self.w.arrived(self.shard((1 - p.x, 1 - p.y)), self.base + 2)
        b = self.layer(p.z, p.c)
        for j, peer in enumerate(p.z_peers):
            self.send(b, b, 3 + j, peer)
        self.send(b, b, 6, p.twin)

    def after_z(self):
        p = self.p
        for j in range(3):
            b = self.layer(lax.rem(p.z + 3 - j, Z_CHIPS), p.c)
            self.w.arrived(b, self.base + 3 + j)
            self.send(b, b, 7 + j, p.twin)
        for j in range(6, 10):
            self.w.arrived(self.layer(p.z, 1 - p.c), self.base + j)


class Scatter:
    def __init__(self, wires, place, rows, cols, keep, s1, r1, s2, r2, sz, rz, out, out_cols, turn=False):
        self.w, self.p, self.rows, self.cols, self.out_cols = wires, place, rows, cols, out_cols
        self.keep, self.s1, self.r1, self.s2, self.r2, self.sz, self.rz, self.out = keep, s1, r1, s2, r2, sz, rz, out
        self.base, self.quarter, self.packed = wires.slots(5), Z_CHIPS * rows, rows % 16 != 0
        wide = cols.size // 2 if self.packed else cols.size
        self.z_cols = pl.ds(cols.start // 2 if self.packed else cols.start, wide)
        near, far = place.routes(turn)
        self.near, self.far = place.on_chip(near), place.on_chip(far)
        swapped = (1 - place.c) if turn else 0
        self.roles = (0, 1 + swapped, 2 - swapped, 3)

    def begin(self, left, right):
        q = self.quarter
        for i, role in enumerate(self.roles):
            total = contract(left(0, role), right[0], (1,), (0,)) + contract(left(1, role), right[1], (1,), (0,))
            at = pl.ds((i % 2) * q, q)
            if i < 2:
                self.keep[at, self.cols] = total
            else:
                self.s1[at, self.cols] = total.astype(BF16)
        both = pl.ds(0, 2 * q)
        self.w.start(self.s1.at[both, self.cols], self.r1.at[both, self.cols], self.base, self.far)

    def after_far(self):
        q = self.quarter
        self.w.arrived(self.r1.at[pl.ds(0, 2 * q), self.cols], self.base)
        at = pl.ds(q, q)
        self.s2[:, self.cols] = (self.keep[at, self.cols] + self.r1[at, self.cols].astype(F32)).astype(BF16)
        self.w.start(self.s2.at[:, self.cols], self.r2.at[:, self.cols], self.base + 1, self.near)

    def after_near(self):
        q, n = self.quarter, self.rows
        self.w.arrived(self.r2.at[:, self.cols], self.base + 1)
        at = pl.ds(0, q)
        total = self.keep[at, self.cols] + self.r1[at, self.cols].astype(F32) + self.r2[:, self.cols].astype(F32)
        for z in range(Z_CHIPS):
            piece = total[z * n:z * n + n]

            @pl.when(z == self.p.z)
            def _():
                self.out[:, self.out_cols] = piece

            if self.packed:
                half = self.z_cols.size
                piece = jnp.concatenate([piece[:, :half], piece[:, half:]], 0)
            self.sz[z, :, self.z_cols] = piece.astype(BF16)
        for j, (z, peer) in enumerate(zip(self.p.z_slots, self.p.z_peers)):
            self.w.start(self.sz.at[z, :, self.z_cols], self.rz.at[j, :, self.z_cols], self.base + 2 + j, peer)

    def after_z(self):
        total = 0.0
        for j in range(3):
            self.w.arrived(self.rz.at[j, :, self.z_cols], self.base + 2 + j)
            total = total + self.rz[j, :, self.z_cols].astype(F32)
        if self.packed:
            total = jnp.concatenate([total[:self.rows], total[self.rows:]], 1)
        self.out[:, self.out_cols] = self.out[:, self.out_cols] + total


class AlongZFirst(Scatter):
    def __init__(self, *args, zs, zr):
        super().__init__(*args)
        self.zs, self.zr = zs, zr

    def begin(self, left, right):
        n = self.rows
        for role in range(4):
            total = contract(left(0, role), right[0], (1,), (0,)) + contract(left(1, role), right[1], (1,), (0,))
            for z in range(Z_CHIPS):
                piece = total[z * n:z * n + n]
                self.zs[z, role] = piece.astype(BF16)

                @pl.when(z == self.p.z)
                def _():
                    self.keep[pl.ds(role * n, n), self.cols] = piece

        for j, (z, peer) in enumerate(zip(self.p.z_slots, self.p.z_peers)):
            self.w.start(self.zs.at[z], self.zr.at[j], self.base + 2 + j, peer)

    def after_z(self):
        n = self.rows
        for j in range(3):
            self.w.arrived(self.zr.at[j], self.base + 2 + j)
        for role in range(4):
            at = pl.ds(role * n, n)
            total = self.keep[at, self.cols]
            for j in range(3):
                total = total + self.zr[j, role].astype(F32)
            if role < 2:
                self.keep[at, self.cols] = total
            else:
                self.s1[pl.ds((role - 2) * n, n), self.cols] = total.astype(BF16)
        both = pl.ds(0, 2 * n)
        self.w.start(self.s1.at[both, self.cols], self.r1.at[both, self.cols], self.base, self.far)

    def after_far(self):
        n = self.rows
        self.w.arrived(self.r1.at[pl.ds(0, 2 * n), self.cols], self.base)
        at, first = pl.ds(n, n), pl.ds(0, n)
        self.s2[first, self.cols] = (self.keep[at, self.cols] + self.r1[at, self.cols].astype(F32)).astype(BF16)
        self.w.start(self.s2.at[first, self.cols], self.r2.at[first, self.cols], self.base + 1, self.near)

    def after_near(self):
        at = pl.ds(0, self.rows)
        self.w.arrived(self.r2.at[at, self.cols], self.base + 1)
        self.out[:, self.out_cols] = (
            self.keep[at, self.cols] + self.r1[at, self.cols].astype(F32) + self.r2[at, self.cols].astype(F32))


class SmallScatter:
    def __init__(self, wires, place, slabs, from_twin, s1, r1, s2, r2, sz, rz, out):
        self.w, self.p, self.slabs, self.from_twin = wires, place, slabs, from_twin
        self.s1, self.r1, self.s2, self.r2, self.sz, self.rz, self.out = s1, r1, s2, r2, sz, rz, out
        self.base = wires.slots(6)
        near, far = place.routes(False)
        self.chips = ((place.x, place.y), near, far, (1 - place.x, 1 - place.y))
        self.near, self.far = place.on_chip(near), place.on_chip(far)

    def summed(self, role):
        x, y = self.chips[role]
        return self.slabs[:, x, self.p.c, y] + self.from_twin[:, x, y]

    def to_twin(self):
        self.w.start(self.slabs.at[:, :, 1 - self.p.c], self.from_twin, self.base, self.p.twin)

    def begin(self):
        self.w.arrived(self.from_twin, self.base)
        self.s1[0], self.s1[1] = self.summed(2), self.summed(3)
        self.w.start(self.s1, self.r1, self.base + 1, self.far)

    def after_far(self):
        self.w.arrived(self.r1, self.base + 1)
        self.s2[...] = self.summed(1) + self.r1[1]
        self.w.start(self.s2, self.r2, self.base + 2, self.near)

    def after_near(self):
        self.w.arrived(self.r2, self.base + 2)
        self.sz[...] = self.summed(0) + self.r1[0] + self.r2[...]
        for j, (z, peer) in enumerate(zip(self.p.z_slots, self.p.z_peers)):
            self.w.start(self.sz.at[z], self.rz.at[j], self.base + 3 + j, peer)

    def after_z(self):
        total = self.sz[self.p.z]
        for j in range(3):
            self.w.arrived(self.rz.at[j], self.base + 3 + j)
            total = total + self.rz[j]
        self.out[...] = total


def merged(value):
    return value.reshape(-1, value.shape[-1])


def by_rows(step, body, *carry):
    return lax.fori_loop(0, TOKENS // step, lambda i, kept: body(i, pl.ds(pl.multiple_of(i * step, step), step), *kept), carry)


def folded(value):
    return jnp.sum(value.reshape(value.shape[0] // 8, 8, value.shape[1]), 0)


def column_sums(value):
    return contract(jnp.ones((8, value.shape[0]), BF16), value, (1,), (0,))[0:1]


def token_block(i):
    return i // 4, (i // 2) % 2, pl.ds(pl.multiple_of((i % 2) * 32, 32), 32)


def scratch_table(slots):
    k, w = WIDTH // 2, WIDTH
    return [
        ("par", SMALL, F32), ("sums", SMALL, F32), ("bs", (4, 2, 2, 2, 16, 128), BF16),
        ("slabs", (4, 2, 2, 2, 16, 128), F32), ("from_twin", (4, 2, 2, 16, 128), F32), ("s1_s", (2, 4, 16, 128), F32),
        ("r1_s", (2, 4, 16, 128), F32), ("s2_s", (4, 16, 128), F32), ("r2_s", (4, 16, 128), F32),
        ("sz_s", (4, 16, 128), F32), ("rz_s", (3, 16, 128), F32),
        ("w1", (48, 1536), BF16), ("w2", (48, 1536), BF16), ("same", (2, 128, 128), F32), ("time", (2, 1, w), F32),
        ("b1", (4, 2, 2, 2, 48, 1536), BF16), ("b2", (4, 2, 2, 2, 48, 1536), BF16), ("b3", (4, 2, 2, 2, 96, w), BF16),
        ("x0", (2, 2, 64, w), BF16), ("cot", (2, 2, 2, 64, w), BF16),
        ("res_in", (TOKENS, w), F32), ("normed1", (TOKENS, w), BF16), ("qkv", (TOKENS, 3 * w), BF16),
        ("probs", (12, TOKENS, 128), F32), ("att", (TOKENS, w), BF16), ("res_mid", (TOKENS, w), F32),
        ("normed2", (TOKENS, w), BF16), ("slope", (TOKENS, HIDDEN), F32), ("act", (TOKENS, HIDDEN), BF16),
        ("pick", (2, k, w), BF16), ("pick_act", (2, 192, PART), BF16),
        ("t1", (2, k, TOKENS), BF16), ("t1_send", (k, TOKENS), BF16),
        ("to", (2, k, TOKENS), BF16), ("to_send", (k, TOKENS), BF16),
        ("t2", (2, k, TOKENS), BF16), ("t2_send", (k, TOKENS), BF16),
        ("ta", (2, 4, 4, 96, TOKENS), BF16), ("ta_send", (4, 4, 96, TOKENS), BF16),
        ("d_hid", (2, TOKENS, HIDDEN), BF16), ("d_norm", (TOKENS, w), F32),
        ("d_branch", (2, TOKENS, w), BF16), ("d_proj", (2, TOKENS, 3 * w), BF16),
        ("ig", (2, 2, 64, w), F32), ("tg", (2, 8, PART), F32),
        ("keep_d", (768, w), F32), ("s1_d", (768, w), BF16), ("r1_d", (768, w), BF16), ("s2_d", (PART, w), BF16),
        ("r2_d", (PART, w), BF16), ("sz_d", (4, 96, w), BF16), ("rz_d", (3, 96, w), BF16),
        ("zr_d", (3, 4, 96, 256), BF16), ("ig_send", (2, 64, w), BF16),
        ("keep_u", (192, HIDDEN), F32), ("s1_u", (192, HIDDEN), BF16), ("r1_u", (192, HIDDEN), BF16),
        ("s2_u", (96, HIDDEN), BF16), ("r2_u", (96, HIDDEN), BF16), ("sz_u", (4, 48, 1536), BF16), ("rz_u", (3, 48, 1536), BF16),
        ("r1_m", (192, HIDDEN), BF16),
        ("s2_m", (96, HIDDEN), BF16), ("r2_m", (96, HIDDEN), BF16), ("sz_m", (4, 48, 1536), BF16), ("rz_m", (3, 48, 1536), BF16),
        ("send_sem", (slots,), None), ("recv_sem", (slots,), None), ("local_sem", (10,), None),
    ]


SLOTS = 240
AHEAD = 4
TURNED = ()


def iota(shape, dim):
    return lax.broadcasted_iota(jnp.int32, shape, dim)


def piece_place(row, device):
    block = jnp.where(row < 6, device, jnp.where(row < 8, 2 * device + row - 6, 4 * device + row - 8))
    first = jnp.where(row < 6, row, jnp.where(row < 8, 6, 8))
    return jnp.where(row < 12, first + (block >> 5), -1), block & 31


def ones_where(condition):
    return condition.astype(F32).astype(BF16)


def lane_piece(shape):
    return (iota(shape, 1) * 2731) >> 16


def every_piece():
    shape = (128, WIDTH)
    return ones_where(iota(shape, 1) - PIECE * lane_piece(shape) == iota(shape, 0))


def slab_rows(first, count):
    n = iota((SMALL[0], count), 1) + first
    return ones_where(piece_place(n & 15, n >> 4)[0] == iota((SMALL[0], count), 0))


def slab_places(first, count):
    n = iota((count, WIDTH), 0) + first
    return (piece_place(n & 15, n >> 4)[1] == lane_piece((count, WIDTH))).astype(F32)


def whole_of(ref):
    total = 0.0
    for z in range(Z_CHIPS):
        wide = contract(merged(ref[z]), every_piece(), (1,), (0,)) * slab_places(128 * z, 128)
        total = total + contract(slab_rows(128 * z, 128), wide.astype(BF16), (1,), (0,))
    return total


def put_slabs(ref, whole):
    high = whole.astype(BF16)
    parts = (high, (whole - high.astype(F32)).astype(BF16))
    for z in range(Z_CHIPS):
        places, total = slab_places(128 * z, 128), 0.0
        for part in parts:
            wide = contract(slab_rows(128 * z, 128), part, *TOKEN_SUM) * places
            total = total + contract(wide.astype(BF16), every_piece(), *TRANSPOSED)
        ref[z] = total.reshape(ref.shape[1:])


def layer_kernel(names, mix, out, up, w3, small, time, ids, xin, cin,
                 o_mix, o_out, o_up, o_down, o_small, lo_out, ig_out, ig_there, tg_out, *scratch):
    m = SimpleNamespace(**dict(zip(names, scratch)))
    p = Place()
    p.greet()
    wires = Wires(m.send_sem, m.recv_sem, p)
    me, twin = p.c, 1 - p.c
    scale = 1.0 / math.sqrt(HEAD_DIM)

    own, bufs = (m.w1, m.w2, w3), (m.b1, m.b2, m.b3)
    for ref, target, at in ((mix, m.w1, 0), (out, m.w1, 3 * PART), (up, m.w2, 0)):
        half = ref.shape[1] // 2
        value = ref[...].astype(F32)
        target[:, at:at + half] = jnp.concatenate([value[:, :half], value[:, half:]], 0).astype(BF16)
    plan = [(0, PART * i, PART) for i in range(4)] + [(1, PART * i, PART) for i in range(4)] + [(2, 256 * i, 256) for i in range(3)]
    gathers = [Gather(wires, p, own[w], bufs[w], at, wide, k in TURNED) for k, (w, at, wide) in enumerate(plan[:-1])]
    last = LayerFirst(wires, p, own[2], bufs[2], *plan[-1][1:])
    params = Gather(wires, p, small, m.bs, 0, 128)
    params.begin()
    for g in gathers[:AHEAD]:
        g.begin()
    locs = [pltpu.make_async_copy(own[i], bufs[i].at[p.z, p.x, p.c, p.y], m.local_sem.at[i]) for i in range(3)]
    rows_own, rows_other = pl.ds(2 * p.y, 2), pl.ds(2 - 2 * p.y, 2)
    locs.append(pltpu.make_async_copy(xin.at[rows_own], m.x0.at[:, p.y], m.local_sem.at[3]))
    locs.append(pltpu.make_async_copy(cin.at[rows_own], m.cot.at[me, :, p.y], m.local_sem.at[4]))
    for copy in locs:
        copy.start()
    swap = wires.slots(3)
    small_copy = pltpu.make_async_copy(small, m.bs.at[p.z, p.x, p.c, p.y], m.local_sem.at[8])
    small_copy.start()
    wires.start(xin.at[rows_other], m.x0.at[:, p.y], swap, p.y_peer)
    last.begin()
    wires.start(cin.at[rows_other], m.cot.at[me, :, p.y], swap + 1, p.y_peer)

    def z_step(k):
        gathers[k].after_z()
        if k + AHEAD < len(gathers):
            gathers[k + AHEAD].begin()

    def near_step(k):
        gathers[k].after_near()

    def far_step(k):
        gathers[k].after_far()
        if plan[k][0] < 2:
            gathers[k].halves_in_place()

    lane, row = lax.broadcasted_iota(jnp.int32, (24, WIDTH), 1), lax.broadcasted_iota(jnp.int32, (24, WIDTH), 0)
    lane_a, row_a = lax.broadcasted_iota(jnp.int32, (192, PART), 1), lax.broadcasted_iota(jnp.int32, (192, PART), 0)
    for side, c in ((0, me), (1, twin)):
        pieces = []
        for role in range(4):
            x, y = p.of_role(c, role)
            for z in range(Z_CHIPS):
                first = (((z * 2 + x) * 2 + c) * 2 + y) * 24
                pieces.append((lane == row + first).astype(F32))
        m.pick[side] = jnp.concatenate(pieces, 0).astype(BF16)
        m.pick_act[side] = (lane_a == row_a + c * 192).astype(F32).astype(BF16)

    for r in (0, 1):
        m.time[r] = jnp.where(p.y == 0, time[r:r + 1, :].astype(F32), time[r + 2:r + 3, :].astype(F32))
        along = jnp.where(p.y == 0, ids[r:r + 1, :], ids[r + 2:r + 3, :])
        one_hot = (lax.broadcasted_iota(jnp.int32, (8, 128), 0) == along).astype(F32).astype(BF16)
        m.same[r] = contract(one_hot, one_hot, *TOKEN_SUM)

    twin_base = wires.slots(16)

    def transposed(value, ref, send, slot):
        ref[me] = contract(m.pick[0], value, *TRANSPOSED).astype(BF16)
        send[...] = contract(m.pick[1], value, *TRANSPOSED).astype(BF16)
        wires.start(send, ref.at[me], twin_base + slot, p.twin)

    def left_of(ref, quarter=96):
        return lambda core, role: ref[core, pl.ds(role * quarter, quarter), :]

    def left_act(core, role):
        return merged(m.ta[core, role])

    def normal(h):
        centred = h - jnp.mean(h, -1, keepdims=True)
        inv = lax.rsqrt(jnp.mean(centred * centred, -1, keepdims=True) + EPSILON)
        return centred * inv, inv

    def first_norm():
        m.par[...] = whole_of(m.bs)
        for copy in locs[3:]:
            copy.wait()
        wires.arrived(m.x0.at[:, p.y], swap)

        def body(i, at):
            r, half, pos = token_block(i)
            h = m.x0[r, half, pos, :].astype(F32) + m.time[r]
            m.res_in[at, :] = h
            m.normed1[at, :] = (normal(h)[0] * m.par[0:1, :] + m.par[1:2, :]).astype(BF16)
            return ()

        by_rows(32, body)
        transposed(m.normed1[...], m.t1, m.t1_send, 0)

    def projected(k):
        for h in (0, 1):
            weight = merged(m.b1[:, :, :, h, :, pl.ds(PART * k, PART)])
            group, lanes = (3 * h + k) // 2, PART * ((3 * h + k) % 2)
            total = contract(m.normed1[...], weight, (1,), (0,))
            if group != 1:
                total = total + m.par[6 + group // 2:7 + group // 2, lanes:lanes + PART]
            m.qkv[:, WIDTH * group + lanes:WIDTH * group + lanes + PART] = total.astype(BF16)

    low = (lax.broadcasted_iota(jnp.int32, (1, 128), 1) < HEAD_DIM).astype(F32)
    heads_of = [low.astype(BF16), (1.0 - low).astype(BF16)]

    def two_heads(value):
        return jnp.concatenate([value * h for h in heads_of], 0)

    def side_by_side(value):
        return jnp.concatenate([value[:128], value[128:]], 1)

    def at_pair(i):
        return pl.ds(pl.multiple_of((i // 6) * 128, 128), 128), [
            pl.ds(pl.multiple_of((i % 6) * 128 + WIDTH * part, 128), 128) for part in range(3)]

    def attention(first, last):
        def body(i, _):
            rows, (cq, ck, cv) = at_pair(i)
            q2, k, v = two_heads(m.qkv[rows, cq]), m.qkv[rows, ck], m.qkv[rows, cv]
            scores = contract(q2, k, *TRANSPOSED) * scale
            same = m.same[i // 6] > 0.5
            masked = jnp.where(jnp.concatenate([same, same], 0), scores, NEG_FILL)
            e = jnp.exp(masked - jnp.max(masked, -1, keepdims=True))
            probs = e / jnp.sum(e, -1, keepdims=True)
            m.probs[i] = probs
            m.att[rows, cq] = contract(side_by_side(probs.astype(BF16)), two_heads(v), (1,), (0,)).astype(BF16)
            return 0

        lax.fori_loop(first, last, body, 0)

    def out_half(h):
        return merged(m.b1[:, :, :, h, :, pl.ds(3 * PART, PART)])

    def branch():
        transposed(m.att[...], m.to, m.to_send, 1)
        for h in (0, 1):
            at = slice(PART * h, PART * h + PART)
            total = contract(m.att[...], out_half(h), (1,), (0,)) + m.par[2:3, at]
            m.res_mid[:, at] = m.res_in[:, at] + total

        def body(i, at):
            m.normed2[at, :] = (normal(m.res_mid[at, :])[0] * m.par[3:4, :] + m.par[4:5, :]).astype(BF16)
            return ()

        by_rows(32, body)
        transposed(m.normed2[...], m.t2, m.t2_send, 2)

    def up_part(k):
        for h in (0, 1):
            first = 1536 * h + PART * k
            cols, lanes = slice(first, first + PART), first % WIDTH
            weight = merged(m.b2[:, :, :, h, :, pl.ds(PART * k, PART)])
            bias = m.par[8 + first // WIDTH:9 + first // WIDTH, lanes:lanes + PART]
            m.slope[:, cols] = contract(m.normed2[...], weight, (1,), (0,)) + bias

            def body(i, at):
                v = m.slope[at, cols]
                cdf = 0.5 + 0.5 * lax.erf(v * math.sqrt(0.5))
                m.act[at, cols] = (v * cdf).astype(BF16)
                m.slope[at, cols] = cdf + v * jnp.exp(-0.5 * v * v) * (1.0 / math.sqrt(2 * math.pi))
                return ()

            by_rows(32, body)
            z, x = (first // PART) // 2, (first // PART) % 2
            act = m.act[:, cols]
            for side, c in ((0, me), (1, twin)):
                picked = contract(m.pick_act[side], act, *TRANSPOSED).astype(BF16)
                for y in (0, 1):
                    role = p.role(c, x, y)
                    piece = picked[96 * y:96 * y + 96]
                    if side == 0:
                        m.ta[me, role, z] = piece
                    else:
                        m.ta_send[role, z] = piece

    def cot_whole():
        wires.arrived(m.cot.at[me, :, p.y], swap + 1)
        wires.start(m.cot.at[me], m.cot.at[me], twin_base + 3, p.twin)

    twin_act = []

    def act_out():
        twin_act.append(wires.start(m.ta_send, m.ta.at[me], twin_base + 4, p.twin))

    def scatter_of(kind, first, wide, out, out_first):
        cols, out_cols = pl.ds(first, wide), pl.ds(out_first, wide)
        if kind == 0:
            args = wires, p, 96, cols, m.keep_d, m.s1_d, m.r1_d, m.s2_d, m.r2_d, m.sz_d, m.rz_d, out, out_cols
            return Scatter(*args) if first else AlongZFirst(*args, zs=m.ta_send, zr=m.zr_d)
        if kind == 1:
            return Scatter(wires, p, 24, cols, m.keep_u, m.s1_u, m.r1_u, m.s2_u, m.r2_u, m.sz_u, m.rz_u, out, out_cols)
        return Scatter(wires, p, 24, cols, m.slope, m.act, m.r1_m, m.s2_m, m.r2_m, m.sz_m, m.rz_m, out, out_cols)

    down = [scatter_of(0, 256 * i, 256, o_down, 256 * i) for i in range(3)]
    ups = [scatter_of(1, WIDTH * i, WIDTH, o_up, WIDTH * i) for i in range(4)]
    mixes = [scatter_of(2, WIDTH * i, WIDTH, o_mix, WIDTH * i) for i in range(3)]
    outs = scatter_of(2, 3 * WIDTH, WIDTH, o_out, 0)

    def down_grad(i):
        if i == 0:
            wires.arrived(m.cot.at[twin], twin_base + 3)
            wires.arrived(m.ta.at[twin], twin_base + 4)
            wires.left(twin_act)
            m.sums[...] = jnp.zeros(SMALL, F32)
            m.sums[5:6, :] = column_sums(merged(m.cot[me]))
        cols = pl.ds(256 * i, 256)
        down[i].begin(left_act, [merged(m.cot[core, :, :, :, cols]) for core in (0, 1)])

    def hidden_grad(i):
        cot = merged(m.cot[me])
        for part in (2 * i, 2 * i + 1):
            cols = slice(PART * part, PART * part + PART)
            d_act = contract(cot, merged(m.b3[part // 2, part % 2]), *TRANSPOSED)
            grad = (d_act * m.slope[:, cols]).astype(BF16)
            m.d_hid[me, :, cols] = grad
            lanes = PART * (part % 2)
            m.sums[8 + i:9 + i, lanes:lanes + PART] = column_sums(grad)
        at = m.d_hid.at[me, :, pl.ds(WIDTH * i, WIDTH)]
        wires.start(at, at, twin_base + 5 + i, p.twin)

    def up_grad(i):
        if i == 0:
            wires.arrived(m.t2.at[twin], twin_base + 2)
        cols = pl.ds(WIDTH * i, WIDTH)
        wires.arrived(m.d_hid.at[twin, :, cols], twin_base + 5 + i)
        ups[i].begin(left_of(m.t2), [m.d_hid[core, :, cols] for core in (0, 1)])

    def layer_result():
        for i in range(3):
            cols = slice(256 * i, 256 * i + 256)
            total = contract(m.act[...], merged(m.b3[:, :, :, :, :, cols]), (1,), (0,)) + m.par[5:6, cols]
            total = (m.res_mid[:, cols] + total).astype(BF16)
            for r in (0, 1):
                for half in (0, 1):
                    first = r * 128 + half * 64
                    m.x0[r, half, :, cols] = total[first:first + 64]

    back = wires.slots(3)
    lo_copy = pltpu.make_async_copy(m.x0.at[:, p.y], lo_out.at[rows_own], m.local_sem.at[5])
    ig_copy = pltpu.make_async_copy(m.ig.at[:, p.y], ig_out, m.local_sem.at[6])
    tg_copy = pltpu.make_async_copy(m.tg.at[p.y], tg_out.at[p.y], m.local_sem.at[7])

    def result_out():
        lo_copy.start()
        wires.start(m.x0.at[:, 1 - p.y], lo_out.at[rows_own], back, p.y_peer)

    def second_norm_back():
        halves = [merged(m.b2[:, :, :, h]) for h in (0, 1)]
        m.d_norm[...] = contract(m.d_hid[me, :, 0:1536], halves[0], *TRANSPOSED)
        m.d_norm[...] += contract(m.d_hid[me, :, 1536:3072], halves[1], *TRANSPOSED)

        def body(i, at, gain_sum, shift_sum):
            r, half, pos = token_block(i)
            norm, inv = normal(m.res_mid[at, :])
            dn = m.d_norm[at, :]
            dn_norm = dn * norm
            g, gn = dn * m.par[3:4, :], dn_norm * m.par[3:4, :]
            back_in = inv * (g - jnp.mean(g, -1, keepdims=True) - norm * jnp.mean(gn, -1, keepdims=True))
            d_mid = m.cot[me, r, half, pos, :].astype(F32) + back_in
            m.res_mid[at, :] = d_mid
            m.d_branch[me, at, :] = d_mid.astype(BF16)
            return gain_sum + folded(dn_norm), shift_sum + folded(dn)

        zero = jnp.zeros((8, WIDTH), F32)
        gain_sum, shift_sum = by_rows(32, body, zero, zero)
        m.sums[3:4, :] = jnp.sum(gain_sum, 0, keepdims=True)
        m.sums[4:5, :] = jnp.sum(shift_sum, 0, keepdims=True)
        wires.start(m.d_branch.at[me], m.d_branch.at[me], twin_base + 9, p.twin)
        d_branch = m.d_branch[me]
        m.sums[2:3, :] = column_sums(d_branch)
        d_att = contract(d_branch[:, 0:PART], out_half(0), *TRANSPOSED) + contract(d_branch[:, PART:], out_half(1), *TRANSPOSED)
        m.normed2[...] = d_att.astype(BF16)

    def out_grad():
        wires.arrived(m.to.at[twin], twin_base + 1)
        wires.arrived(m.d_branch.at[twin], twin_base + 9)
        outs.begin(left_of(m.to), [m.d_branch[core] for core in (0, 1)])

    def attention_back(first, last):
        def body(i, _):
            rows, (cq, ck, cv) = at_pair(i)
            q2, k, v = two_heads(m.qkv[rows, cq]), m.qkv[rows, ck], m.qkv[rows, cv]
            da2 = two_heads(m.normed2[rows, cq])
            probs = m.probs[i]
            d_probs = contract(da2, v, *TRANSPOSED)
            delta = jnp.sum(probs * d_probs, -1, keepdims=True)
            d_scores = (probs * (d_probs - delta)).astype(BF16)
            m.d_proj[me, rows, cq] = (contract(side_by_side(d_scores), two_heads(k), (1,), (0,)) * scale).astype(BF16)
            m.d_proj[me, rows, ck] = (contract(d_scores, q2, *TOKEN_SUM) * scale).astype(BF16)
            m.d_proj[me, rows, cv] = contract(probs.astype(BF16), da2, *TOKEN_SUM).astype(BF16)
            return 0

        lax.fori_loop(first, last, body, 0)

    def proj_out():
        for i in range(3):
            at = m.d_proj.at[me, :, pl.ds(WIDTH * i, WIDTH)]
            wires.start(at, at, twin_base + 10 + i, p.twin)

    def mix_grad(i):
        if i == 0:
            wires.arrived(m.t1.at[twin], twin_base)
        cols = pl.ds(WIDTH * i, WIDTH)
        if i != 1:
            m.sums[6 + i // 2:7 + i // 2, :] = column_sums(m.d_proj[me, :, cols])
        wires.arrived(m.d_proj.at[twin, :, cols], twin_base + 10 + i)
        mixes[i].begin(left_of(m.t1), [m.d_proj[core, :, cols] for core in (0, 1)])

    def first_norm_back():
        halves = [merged(m.b1[:, :, :, h, :, 0:3 * PART]) for h in (0, 1)]
        m.d_norm[...] = contract(m.d_proj[me, :, 0:3 * PART], halves[0], *TRANSPOSED)
        m.d_norm[...] += contract(m.d_proj[me, :, 3 * PART:], halves[1], *TRANSPOSED)

        def body(i, at, gain_sum, shift_sum, row_sum):
            r, half, pos = token_block(i)
            norm, inv = normal(m.res_in[at, :])
            dn = m.d_norm[at, :]
            dn_norm = dn * norm
            g, gn = dn * m.par[0:1, :], dn_norm * m.par[0:1, :]
            grad = m.res_mid[at, :] + inv * (g - jnp.mean(g, -1, keepdims=True) - norm * jnp.mean(gn, -1, keepdims=True))
            m.ig[r, half, pos, :] = grad
            sums = folded(grad)
            first = (r == 0).astype(F32)
            return (gain_sum + folded(dn_norm), shift_sum + folded(dn),
                    row_sum + jnp.concatenate([sums * first, sums * (1.0 - first)], 0))

        zero = jnp.zeros((8, WIDTH), F32)
        gain_sum, shift_sum, row_sum = by_rows(32, body, zero, zero, jnp.zeros((16, WIDTH), F32))
        m.sums[0:1, :] = jnp.sum(gain_sum, 0, keepdims=True)
        m.sums[1:2, :] = jnp.sum(shift_sum, 0, keepdims=True)
        for r in (0, 1):
            total = jnp.sum(row_sum[8 * r:8 * r + 8], 0, keepdims=True)
            for half in (0, 1):
                m.tg[half, r:r + 1, :] = total[:, PART * half:PART * half + PART]
        ig_copy.start()
        m.ig_send[...] = m.ig[:, 1 - p.y].astype(BF16)
        wires.start(m.ig_send, ig_there, back + 1, p.y_peer)
        tg_copy.start()
        wires.start(m.tg.at[1 - p.y], tg_out.at[p.y], back + 2, p.y_peer)

    totals = SmallScatter(wires, p, m.slabs, m.from_twin, m.s1_s, m.r1_s, m.s2_s, m.r2_s, m.sz_s, m.rz_s, o_small)

    def small_out():
        put_slabs(m.slabs, m.sums[...])
        totals.to_twin()

    small_copy.wait()
    for copy in locs[:3]:
        copy.wait()
    params.after_z()
    z_step(0)
    params.after_near()
    last.forward()
    z_step(1)
    near_step(0)
    params.after_far()
    z_step(2)
    near_step(1)
    first_norm()
    far_step(0)
    projected(0)
    z_step(3)
    near_step(2)
    far_step(1)
    projected(1)
    cot_whole()
    z_step(4)
    near_step(3)
    far_step(2)
    projected(2)
    attention(0, 4)
    z_step(5)
    near_step(4)
    attention(4, 8)
    far_step(3)
    attention(8, 12)
    z_step(6)
    last.along_z()
    near_step(5)
    branch()
    far_step(4)
    up_part(0)
    z_step(7)
    near_step(6)
    far_step(5)
    up_part(1)
    z_step(8)
    near_step(7)
    far_step(6)
    up_part(2)
    z_step(9)
    near_step(8)
    far_step(7)
    up_part(3)
    act_out()
    down_grad(0)
    near_step(9)
    down_grad(1)
    down_grad(2)
    far_step(8)
    down[1].after_far()
    far_step(9)
    down[2].after_far()
    last.after_z()
    hidden_grad(0)
    hidden_grad(1)
    up_grad(0)
    down[1].after_near()
    hidden_grad(2)
    up_grad(1)
    hidden_grad(3)
    up_grad(2)
    down[2].after_near()
    up_grad(3)
    layer_result()
    result_out()
    second_norm_back()
    down[1].after_z()
    ups[0].after_far()
    attention_back(0, 4)
    out_grad()
    down[0].after_z()
    ups[1].after_far()
    ups[0].after_near()
    attention_back(4, 8)
    ups[2].after_far()
    ups[1].after_near()
    attention_back(8, 12)
    proj_out()
    for i in range(3):
        mix_grad(i)
    first_norm_back()
    small_out()
    ups[3].after_far()
    ups[2].after_near()
    totals.begin()
    down[0].after_far()
    outs.after_far()
    ups[3].after_near()
    down[2].after_z()
    mixes[0].after_far()
    outs.after_near()
    ups[0].after_z()
    down[0].after_near()
    mixes[1].after_far()
    mixes[0].after_near()
    ups[1].after_z()
    mixes[2].after_far()
    totals.after_far()
    mixes[1].after_near()
    ups[2].after_z()
    ups[3].after_z()
    outs.after_z()
    mixes[2].after_near()
    totals.after_near()
    for s in mixes:
        s.after_z()
    totals.after_z()
    wires.arrived(lo_out.at[rows_own], back)
    wires.arrived(ig_there, back + 1)
    wires.arrived(tg_out.at[p.y], back + 2)
    for copy in (lo_copy, ig_copy, tg_copy):
        copy.wait()
    wires.finish()


def results_kernel(mix, out, up, down, lo, ig, ig_there, tg, small, lo_out, ig_out, time_out, *rest):
    gain1, shift1, o_mix, mbias, o_out, obias, gain2, shift2, o_up, ubias, o_down, dbias, wide, sem = rest
    y = lax.axis_index(SEQ)
    pairs = [(mix, o_mix), (out, o_out), (up, o_up), (down, o_down), (lo, lo_out), (ig, ig_out.at[pl.ds(2 * y, 2)])]
    copies = [pltpu.make_async_copy(src, dst, sem.at[i]) for i, (src, dst) in enumerate(pairs)]
    wide[...] = ig_there[...].astype(F32)
    copies.append(pltpu.make_async_copy(wide, ig_out.at[pl.ds(2 - 2 * y, 2)], sem.at[len(pairs)]))
    for copy in copies:
        copy.start()
    time_out[...] = jnp.concatenate([tg[0, 0:2], tg[1, 0:2]], 0)
    first = 0
    for ref in (gain1, shift1, obias, gain2, shift2, dbias, mbias, ubias):
        count = ref.shape[0] // PIECE
        ref[...] = jnp.concatenate([small[first + i:first + i + 1, :PIECE] for i in range(count)], 1)[0]
        first += count
    for copy in copies:
        copy.wait()


def in_one_kernel(inputs, time_embed, segment_ids, cotangent, gain1, shift1, mix, mbias, out, obias, gain2, shift2, up, ubias,
                  down, dbias):
    pieces = jnp.concatenate([v.reshape(-1, PIECE) for v in (gain1, shift1, obias, gain2, shift2, dbias, mbias, ubias)])
    raw = jnp.pad(pieces, ((0, 16 - pieces.shape[0]), (0, 128 - PIECE)))
    table = scratch_table(SLOTS)
    anywhere, vmem = pl.BlockSpec(memory_space=pl.ANY), pl.BlockSpec(memory_space=pltpu.VMEM)
    shape = jax.ShapeDtypeStruct
    tokens = inputs.shape
    here = (tokens[0] // 2,) + tokens[1:]
    g_mix, g_out, g_up, g_down, small, lo, ig, ig_there, tg = pl.pallas_call(
        partial(layer_kernel, [name for name, _, _ in table]),
        out_shape=[shape(w.shape, F32) for w in (mix, out, up, down)]
        + [shape((16, 128), F32), shape(tokens, BF16), shape(here, F32), shape(here, BF16), shape((2, 8, PART), F32)],
        in_specs=[vmem] * 7 + [anywhere] * 2,
        out_specs=[vmem] * 5 + [anywhere] * 4,
        scratch_shapes=[pltpu.SemaphoreType.DMA(shape) if kind is None else pltpu.VMEM(shape, kind) for _, shape, kind in table],
        compiler_params=pltpu.CompilerParams(collective_id=0, has_side_effects=True, vmem_limit_bytes=60 * 2**20),
    )(mix, out, up, down, raw, time_embed, segment_ids, inputs, cotangent)
    params = (gain1, shift1, mix, mbias, out, obias, gain2, shift2, up, ubias, down, dbias)
    return tuple(pl.pallas_call(
        results_kernel,
        out_shape=[shape(tokens, BF16), shape(tokens, F32), shape((tokens[0], PART), F32)] + [shape(w.shape, F32) for w in params],
        in_specs=[vmem] * 9,
        out_specs=[anywhere] * 2 + [vmem] + [anywhere if w.ndim == 2 else vmem for w in params],
        scratch_shapes=[pltpu.VMEM(here, F32), pltpu.SemaphoreType.DMA((7,))],
    )(g_mix, g_out, g_up, g_down, lo, ig, ig_there, tg, small))


def solution(mesh):
    fits = mesh.shape[BATCH] == 16 and mesh.shape[SEQ] == 2
    tokens, rows, vector, matrix = P(BATCH, SEQ, None), P(BATCH, None), P(AXES), P(AXES, None)
    params = (vector, vector, matrix, vector, matrix, vector, vector, vector, matrix, vector, matrix, vector)
    return jax.shard_map(
        in_one_kernel if fits else any_mesh,
        mesh=mesh,
        in_specs=(tokens, rows, rows, tokens) + params,
        out_specs=(tokens, tokens, P(BATCH, SEQ)) + params,
        check_vma=False,
    )
```

```python
from functools import partial
import math
from types import SimpleNamespace

import jax
import jax.numpy as jnp
from jax import lax
from jax.experimental import pallas as pl
from jax.experimental.pallas import tpu as pltpu
from jax.sharding import PartitionSpec as P

HEAD_DIM = 64
EPSILON = 1e-05
NEG_FILL = -1e30
BATCH, SEQ = "batch", "seq"
AXES = (BATCH, SEQ)
F32, BF16 = jnp.float32, jnp.bfloat16


def norm_back(d_out, normal, inv, gain):
    g = d_out * gain
    return inv * (g - jnp.mean(g, -1, keepdims=True) - normal * jnp.mean(g * normal, -1, keepdims=True))


def normal_part(hidden):
    centred = hidden - jnp.mean(hidden, -1, keepdims=True)
    inv = lax.rsqrt(jnp.mean(centred * centred, -1, keepdims=True) + EPSILON)
    return centred * inv, inv


def contract(a, b, over_a, over_b, batch=((), ())):
    return lax.dot_general(a, b, ((over_a, over_b), batch), preferred_element_type=F32)


def layer(inputs, time, ids, cot, params):
    (gain1, shift1, mix, mbias, out, obias, gain2, shift2, up, ubias, down, dbias) = params
    gain1, shift1, mbias, obias, gain2, shift2, ubias, dbias = (
        v.astype(F32) for v in (gain1, shift1, mbias, obias, gain2, shift2, ubias, dbias))
    rows, length, width = inputs.shape
    heads = width // HEAD_DIM
    scale = 1.0 / math.sqrt(HEAD_DIM)
    flat = lambda t: t.reshape(rows * length, -1)
    by_head = lambda t: t.reshape(rows, length, heads, HEAD_DIM).transpose(0, 2, 1, 3).reshape(rows * heads, length, HEAD_DIM)
    unhead = lambda t: flat(t.reshape(rows, heads, length, HEAD_DIM).transpose(0, 2, 1, 3))
    each = ((0,), (0,))
    cot = flat(cot)
    res_in = flat(inputs.astype(F32) + time.astype(F32)[:, None, :])
    norm1, inv1 = normal_part(res_in)
    normed1 = (norm1 * gain1 + shift1).astype(BF16)
    proj = contract(normed1, mix, (1,), (0,))
    q = by_head((proj[:, :width] + mbias[:width]).astype(BF16))
    k = by_head(proj[:, width:2 * width].astype(BF16))
    v = by_head((proj[:, 2 * width:] + mbias[width:]).astype(BF16))
    scores = contract(q, k, (2,), (2,), each) * scale
    same = jnp.repeat(ids[:, :, None] == ids[:, None, :], heads, axis=0)
    masked = jnp.where(same, scores, NEG_FILL)
    top = jnp.max(masked, -1, keepdims=True)
    log_total = top + jnp.log(jnp.sum(jnp.exp(masked - top), -1, keepdims=True))
    probs = jnp.exp(masked - log_total)
    probs16 = probs.astype(BF16)
    att = unhead(contract(probs16, v, (2,), (1,), each).astype(BF16))
    res_mid = res_in + (contract(att, out, (1,), (0,)) + obias)
    norm2, inv2 = normal_part(res_mid)
    normed2 = (norm2 * gain2 + shift2).astype(BF16)
    hid = contract(normed2, up, (1,), (0,)) + ubias
    cdf = 0.5 * (1.0 + lax.erf(hid * math.sqrt(0.5)))
    act = (hid * cdf).astype(BF16)
    layer_out = (res_mid + contract(act, down, (1,), (0,)) + dbias).astype(BF16)

    cot32 = cot.astype(F32)
    slope = cdf + hid * jnp.exp(-0.5 * hid * hid) * (1.0 / math.sqrt(2 * math.pi))
    d_hid = (contract(cot, down, (1,), (1,)) * slope).astype(BF16)
    d_n2 = contract(d_hid, up, (1,), (1,))
    d_mid = cot32 + norm_back(d_n2, norm2, inv2, gain2)
    d_br = d_mid.astype(BF16)
    d_att = by_head(contract(d_br, out, (1,), (1,)).astype(BF16))
    d_pr = contract(d_att, v, (2,), (2,), each)
    d_sc = (probs * (d_pr - jnp.sum(probs * d_pr, -1, keepdims=True))).astype(BF16)
    d_q = unhead((contract(d_sc, k, (2,), (1,), each) * scale).astype(BF16))
    d_k = unhead((contract(d_sc, q, (1,), (1,), each) * scale).astype(BF16))
    d_v = unhead(contract(probs16, d_att, (1,), (1,), each).astype(BF16))
    d_proj = jnp.concatenate([d_q, d_k, d_v], -1)
    d_n1 = contract(d_proj, mix, (1,), (1,))
    x_grad = d_mid + norm_back(d_n1, norm1, inv1, gain1)

    def col(t):
        return jnp.sum(t.astype(F32), axis=0)

    weigh = lambda a, b: contract(a, b, (0,), (0,))
    grads = (col(d_n1 * norm1), col(d_n1), weigh(normed1, d_proj), jnp.concatenate([col(d_q), col(d_v)]),
             weigh(att, d_br), col(d_br), col(d_n2 * norm2), col(d_n2), weigh(normed2, d_hid), col(d_hid),
             weigh(act, cot), col(cot32))
    return layer_out.reshape(inputs.shape), x_grad.reshape(inputs.shape), grads


def gather_all(shard):
    return lax.all_gather(shard, AXES, axis=0, tiled=True)


def scatter_sum(grad):
    return lax.psum_scatter(grad, AXES, scatter_dimension=0, tiled=True)


def rows_whole(tensor):
    return lax.all_to_all(tensor, SEQ, split_axis=0, concat_axis=1, tiled=True)


def rows_split(tensor):
    return lax.all_to_all(tensor, SEQ, split_axis=1, concat_axis=0, tiled=True)


def any_mesh(inputs, time_embed, segment_ids, cotangent, *shards):
    y, count = lax.axis_index(SEQ), inputs.shape[0] // lax.axis_size(SEQ)
    mine = [lax.dynamic_slice_in_dim(t, y * count, count, 0) for t in (time_embed, segment_ids)]
    layer_out, x_grad, grads = layer(
        rows_whole(inputs), mine[0], mine[1], rows_whole(cotangent), [gather_all(w) for w in shards])
    time_grad = lax.all_to_all(jnp.sum(x_grad, 1), SEQ, split_axis=1, concat_axis=0, tiled=True)
    return (rows_split(layer_out), rows_split(x_grad), time_grad) + tuple(scatter_sum(g) for g in grads)


MESH = pl.DeviceIdType.MESH
Z_CHIPS = 4
TOKENS, WIDTH, HIDDEN, PART = 256, 768, 3072, 384
SMALL = (16, WIDTH)
PIECE = 24
TRANSPOSED = ((1,), (1,))
TOKEN_SUM = ((0,), (0,))


class Place:
    def __init__(self):
        b, self.y = lax.axis_index(BATCH), lax.axis_index(SEQ)
        self.z, self.x, self.c = b // 4, (b // 2) % 2, b % 2
        z, x, c, y = self.z, self.x, self.c, self.y
        self.twin = self.at(z, x, 1 - c, y)
        self.x_peer = self.at(z, 1 - x, c, y)
        self.y_peer = self.at(z, x, c, 1 - y)
        self.z_slots = [lax.rem(z + d, Z_CHIPS) for d in (1, 2, 3)]
        self.z_peers = [self.at(q, x, c, y) for q in self.z_slots]

    @staticmethod
    def at(z, x, c, y):
        return ((z * 2 + x) * 2 + c, y)

    def routes(self, turn):
        c = 1 if turn else self.c
        x, y = self.x, self.y
        return (x + (1 - 2 * x) * (1 - c), y + (1 - 2 * y) * c), (x + (1 - 2 * x) * c, y + (1 - 2 * y) * (1 - c))

    def on_chip(self, chip):
        return self.at(self.z, chip[0], self.c, chip[1])

    def role(self, c, x, y):
        dx, dy = (x + self.x) % 2, (y + self.y) % 2
        return (dx + 2 * dy) * (1 - c) + (dy + 2 * dx) * c

    def of_role(self, c, role):
        low, high = role % 2, role // 2
        dx, dy = low * (1 - c) + high * c, high * (1 - c) + low * c
        return (self.x + dx) % 2, (self.y + dy) % 2

    def greet(self):
        self.partners = self.z_peers + [self.x_peer, self.y_peer, self.twin]
        for partner in self.partners:
            pl.semaphore_signal(pltpu.get_barrier_semaphore(), inc=1, device_id=partner, device_id_type=MESH)

    def all_here(self):
        pl.semaphore_wait(pltpu.get_barrier_semaphore(), len(self.partners))


class Wires:
    def __init__(self, send_sem, recv_sem, place):
        self.send_sem, self.recv_sem, self.place = send_sem, recv_sem, place
        self.sent, self.used = [], 0

    def slots(self, count):
        self.used += count
        return self.used - count

    def start(self, src, dst, slot, device):
        copy = pltpu.make_async_remote_copy(
            src_ref=src, dst_ref=dst, send_sem=self.send_sem.at[slot], recv_sem=self.recv_sem.at[slot],
            device_id=device, device_id_type=MESH,
        )
        copy.start()
        self.sent.append(copy)
        return copy

    def arrived(self, dst, slot):
        pltpu.make_async_remote_copy(
            src_ref=dst, dst_ref=dst, send_sem=self.send_sem.at[slot], recv_sem=self.recv_sem.at[slot],
            device_id=self.place.twin, device_id_type=MESH,
        ).wait_recv()

    def left(self, copies):
        for copy in copies:
            copy.wait_send()
        self.sent = [kept for kept in self.sent if all(kept is not copy for copy in copies)]

    def finish(self):
        for copy in self.sent:
            copy.wait_send()
        self.sent = []


class Gather:
    def __init__(self, wires, place, own, buf, at, wide, turn=False):
        self.w, self.p, self.own, self.buf, self.cols = wires, place, own, buf, pl.ds(at, wide)
        self.base, self.copies = wires.slots(10), []
        self.near, self.far = place.routes(turn)

    def send(self, src, dst, slot, device):
        self.copies.append(self.w.start(src, dst, self.base + slot, device))

    def mine(self):
        p = self.p
        return self.buf.at[p.z, p.x, p.c, p.y, :, self.cols]

    def block(self, x, y, c):
        return self.buf.at[:, x, c, y, :, self.cols]

    def begin(self):
        for j, peer in enumerate(self.p.z_peers):
            self.send(self.own.at[:, self.cols], self.mine(), j, peer)

    def after_z(self):
        p = self.p
        for j in range(3):
            self.w.arrived(self.mine(), self.base + j)
        b = self.block(p.x, p.y, p.c)
        self.send(b, b, 3, p.on_chip(self.near))
        self.send(b, b, 4, p.on_chip(self.far))
        self.send(b, b, 6, p.twin)

    def after_near(self):
        p = self.p
        b = self.block(*self.near, p.c)
        self.w.arrived(b, self.base + 3)
        self.send(b, b, 5, p.on_chip(self.far))
        self.send(b, b, 7, p.twin)

    def after_far(self):
        p = self.p
        b = self.block(*self.far, p.c)
        self.w.arrived(b, self.base + 4)
        self.send(b, b, 8, p.twin)
        b = self.block(1 - p.x, 1 - p.y, p.c)
        self.w.arrived(b, self.base + 5)
        self.send(b, b, 9, p.twin)
        for j in range(6, 10):
            self.w.arrived(self.block(p.x, p.y, 1 - p.c), self.base + j)

    def halves_in_place(self):
        self.w.left(self.copies)
        rows = self.buf.shape[-2] // 2

        @pl.loop(0, 16)
        def _(pair):
            z, x, c = pair // 4, (pair // 2) % 2, pair % 2
            v = [self.buf[z, x, c, y, :, self.cols].astype(F32) for y in (0, 1)]
            for h in (0, 1):
                part = slice(h * rows, h * rows + rows)
                self.buf[z, x, c, h, :, self.cols] = jnp.concatenate([v[0][part], v[1][part]], 0).astype(BF16)


class LayerFirst(Gather):
    def begin(self):
        for j, chip in enumerate((self.near, self.far)):
            self.send(self.own.at[:, self.cols], self.mine(), j, self.p.on_chip(chip))

    def shard(self, chip):
        return self.buf.at[self.p.z, chip[0], self.p.c, chip[1], :, self.cols]

    def layer(self, z, c):
        return self.buf.at[z, :, c, :, :, self.cols]

    def forward(self):
        b = self.shard(self.near)
        self.w.arrived(b, self.base)
        self.send(b, b, 2, self.p.on_chip(self.far))

    def along_z(self):
        p = self.p
        self.w.arrived(self.shard(self.far), self.base + 1)
        self.w.arrived(self.shard((1 - p.x, 1 - p.y)), self.base + 2)
        b = self.layer(p.z, p.c)
        for j, peer in enumerate(p.z_peers):
            self.send(b, b, 3 + j, peer)
        self.send(b, b, 6, p.twin)

    def after_z(self):
        p = self.p
        for j in range(3):
            b = self.layer(lax.rem(p.z + 3 - j, Z_CHIPS), p.c)
            self.w.arrived(b, self.base + 3 + j)
            self.send(b, b, 7 + j, p.twin)
        for j in range(6, 10):
            self.w.arrived(self.layer(p.z, 1 - p.c), self.base + j)


class Scatter:
    def __init__(self, wires, place, rows, cols, keep, s1, r1, s2, r2, sz, rz, out, out_cols, turn=False):
        self.w, self.p, self.rows, self.cols, self.out_cols = wires, place, rows, cols, out_cols
        self.keep, self.s1, self.r1, self.s2, self.r2, self.sz, self.rz, self.out = keep, s1, r1, s2, r2, sz, rz, out
        self.base, self.quarter, self.packed = wires.slots(5), Z_CHIPS * rows, rows % 16 != 0
        wide = cols.size // 2 if self.packed else cols.size
        self.z_cols = pl.ds(cols.start // 2 if self.packed else cols.start, wide)
        near, far = place.routes(turn)
        self.near, self.far = place.on_chip(near), place.on_chip(far)
        swapped = (1 - place.c) if turn else 0
        self.roles = (0, 1 + swapped, 2 - swapped, 3)

    def begin(self, left, right):
        q = self.quarter
        for i, role in enumerate(self.roles):
            total = contract(left(0, role), right[0], (1,), (0,)) + contract(left(1, role), right[1], (1,), (0,))
            at = pl.ds((i % 2) * q, q)
            if i < 2:
                self.keep[at, self.cols] = total
            else:
                self.s1[at, self.cols] = total.astype(BF16)
    def launch(self):
        both = pl.ds(0, 2 * self.quarter)
        self.w.start(self.s1.at[both, self.cols], self.r1.at[both, self.cols], self.base, self.far)

    def after_far(self):
        q = self.quarter
        self.w.arrived(self.r1.at[pl.ds(0, 2 * q), self.cols], self.base)
        at = pl.ds(q, q)
        self.s2[:, self.cols] = (self.keep[at, self.cols] + self.r1[at, self.cols].astype(F32)).astype(BF16)
        self.w.start(self.s2.at[:, self.cols], self.r2.at[:, self.cols], self.base + 1, self.near)

    def after_near(self):
        q, n = self.quarter, self.rows
        self.w.arrived(self.r2.at[:, self.cols], self.base + 1)
        at = pl.ds(0, q)
        total = self.keep[at, self.cols] + self.r1[at, self.cols].astype(F32) + self.r2[:, self.cols].astype(F32)
        for z in range(Z_CHIPS):
            piece = total[z * n:z * n + n]

            @pl.when(z == self.p.z)
            def _():
                self.out[:, self.out_cols] = piece

            if self.packed:
                half = self.z_cols.size
                piece = jnp.concatenate([piece[:, :half], piece[:, half:]], 0)
            self.sz[z, :, self.z_cols] = piece.astype(BF16)
        for j, (z, peer) in enumerate(zip(self.p.z_slots, self.p.z_peers)):
            self.w.start(self.sz.at[z, :, self.z_cols], self.rz.at[j, :, self.z_cols], self.base + 2 + j, peer)

    def after_z(self):
        total = 0.0
        for j in range(3):
            self.w.arrived(self.rz.at[j, :, self.z_cols], self.base + 2 + j)
            total = total + self.rz[j, :, self.z_cols].astype(F32)
        if self.packed:
            total = jnp.concatenate([total[:self.rows], total[self.rows:]], 1)
        self.out[:, self.out_cols] = self.out[:, self.out_cols] + total


class AlongZFirst(Scatter):
    def __init__(self, *args, zs, zr):
        super().__init__(*args)
        self.zs, self.zr = zs, zr

    def begin(self, left, right):
        n = self.rows
        for role in range(4):
            total = contract(left(0, role), right[0], (1,), (0,)) + contract(left(1, role), right[1], (1,), (0,))
            for z in range(Z_CHIPS):
                piece = total[z * n:z * n + n]
                self.zs[z, role] = piece.astype(BF16)

                @pl.when(z == self.p.z)
                def _():
                    self.keep[pl.ds(role * n, n), self.cols] = piece

        for j, (z, peer) in enumerate(zip(self.p.z_slots, self.p.z_peers)):
            self.w.start(self.zs.at[z], self.zr.at[j], self.base + 2 + j, peer)

    def after_z(self):
        n = self.rows
        for j in range(3):
            self.w.arrived(self.zr.at[j], self.base + 2 + j)
        for role in range(4):
            at = pl.ds(role * n, n)
            total = self.keep[at, self.cols]
            for j in range(3):
                total = total + self.zr[j, role].astype(F32)
            if role < 2:
                self.keep[at, self.cols] = total
            else:
                self.s1[pl.ds((role - 2) * n, n), self.cols] = total.astype(BF16)
        both = pl.ds(0, 2 * n)
        self.w.start(self.s1.at[both, self.cols], self.r1.at[both, self.cols], self.base, self.far)

    def after_far(self):
        n = self.rows
        self.w.arrived(self.r1.at[pl.ds(0, 2 * n), self.cols], self.base)
        at, first = pl.ds(n, n), pl.ds(0, n)
        self.s2[first, self.cols] = (self.keep[at, self.cols] + self.r1[at, self.cols].astype(F32)).astype(BF16)
        self.w.start(self.s2.at[first, self.cols], self.r2.at[first, self.cols], self.base + 1, self.near)

    def after_near(self):
        at = pl.ds(0, self.rows)
        self.w.arrived(self.r2.at[at, self.cols], self.base + 1)
        self.out[:, self.out_cols] = (
            self.keep[at, self.cols] + self.r1[at, self.cols].astype(F32) + self.r2[at, self.cols].astype(F32))


class SmallScatter:
    def __init__(self, wires, place, slabs, from_twin, s1, r1, s2, r2, sz, rz, out):
        self.w, self.p, self.slabs, self.from_twin = wires, place, slabs, from_twin
        self.s1, self.r1, self.s2, self.r2, self.sz, self.rz, self.out = s1, r1, s2, r2, sz, rz, out
        self.base = wires.slots(6)
        near, far = place.routes(False)
        self.chips = ((place.x, place.y), near, far, (1 - place.x, 1 - place.y))
        self.near, self.far = place.on_chip(near), place.on_chip(far)

    def summed(self, role):
        x, y = self.chips[role]
        return self.slabs[:, x, self.p.c, y] + self.from_twin[:, x, y]

    def to_twin(self):
        self.w.start(self.slabs.at[:, :, 1 - self.p.c], self.from_twin, self.base, self.p.twin)

    def begin(self):
        self.w.arrived(self.from_twin, self.base)
        self.s1[0], self.s1[1] = self.summed(2), self.summed(3)
        self.w.start(self.s1, self.r1, self.base + 1, self.far)

    def after_far(self):
        self.w.arrived(self.r1, self.base + 1)
        self.s2[...] = self.summed(1) + self.r1[1]
        self.w.start(self.s2, self.r2, self.base + 2, self.near)

    def after_near(self):
        self.w.arrived(self.r2, self.base + 2)
        self.sz[...] = self.summed(0) + self.r1[0] + self.r2[...]
        for j, (z, peer) in enumerate(zip(self.p.z_slots, self.p.z_peers)):
            self.w.start(self.sz.at[z], self.rz.at[j], self.base + 3 + j, peer)

    def after_z(self):
        total = self.sz[self.p.z]
        for j in range(3):
            self.w.arrived(self.rz.at[j], self.base + 3 + j)
            total = total + self.rz[j]
        self.out[...] = total


def merged(value):
    return value.reshape(-1, value.shape[-1])


def by_rows(step, body, *carry):
    return lax.fori_loop(0, TOKENS // step, lambda i, kept: body(i, pl.ds(pl.multiple_of(i * step, step), step), *kept), carry)


def folded(value):
    return jnp.sum(value.reshape(value.shape[0] // 8, 8, value.shape[1]), 0)


def column_sums(value):
    return contract(jnp.ones((8, value.shape[0]), BF16), value, (1,), (0,))[0:1]


def token_block(i):
    return i // 4, (i // 2) % 2, pl.ds(pl.multiple_of((i % 2) * 32, 32), 32)


def scratch_table(slots):
    k, w = WIDTH // 2, WIDTH
    return [
        ("par", SMALL, F32), ("sums", SMALL, F32), ("small", (16, 128), BF16), ("bs", (4, 2, 2, 2, 16, 128), BF16),
        ("slabs", (4, 2, 2, 2, 16, 128), F32), ("from_twin", (4, 2, 2, 16, 128), F32), ("s1_s", (2, 4, 16, 128), F32),
        ("r1_s", (2, 4, 16, 128), F32), ("s2_s", (4, 16, 128), F32), ("r2_s", (4, 16, 128), F32),
        ("sz_s", (4, 16, 128), F32), ("rz_s", (3, 16, 128), F32),
        ("w1", (48, 1536), BF16), ("w2", (48, 1536), BF16), ("same", (2, 128, 128), F32), ("time", (2, 1, w), F32),
        ("b1", (4, 2, 2, 2, 48, 1536), BF16), ("b2", (4, 2, 2, 2, 48, 1536), BF16), ("b3", (4, 2, 2, 2, 96, w), BF16),
        ("x0", (2, 2, 64, w), BF16), ("cot", (2, 2, 2, 64, w), BF16),
        ("res_in", (TOKENS, w), F32), ("normed1", (TOKENS, w), BF16), ("qkv", (TOKENS, 3 * w), BF16),
        ("probs", (12, TOKENS, 128), F32), ("att", (TOKENS, w), BF16), ("res_mid", (TOKENS, w), F32),
        ("normed2", (TOKENS, w), BF16), ("slope", (TOKENS, HIDDEN), F32), ("act", (TOKENS, HIDDEN), BF16),
        ("pick", (2, k, w), BF16), ("pick_act", (2, 192, PART), BF16),
        ("t1", (2, k, TOKENS), BF16), ("t1_send", (k, TOKENS), BF16),
        ("to", (2, k, TOKENS), BF16), ("to_send", (k, TOKENS), BF16),
        ("t2", (2, k, TOKENS), BF16), ("t2_send", (k, TOKENS), BF16),
        ("ta", (2, 4, 4, 96, TOKENS), BF16), ("ta_send", (4, 4, 96, TOKENS), BF16),
        ("d_hid", (2, TOKENS, HIDDEN), BF16), ("d_norm", (TOKENS, w), F32),
        ("d_branch", (2, TOKENS, w), BF16), ("d_proj", (2, TOKENS, 3 * w), BF16),
        ("ig", (2, 2, 64, w), F32), ("tg", (2, 8, PART), F32),
        ("keep_d", (768, w), F32), ("s1_d", (768, w), BF16), ("r1_d", (768, w), BF16), ("s2_d", (PART, w), BF16),
        ("r2_d", (PART, w), BF16), ("sz_d", (4, 96, w), BF16), ("rz_d", (3, 96, w), BF16),
        ("zr_d", (3, 4, 96, 256), BF16), ("ig_send", (2, 64, w), BF16),
        ("keep_u", (192, HIDDEN), F32), ("s1_u", (192, HIDDEN), BF16), ("r1_u", (192, HIDDEN), BF16),
        ("s2_u", (96, HIDDEN), BF16), ("r2_u", (96, HIDDEN), BF16), ("sz_u", (4, 48, 1536), BF16), ("rz_u", (3, 48, 1536), BF16),
        ("r1_m", (192, HIDDEN), BF16),
        ("s2_m", (96, HIDDEN), BF16), ("r2_m", (96, HIDDEN), BF16), ("sz_m", (4, 48, 1536), BF16), ("rz_m", (3, 48, 1536), BF16),
        ("send_sem", (slots,), None), ("recv_sem", (slots,), None), ("local_sem", (10,), None),
    ]


SLOTS = 240
AHEAD = 4
TURNED = ()
UPS_TURNED, MIX_TURNED = (), (1, 3)


def iota(shape, dim):
    return lax.broadcasted_iota(jnp.int32, shape, dim)


def piece_place(row, device):
    block = jnp.where(row < 6, device, jnp.where(row < 8, 2 * device + row - 6, 4 * device + row - 8))
    first = jnp.where(row < 6, row, jnp.where(row < 8, 6, 8))
    return jnp.where(row < 12, first + (block >> 5), -1), block & 31


def ones_where(condition):
    return condition.astype(F32).astype(BF16)


def lane_piece(shape):
    return (iota(shape, 1) * 2731) >> 16


def every_piece():
    shape = (128, WIDTH)
    return ones_where(iota(shape, 1) - PIECE * lane_piece(shape) == iota(shape, 0))


def slab_rows(first, count):
    n = iota((SMALL[0], count), 1) + first
    return ones_where(piece_place(n & 15, n >> 4)[0] == iota((SMALL[0], count), 0))


def slab_places(first, count):
    n = iota((count, WIDTH), 0) + first
    return (piece_place(n & 15, n >> 4)[1] == lane_piece((count, WIDTH))).astype(F32)


def whole_of(ref):
    total = 0.0
    for z in range(Z_CHIPS):
        wide = contract(merged(ref[z]), every_piece(), (1,), (0,)) * slab_places(128 * z, 128)
        total = total + contract(slab_rows(128 * z, 128), wide.astype(BF16), (1,), (0,))
    return total


def put_slabs(ref, whole):
    high = whole.astype(BF16)
    parts = (high, (whole - high.astype(F32)).astype(BF16))
    for z in range(Z_CHIPS):
        places, total = slab_places(128 * z, 128), 0.0
        for part in parts:
            wide = contract(slab_rows(128 * z, 128), part, *TOKEN_SUM) * places
            total = total + contract(wide.astype(BF16), every_piece(), *TRANSPOSED)
        ref[z] = total.reshape(ref.shape[1:])


def layer_kernel(names, mix, out, up, w3, gain1, shift1, obias, gain2, shift2, dbias, mbias, ubias, time, ids, xin, cin,
                 o_mix, o_out, o_up, o_down, o_small, lo_out, ig_out, ig_there, tg_out, *scratch):
    m = SimpleNamespace(**dict(zip(names, scratch)))
    p = Place()
    p.greet()
    wires = Wires(m.send_sem, m.recv_sem, p)
    me, twin = p.c, 1 - p.c
    scale = 1.0 / math.sqrt(HEAD_DIM)

    own, bufs = (m.w1, m.w2, w3), (m.b1, m.b2, m.b3)
    for ref, target, at in ((mix, m.w1, 0), (out, m.w1, 3 * PART), (up, m.w2, 0)):
        half = ref.shape[1] // 2
        value = ref[...].astype(F32)
        target[:, at:at + half] = jnp.concatenate([value[:, :half], value[:, half:]], 0).astype(BF16)
    pieces = []
    for ref in (gain1, shift1, obias, gain2, shift2, dbias, mbias, ubias):
        value = ref[...].astype(F32).reshape(1, ref.shape[0])
        pieces += [value[:, at:at + PIECE] for at in range(0, ref.shape[0], PIECE)]
    pieces.append(jnp.zeros((16 - len(pieces), PIECE), F32))
    m.small[...] = jnp.concatenate([jnp.concatenate(pieces, 0), jnp.zeros((16, 128 - PIECE), F32)], 1).astype(BF16)
    p.all_here()
    plan = [(0, PART * i, PART) for i in range(4)] + [(1, PART * i, PART) for i in range(4)] + [(2, 256 * i, 256) for i in range(3)]
    gathers = [Gather(wires, p, own[w], bufs[w], at, wide, k in TURNED) for k, (w, at, wide) in enumerate(plan[:-1])]
    last = LayerFirst(wires, p, own[2], bufs[2], *plan[-1][1:])
    params = Gather(wires, p, m.small, m.bs, 0, 128)
    params.begin()
    for g in gathers[:AHEAD]:
        g.begin()
    locs = [pltpu.make_async_copy(own[i], bufs[i].at[p.z, p.x, p.c, p.y], m.local_sem.at[i]) for i in range(3)]
    rows_own, rows_other = pl.ds(2 * p.y, 2), pl.ds(2 - 2 * p.y, 2)
    locs.append(pltpu.make_async_copy(xin.at[rows_own], m.x0.at[:, p.y], m.local_sem.at[3]))
    locs.append(pltpu.make_async_copy(cin.at[rows_own], m.cot.at[me, :, p.y], m.local_sem.at[4]))
    for copy in locs:
        copy.start()
    swap = wires.slots(3)
    small_copy = pltpu.make_async_copy(m.small, m.bs.at[p.z, p.x, p.c, p.y], m.local_sem.at[8])
    small_copy.start()
    wires.start(xin.at[rows_other], m.x0.at[:, p.y], swap, p.y_peer)
    last.begin()
    wires.start(cin.at[rows_other], m.cot.at[me, :, p.y], swap + 1, p.y_peer)

    def z_step(k):
        gathers[k].after_z()
        if k + AHEAD < len(gathers):
            gathers[k + AHEAD].begin()

    def near_step(k):
        gathers[k].after_near()

    def far_step(k):
        gathers[k].after_far()
        if plan[k][0] < 2:
            gathers[k].halves_in_place()

    lane, row = lax.broadcasted_iota(jnp.int32, (24, WIDTH), 1), lax.broadcasted_iota(jnp.int32, (24, WIDTH), 0)
    lane_a, row_a = lax.broadcasted_iota(jnp.int32, (192, PART), 1), lax.broadcasted_iota(jnp.int32, (192, PART), 0)
    for side, c in ((0, me), (1, twin)):
        pieces = []
        for role in range(4):
            x, y = p.of_role(c, role)
            for z in range(Z_CHIPS):
                first = (((z * 2 + x) * 2 + c) * 2 + y) * 24
                pieces.append((lane == row + first).astype(F32))
        m.pick[side] = jnp.concatenate(pieces, 0).astype(BF16)
        m.pick_act[side] = (lane_a == row_a + c * 192).astype(F32).astype(BF16)

    for r in (0, 1):
        m.time[r] = jnp.where(p.y == 0, time[r:r + 1, :].astype(F32), time[r + 2:r + 3, :].astype(F32))
        along = jnp.where(p.y == 0, ids[r:r + 1, :], ids[r + 2:r + 3, :])
        one_hot = (lax.broadcasted_iota(jnp.int32, (8, 128), 0) == along).astype(F32).astype(BF16)
        m.same[r] = contract(one_hot, one_hot, *TOKEN_SUM)

    twin_base = wires.slots(16)

    def transposed(value, ref, send, slot):
        ref[me] = contract(m.pick[0], value, *TRANSPOSED).astype(BF16)
        send[...] = contract(m.pick[1], value, *TRANSPOSED).astype(BF16)
        wires.start(send, ref.at[me], twin_base + slot, p.twin)

    def left_of(ref, quarter=96):
        return lambda core, role: ref[core, pl.ds(role * quarter, quarter), :]

    def left_act(core, role):
        return merged(m.ta[core, role])

    def normal(h):
        centred = h - jnp.mean(h, -1, keepdims=True)
        inv = lax.rsqrt(jnp.mean(centred * centred, -1, keepdims=True) + EPSILON)
        return centred * inv, inv

    def first_norm():
        m.par[...] = whole_of(m.bs)
        for copy in locs[3:]:
            copy.wait()
        wires.arrived(m.x0.at[:, p.y], swap)

        def body(i, at):
            r, half, pos = token_block(i)
            h = m.x0[r, half, pos, :].astype(F32) + m.time[r]
            m.res_in[at, :] = h
            m.normed1[at, :] = (normal(h)[0] * m.par[0:1, :] + m.par[1:2, :]).astype(BF16)
            return ()

        by_rows(32, body)
        transposed(m.normed1[...], m.t1, m.t1_send, 0)

    def projected(k):
        for h in (0, 1):
            weight = merged(m.b1[:, :, :, h, :, pl.ds(PART * k, PART)])
            group, lanes = (3 * h + k) // 2, PART * ((3 * h + k) % 2)
            total = contract(m.normed1[...], weight, (1,), (0,))
            if group != 1:
                total = total + m.par[6 + group // 2:7 + group // 2, lanes:lanes + PART]
            m.qkv[:, WIDTH * group + lanes:WIDTH * group + lanes + PART] = total.astype(BF16)

    low = (lax.broadcasted_iota(jnp.int32, (1, 128), 1) < HEAD_DIM).astype(F32)
    heads_of = [low.astype(BF16), (1.0 - low).astype(BF16)]

    def two_heads(value):
        return jnp.concatenate([value * h for h in heads_of], 0)

    def side_by_side(value):
        return jnp.concatenate([value[:128], value[128:]], 1)

    def at_pair(i):
        return pl.ds(pl.multiple_of((i // 6) * 128, 128), 128), [
            pl.ds(pl.multiple_of((i % 6) * 128 + WIDTH * part, 128), 128) for part in range(3)]

    def attention(first, last):
        def body(i, _):
            rows, (cq, ck, cv) = at_pair(i)
            q2, k, v = two_heads(m.qkv[rows, cq]), m.qkv[rows, ck], m.qkv[rows, cv]
            scores = contract(q2, k, *TRANSPOSED) * scale
            same = m.same[i // 6] > 0.5
            masked = jnp.where(jnp.concatenate([same, same], 0), scores, NEG_FILL)
            e = jnp.exp(masked - jnp.max(masked, -1, keepdims=True))
            probs = e / jnp.sum(e, -1, keepdims=True)
            m.probs[i] = probs
            m.att[rows, cq] = contract(side_by_side(probs.astype(BF16)), two_heads(v), (1,), (0,)).astype(BF16)
            return 0

        lax.fori_loop(first, last, body, 0)

    def out_half(h):
        return merged(m.b1[:, :, :, h, :, pl.ds(3 * PART, PART)])

    def branch():
        transposed(m.att[...], m.to, m.to_send, 1)
        for h in (0, 1):
            at = slice(PART * h, PART * h + PART)
            total = contract(m.att[...], out_half(h), (1,), (0,)) + m.par[2:3, at]
            m.res_mid[:, at] = m.res_in[:, at] + total

        def body(i, at):
            m.normed2[at, :] = (normal(m.res_mid[at, :])[0] * m.par[3:4, :] + m.par[4:5, :]).astype(BF16)
            return ()

        by_rows(32, body)
        transposed(m.normed2[...], m.t2, m.t2_send, 2)

    def up_part(k):
        for h in (0, 1):
            first = 1536 * h + PART * k
            cols, lanes = slice(first, first + PART), first % WIDTH
            weight = merged(m.b2[:, :, :, h, :, pl.ds(PART * k, PART)])
            bias = m.par[8 + first // WIDTH:9 + first // WIDTH, lanes:lanes + PART]
            m.slope[:, cols] = contract(m.normed2[...], weight, (1,), (0,)) + bias

            def body(i, at):
                v = m.slope[at, cols]
                cdf = 0.5 + 0.5 * lax.erf(v * math.sqrt(0.5))
                m.act[at, cols] = (v * cdf).astype(BF16)
                m.slope[at, cols] = cdf + v * jnp.exp(-0.5 * v * v) * (1.0 / math.sqrt(2 * math.pi))
                return ()

            by_rows(32, body)
            z, x = (first // PART) // 2, (first // PART) % 2
            act = m.act[:, cols]
            for side, c in ((0, me), (1, twin)):
                picked = contract(m.pick_act[side], act, *TRANSPOSED).astype(BF16)
                for y in (0, 1):
                    role = p.role(c, x, y)
                    piece = picked[96 * y:96 * y + 96]
                    if side == 0:
                        m.ta[me, role, z] = piece
                    else:
                        m.ta_send[role, z] = piece

    def cot_whole():
        wires.arrived(m.cot.at[me, :, p.y], swap + 1)
        wires.start(m.cot.at[me], m.cot.at[me], twin_base + 3, p.twin)

    twin_act = []

    def act_out():
        twin_act.append(wires.start(m.ta_send, m.ta.at[me], twin_base + 4, p.twin))

    def scatter_of(kind, first, wide, out, out_first, turn=False):
        cols, out_cols = pl.ds(first, wide), pl.ds(out_first, wide)
        if kind == 0:
            args = wires, p, 96, cols, m.keep_d, m.s1_d, m.r1_d, m.s2_d, m.r2_d, m.sz_d, m.rz_d, out, out_cols
            return Scatter(*args) if first else AlongZFirst(*args, zs=m.ta_send, zr=m.zr_d)
        if kind == 1:
            return Scatter(wires, p, 24, cols, m.keep_u, m.s1_u, m.r1_u, m.s2_u, m.r2_u, m.sz_u, m.rz_u, out, out_cols, turn)
        return Scatter(wires, p, 24, cols, m.slope, m.act, m.r1_m, m.s2_m, m.r2_m, m.sz_m, m.rz_m, out, out_cols, turn)

    down = [scatter_of(0, 256 * i, 256, o_down, 256 * i) for i in range(3)]
    ups = [scatter_of(1, WIDTH * i, WIDTH, o_up, WIDTH * i, i in UPS_TURNED) for i in range(4)]
    mix_plan = [(0, WIDTH), (WIDTH, WIDTH), (2 * WIDTH, 512), (2 * WIDTH + 512, 256)]
    mixes = [scatter_of(2, at, wide, o_mix, at, i in MIX_TURNED) for i, (at, wide) in enumerate(mix_plan)]
    outs = scatter_of(2, 3 * WIDTH, WIDTH, o_out, 0)

    def down_grad(i):
        if i == 0:
            wires.arrived(m.cot.at[twin], twin_base + 3)
            wires.arrived(m.ta.at[twin], twin_base + 4)
            wires.left(twin_act)
            m.sums[...] = jnp.zeros(SMALL, F32)
            m.sums[5:6, :] = column_sums(merged(m.cot[me]))
        cols = pl.ds(256 * i, 256)
        down[i].begin(left_act, [merged(m.cot[core, :, :, :, cols]) for core in (0, 1)])

    def hidden_grad(i):
        cot = merged(m.cot[me])
        for part in (2 * i, 2 * i + 1):
            cols = slice(PART * part, PART * part + PART)
            d_act = contract(cot, merged(m.b3[part // 2, part % 2]), *TRANSPOSED)
            grad = (d_act * m.slope[:, cols]).astype(BF16)
            m.d_hid[me, :, cols] = grad
            lanes = PART * (part % 2)
            m.sums[8 + i:9 + i, lanes:lanes + PART] = column_sums(grad)
        at = m.d_hid.at[me, :, pl.ds(WIDTH * i, WIDTH)]
        wires.start(at, at, twin_base + 5 + i, p.twin)

    def up_grad(i):
        if i == 0:
            wires.arrived(m.t2.at[twin], twin_base + 2)
        cols = pl.ds(WIDTH * i, WIDTH)
        wires.arrived(m.d_hid.at[twin, :, cols], twin_base + 5 + i)
        ups[i].begin(left_of(m.t2), [m.d_hid[core, :, cols] for core in (0, 1)])

    def layer_result(*parts):
        for i in parts:
            cols = slice(256 * i, 256 * i + 256)
            total = contract(m.act[...], merged(m.b3[:, :, :, :, :, cols]), (1,), (0,)) + m.par[5:6, cols]
            total = (m.res_mid[:, cols] + total).astype(BF16)
            for r in (0, 1):
                for half in (0, 1):
                    first = r * 128 + half * 64
                    m.x0[r, half, :, cols] = total[first:first + 64]

    back = wires.slots(3)
    lo_copy = pltpu.make_async_copy(m.x0.at[:, p.y], lo_out.at[rows_own], m.local_sem.at[5])
    ig_copy = pltpu.make_async_copy(m.ig.at[:, p.y], ig_out, m.local_sem.at[6])
    tg_copy = pltpu.make_async_copy(m.tg.at[p.y], tg_out.at[p.y], m.local_sem.at[7])

    def result_out():
        lo_copy.start()
        wires.start(m.x0.at[:, 1 - p.y], lo_out.at[rows_own], back, p.y_peer)

    def second_norm_back():
        halves = [merged(m.b2[:, :, :, h]) for h in (0, 1)]
        m.d_norm[...] = contract(m.d_hid[me, :, 0:1536], halves[0], *TRANSPOSED)
        m.d_norm[...] += contract(m.d_hid[me, :, 1536:3072], halves[1], *TRANSPOSED)

        def body(i, at, gain_sum, shift_sum):
            r, half, pos = token_block(i)
            norm, inv = normal(m.res_mid[at, :])
            dn = m.d_norm[at, :]
            dn_norm = dn * norm
            g, gn = dn * m.par[3:4, :], dn_norm * m.par[3:4, :]
            back_in = inv * (g - jnp.mean(g, -1, keepdims=True) - norm * jnp.mean(gn, -1, keepdims=True))
            d_mid = m.cot[me, r, half, pos, :].astype(F32) + back_in
            m.res_mid[at, :] = d_mid
            m.d_branch[me, at, :] = d_mid.astype(BF16)
            return gain_sum + folded(dn_norm), shift_sum + folded(dn)

        zero = jnp.zeros((8, WIDTH), F32)
        gain_sum, shift_sum = by_rows(32, body, zero, zero)
        m.sums[3:4, :] = jnp.sum(gain_sum, 0, keepdims=True)
        m.sums[4:5, :] = jnp.sum(shift_sum, 0, keepdims=True)
        wires.start(m.d_branch.at[me], m.d_branch.at[me], twin_base + 9, p.twin)
        d_branch = m.d_branch[me]
        m.sums[2:3, :] = column_sums(d_branch)
        d_att = contract(d_branch[:, 0:PART], out_half(0), *TRANSPOSED) + contract(d_branch[:, PART:], out_half(1), *TRANSPOSED)
        m.normed2[...] = d_att.astype(BF16)

    def out_grad():
        wires.arrived(m.to.at[twin], twin_base + 1)
        wires.arrived(m.d_branch.at[twin], twin_base + 9)
        outs.begin(left_of(m.to), [m.d_branch[core] for core in (0, 1)])

    def attention_back(first, last):
        def body(i, _):
            rows, (cq, ck, cv) = at_pair(i)
            q2, k, v = two_heads(m.qkv[rows, cq]), m.qkv[rows, ck], m.qkv[rows, cv]
            da2 = two_heads(m.normed2[rows, cq])
            probs = m.probs[i]
            d_probs = contract(da2, v, *TRANSPOSED)
            delta = jnp.sum(probs * d_probs, -1, keepdims=True)
            d_scores = (probs * (d_probs - delta)).astype(BF16)
            m.d_proj[me, rows, cq] = (contract(side_by_side(d_scores), two_heads(k), (1,), (0,)) * scale).astype(BF16)
            m.d_proj[me, rows, ck] = (contract(d_scores, q2, *TOKEN_SUM) * scale).astype(BF16)
            m.d_proj[me, rows, cv] = contract(probs.astype(BF16), da2, *TOKEN_SUM).astype(BF16)
            return 0

        lax.fori_loop(first, last, body, 0)

    def proj_out():
        for i in range(3):
            at = m.d_proj.at[me, :, pl.ds(WIDTH * i, WIDTH)]
            wires.start(at, at, twin_base + 10 + i, p.twin)

    def mix_grad(i):
        if i == 0:
            wires.arrived(m.t1.at[twin], twin_base)
        at, wide = mix_plan[i]
        cols, whole = pl.ds(at, wide), pl.ds(at // WIDTH * WIDTH, WIDTH)
        if i < 3:
            if i != 1:
                m.sums[6 + i // 2:7 + i // 2, :] = column_sums(m.d_proj[me, :, whole])
            wires.arrived(m.d_proj.at[twin, :, whole], twin_base + 10 + i)
        mixes[i].begin(left_of(m.t1), [m.d_proj[core, :, cols] for core in (0, 1)])

    def first_norm_back():
        halves = [merged(m.b1[:, :, :, h, :, 0:3 * PART]) for h in (0, 1)]
        m.d_norm[...] = contract(m.d_proj[me, :, 0:3 * PART], halves[0], *TRANSPOSED)
        m.d_norm[...] += contract(m.d_proj[me, :, 3 * PART:], halves[1], *TRANSPOSED)

        def body(i, at, gain_sum, shift_sum, row_sum):
            r, half, pos = token_block(i)
            norm, inv = normal(m.res_in[at, :])
            dn = m.d_norm[at, :]
            dn_norm = dn * norm
            g, gn = dn * m.par[0:1, :], dn_norm * m.par[0:1, :]
            grad = m.res_mid[at, :] + inv * (g - jnp.mean(g, -1, keepdims=True) - norm * jnp.mean(gn, -1, keepdims=True))
            m.ig[r, half, pos, :] = grad
            sums = folded(grad)
            first = (r == 0).astype(F32)
            return (gain_sum + folded(dn_norm), shift_sum + folded(dn),
                    row_sum + jnp.concatenate([sums * first, sums * (1.0 - first)], 0))

        zero = jnp.zeros((8, WIDTH), F32)
        gain_sum, shift_sum, row_sum = by_rows(32, body, zero, zero, jnp.zeros((16, WIDTH), F32))
        m.sums[0:1, :] = jnp.sum(gain_sum, 0, keepdims=True)
        m.sums[1:2, :] = jnp.sum(shift_sum, 0, keepdims=True)
        for r in (0, 1):
            total = jnp.sum(row_sum[8 * r:8 * r + 8], 0, keepdims=True)
            for half in (0, 1):
                m.tg[half, r:r + 1, :] = total[:, PART * half:PART * half + PART]
        ig_copy.start()
        m.ig_send[...] = m.ig[:, 1 - p.y].astype(BF16)
        wires.start(m.ig_send, ig_there, back + 1, p.y_peer)
        tg_copy.start()
        wires.start(m.tg.at[1 - p.y], tg_out.at[p.y], back + 2, p.y_peer)

    totals = SmallScatter(wires, p, m.slabs, m.from_twin, m.s1_s, m.r1_s, m.s2_s, m.r2_s, m.sz_s, m.rz_s, o_small)

    def small_out():
        put_slabs(m.slabs, m.sums[...])
        totals.to_twin()

    small_copy.wait()
    for copy in locs[:3]:
        copy.wait()
    params.after_z()
    z_step(0)
    params.after_near()
    last.forward()
    z_step(1)
    near_step(0)
    params.after_far()
    z_step(2)
    near_step(1)
    first_norm()
    far_step(0)
    projected(0)
    z_step(3)
    near_step(2)
    far_step(1)
    projected(1)
    cot_whole()
    z_step(4)
    near_step(3)
    far_step(2)
    projected(2)
    attention(0, 4)
    z_step(5)
    near_step(4)
    attention(4, 8)
    far_step(3)
    attention(8, 12)
    z_step(6)
    last.along_z()
    near_step(5)
    branch()
    far_step(4)
    up_part(0)
    z_step(7)
    near_step(6)
    far_step(5)
    up_part(1)
    z_step(8)
    near_step(7)
    far_step(6)
    up_part(2)
    z_step(9)
    near_step(8)
    far_step(7)
    up_part(3)
    act_out()
    down_grad(0)
    near_step(9)
    down_grad(1)
    down[1].launch()
    down_grad(2)
    down[2].launch()
    far_step(8)
    down[1].after_far()
    layer_result(0)
    far_step(9)
    down[2].after_far()
    layer_result(1)
    last.after_z()
    hidden_grad(0)
    hidden_grad(1)
    up_grad(0)
    ups[0].launch()
    down[1].after_near()
    hidden_grad(2)
    up_grad(1)
    ups[1].launch()
    hidden_grad(3)
    up_grad(2)
    ups[2].launch()
    down[2].after_near()
    up_grad(3)
    layer_result(2)
    result_out()
    second_norm_back()
    ups[0].after_far()
    ups[3].launch()
    down[1].after_z()
    attention_back(0, 3)
    out_grad()
    ups[1].after_far()
    outs.launch()
    attention_back(3, 6)
    ups[0].after_near()
    down[2].after_z()
    attention_back(6, 9)
    down[0].after_z()
    ups[2].after_far()
    attention_back(9, 12)
    ups[1].after_near()
    proj_out()
    mix_grad(0)
    mixes[0].launch()
    mix_grad(1)
    ups[3].after_far()
    mixes[1].launch()
    ups[2].after_near()
    ups[0].after_z()
    mix_grad(2)
    mix_grad(3)
    down[0].after_far()
    first_norm_back()
    small_out()
    outs.after_far()
    mixes[2].launch()
    ups[3].after_near()
    ups[1].after_z()
    totals.begin()
    down[0].after_near()
    mixes[0].after_far()
    mixes[3].launch()
    outs.after_near()
    ups[2].after_z()
    mixes[1].after_far()
    mixes[0].after_near()
    ups[3].after_z()
    mixes[2].after_far()
    totals.after_far()
    mixes[1].after_near()
    outs.after_z()
    mixes[3].after_far()
    mixes[2].after_near()
    mixes[0].after_z()
    totals.after_near()
    mixes[3].after_near()
    for s in mixes[1:]:
        s.after_z()
    totals.after_z()
    wires.arrived(lo_out.at[rows_own], back)
    wires.arrived(ig_there, back + 1)
    wires.arrived(tg_out.at[p.y], back + 2)
    for copy in (lo_copy, ig_copy, tg_copy):
        copy.wait()
    wires.finish()


def results_kernel(mix, out, up, down, lo, ig, ig_there, tg, small, lo_out, ig_out, time_out, *rest):
    gain1, shift1, o_mix, mbias, o_out, obias, gain2, shift2, o_up, ubias, o_down, dbias, wide, sem = rest
    y = lax.axis_index(SEQ)
    pairs = [(mix, o_mix), (out, o_out), (up, o_up), (down, o_down), (lo, lo_out), (ig, ig_out.at[pl.ds(2 * y, 2)])]
    copies = [pltpu.make_async_copy(src, dst, sem.at[i]) for i, (src, dst) in enumerate(pairs)]
    wide[...] = ig_there[...].astype(F32)
    copies.append(pltpu.make_async_copy(wide, ig_out.at[pl.ds(2 - 2 * y, 2)], sem.at[len(pairs)]))
    for copy in copies:
        copy.start()
    time_out[...] = jnp.concatenate([tg[0, 0:2], tg[1, 0:2]], 0)
    first = 0
    for ref in (gain1, shift1, obias, gain2, shift2, dbias, mbias, ubias):
        count = ref.shape[0] // PIECE
        ref[...] = jnp.concatenate([small[first + i:first + i + 1, :PIECE] for i in range(count)], 1)[0]
        first += count
    for copy in copies:
        copy.wait()


def in_one_kernel(inputs, time_embed, segment_ids, cotangent, gain1, shift1, mix, mbias, out, obias, gain2, shift2, up, ubias,
                  down, dbias):
    table = scratch_table(SLOTS)
    anywhere, vmem = pl.BlockSpec(memory_space=pl.ANY), pl.BlockSpec(memory_space=pltpu.VMEM)
    shape = jax.ShapeDtypeStruct
    tokens = inputs.shape
    here = (tokens[0] // 2,) + tokens[1:]
    g_mix, g_out, g_up, g_down, small, lo, ig, ig_there, tg = pl.pallas_call(
        partial(layer_kernel, [name for name, _, _ in table]),
        out_shape=[shape(w.shape, F32) for w in (mix, out, up, down)]
        + [shape((16, 128), F32), shape(tokens, BF16), shape(here, F32), shape(here, BF16), shape((2, 8, PART), F32)],
        in_specs=[vmem] * 14 + [anywhere] * 2,
        out_specs=[vmem] * 5 + [anywhere] * 4,
        scratch_shapes=[pltpu.SemaphoreType.DMA(shape) if kind is None else pltpu.VMEM(shape, kind) for _, shape, kind in table],
        compiler_params=pltpu.CompilerParams(collective_id=0, has_side_effects=True, vmem_limit_bytes=60 * 2**20),
    )(mix, out, up, down, gain1, shift1, obias, gain2, shift2, dbias, mbias, ubias, time_embed, segment_ids, inputs, cotangent)
    params = (gain1, shift1, mix, mbias, out, obias, gain2, shift2, up, ubias, down, dbias)
    return tuple(pl.pallas_call(
        results_kernel,
        out_shape=[shape(tokens, BF16), shape(tokens, F32), shape((tokens[0], PART), F32)] + [shape(w.shape, F32) for w in params],
        in_specs=[vmem] * 9,
        out_specs=[anywhere] * 2 + [vmem] + [anywhere if w.ndim == 2 else vmem for w in params],
        scratch_shapes=[pltpu.VMEM(here, F32), pltpu.SemaphoreType.DMA((7,))],
    )(g_mix, g_out, g_up, g_down, lo, ig, ig_there, tg, small))


def solution(mesh):
    fits = mesh.shape[BATCH] == 16 and mesh.shape[SEQ] == 2
    tokens, rows, vector, matrix = P(BATCH, SEQ, None), P(BATCH, None), P(AXES), P(AXES, None)
    params = (vector, vector, matrix, vector, matrix, vector, vector, vector, matrix, vector, matrix, vector)
    return jax.shard_map(
        in_one_kernel if fits else any_mesh,
        mesh=mesh,
        in_specs=(tokens, rows, rows, tokens) + params,
        out_specs=(tokens, tokens, P(BATCH, SEQ)) + params,
        check_vma=False,
    )
```

```python
from functools import partial
import math
from types import SimpleNamespace

import jax
import jax.numpy as jnp
from jax import lax
from jax.experimental import pallas as pl
from jax.experimental.pallas import tpu as pltpu
from jax.sharding import PartitionSpec as P

HEAD_DIM = 64
EPSILON = 1e-05
NEG_FILL = -1e30
BATCH, SEQ = "batch", "seq"
AXES = (BATCH, SEQ)
F32, BF16 = jnp.float32, jnp.bfloat16


def norm_back(d_out, normal, inv, gain):
    g = d_out * gain
    return inv * (g - jnp.mean(g, -1, keepdims=True) - normal * jnp.mean(g * normal, -1, keepdims=True))


def normal_part(hidden):
    centred = hidden - jnp.mean(hidden, -1, keepdims=True)
    inv = lax.rsqrt(jnp.mean(centred * centred, -1, keepdims=True) + EPSILON)
    return centred * inv, inv


def contract(a, b, over_a, over_b, batch=((), ())):
    return lax.dot_general(a, b, ((over_a, over_b), batch), preferred_element_type=F32)


def layer(inputs, time, ids, cot, params):
    (gain1, shift1, mix, mbias, out, obias, gain2, shift2, up, ubias, down, dbias) = params
    gain1, shift1, mbias, obias, gain2, shift2, ubias, dbias = (
        v.astype(F32) for v in (gain1, shift1, mbias, obias, gain2, shift2, ubias, dbias))
    rows, length, width = inputs.shape
    heads = width // HEAD_DIM
    scale = 1.0 / math.sqrt(HEAD_DIM)
    flat = lambda t: t.reshape(rows * length, -1)
    by_head = lambda t: t.reshape(rows, length, heads, HEAD_DIM).transpose(0, 2, 1, 3).reshape(rows * heads, length, HEAD_DIM)
    unhead = lambda t: flat(t.reshape(rows, heads, length, HEAD_DIM).transpose(0, 2, 1, 3))
    each = ((0,), (0,))
    cot = flat(cot)
    res_in = flat(inputs.astype(F32) + time.astype(F32)[:, None, :])
    norm1, inv1 = normal_part(res_in)
    normed1 = (norm1 * gain1 + shift1).astype(BF16)
    proj = contract(normed1, mix, (1,), (0,))
    q = by_head((proj[:, :width] + mbias[:width]).astype(BF16))
    k = by_head(proj[:, width:2 * width].astype(BF16))
    v = by_head((proj[:, 2 * width:] + mbias[width:]).astype(BF16))
    scores = contract(q, k, (2,), (2,), each) * scale
    same = jnp.repeat(ids[:, :, None] == ids[:, None, :], heads, axis=0)
    masked = jnp.where(same, scores, NEG_FILL)
    top = jnp.max(masked, -1, keepdims=True)
    log_total = top + jnp.log(jnp.sum(jnp.exp(masked - top), -1, keepdims=True))
    probs = jnp.exp(masked - log_total)
    probs16 = probs.astype(BF16)
    att = unhead(contract(probs16, v, (2,), (1,), each).astype(BF16))
    res_mid = res_in + (contract(att, out, (1,), (0,)) + obias)
    norm2, inv2 = normal_part(res_mid)
    normed2 = (norm2 * gain2 + shift2).astype(BF16)
    hid = contract(normed2, up, (1,), (0,)) + ubias
    cdf = 0.5 * (1.0 + lax.erf(hid * math.sqrt(0.5)))
    act = (hid * cdf).astype(BF16)
    layer_out = (res_mid + contract(act, down, (1,), (0,)) + dbias).astype(BF16)

    cot32 = cot.astype(F32)
    slope = cdf + hid * jnp.exp(-0.5 * hid * hid) * (1.0 / math.sqrt(2 * math.pi))
    d_hid = (contract(cot, down, (1,), (1,)) * slope).astype(BF16)
    d_n2 = contract(d_hid, up, (1,), (1,))
    d_mid = cot32 + norm_back(d_n2, norm2, inv2, gain2)
    d_br = d_mid.astype(BF16)
    d_att = by_head(contract(d_br, out, (1,), (1,)).astype(BF16))
    d_pr = contract(d_att, v, (2,), (2,), each)
    d_sc = (probs * (d_pr - jnp.sum(probs * d_pr, -1, keepdims=True))).astype(BF16)
    d_q = unhead((contract(d_sc, k, (2,), (1,), each) * scale).astype(BF16))
    d_k = unhead((contract(d_sc, q, (1,), (1,), each) * scale).astype(BF16))
    d_v = unhead(contract(probs16, d_att, (1,), (1,), each).astype(BF16))
    d_proj = jnp.concatenate([d_q, d_k, d_v], -1)
    d_n1 = contract(d_proj, mix, (1,), (1,))
    x_grad = d_mid + norm_back(d_n1, norm1, inv1, gain1)

    def col(t):
        return jnp.sum(t.astype(F32), axis=0)

    weigh = lambda a, b: contract(a, b, (0,), (0,))
    grads = (col(d_n1 * norm1), col(d_n1), weigh(normed1, d_proj), jnp.concatenate([col(d_q), col(d_v)]),
             weigh(att, d_br), col(d_br), col(d_n2 * norm2), col(d_n2), weigh(normed2, d_hid), col(d_hid),
             weigh(act, cot), col(cot32))
    return layer_out.reshape(inputs.shape), x_grad.reshape(inputs.shape), grads


def gather_all(shard):
    return lax.all_gather(shard, AXES, axis=0, tiled=True)


def scatter_sum(grad):
    return lax.psum_scatter(grad, AXES, scatter_dimension=0, tiled=True)


def rows_whole(tensor):
    return lax.all_to_all(tensor, SEQ, split_axis=0, concat_axis=1, tiled=True)


def rows_split(tensor):
    return lax.all_to_all(tensor, SEQ, split_axis=1, concat_axis=0, tiled=True)


def any_mesh(inputs, time_embed, segment_ids, cotangent, *shards):
    y, count = lax.axis_index(SEQ), inputs.shape[0] // lax.axis_size(SEQ)
    mine = [lax.dynamic_slice_in_dim(t, y * count, count, 0) for t in (time_embed, segment_ids)]
    layer_out, x_grad, grads = layer(
        rows_whole(inputs), mine[0], mine[1], rows_whole(cotangent), [gather_all(w) for w in shards])
    time_grad = lax.all_to_all(jnp.sum(x_grad, 1), SEQ, split_axis=1, concat_axis=0, tiled=True)
    return (rows_split(layer_out), rows_split(x_grad), time_grad) + tuple(scatter_sum(g) for g in grads)


MESH = pl.DeviceIdType.MESH
Z_CHIPS = 4
TOKENS, WIDTH, HIDDEN, PART = 256, 768, 3072, 384
SMALL = (16, WIDTH)
PIECE = 24
TRANSPOSED = ((1,), (1,))
TOKEN_SUM = ((0,), (0,))


class Place:
    def __init__(self):
        b, self.y = lax.axis_index(BATCH), lax.axis_index(SEQ)
        self.z, self.x, self.c = b // 4, (b // 2) % 2, b % 2
        z, x, c, y = self.z, self.x, self.c, self.y
        self.twin = self.at(z, x, 1 - c, y)
        self.x_peer = self.at(z, 1 - x, c, y)
        self.y_peer = self.at(z, x, c, 1 - y)
        self.z_slots = [lax.rem(z + d, Z_CHIPS) for d in (1, 2, 3)]
        self.z_peers = [self.at(q, x, c, y) for q in self.z_slots]

    @staticmethod
    def at(z, x, c, y):
        return ((z * 2 + x) * 2 + c, y)

    def routes(self, turn):
        c = 1 if turn else self.c
        x, y = self.x, self.y
        return (x + (1 - 2 * x) * (1 - c), y + (1 - 2 * y) * c), (x + (1 - 2 * x) * c, y + (1 - 2 * y) * (1 - c))

    def on_chip(self, chip):
        return self.at(self.z, chip[0], self.c, chip[1])

    def role(self, c, x, y):
        dx, dy = (x + self.x) % 2, (y + self.y) % 2
        return (dx + 2 * dy) * (1 - c) + (dy + 2 * dx) * c

    def of_role(self, c, role):
        low, high = role % 2, role // 2
        dx, dy = low * (1 - c) + high * c, high * (1 - c) + low * c
        return (self.x + dx) % 2, (self.y + dy) % 2

    def greet(self):
        self.partners = self.z_peers + [self.x_peer, self.y_peer, self.twin]
        for partner in self.partners:
            pl.semaphore_signal(pltpu.get_barrier_semaphore(), inc=1, device_id=partner, device_id_type=MESH)

    def all_here(self):
        pl.semaphore_wait(pltpu.get_barrier_semaphore(), len(self.partners))


class Wires:
    def __init__(self, send_sem, recv_sem, place):
        self.send_sem, self.recv_sem, self.place = send_sem, recv_sem, place
        self.sent, self.used = [], 0

    def slots(self, count):
        self.used += count
        return self.used - count

    def start(self, src, dst, slot, device):
        copy = pltpu.make_async_remote_copy(
            src_ref=src, dst_ref=dst, send_sem=self.send_sem.at[slot], recv_sem=self.recv_sem.at[slot],
            device_id=device, device_id_type=MESH,
        )
        copy.start()
        self.sent.append(copy)
        return copy

    def arrived(self, dst, slot):
        pltpu.make_async_remote_copy(
            src_ref=dst, dst_ref=dst, send_sem=self.send_sem.at[slot], recv_sem=self.recv_sem.at[slot],
            device_id=self.place.twin, device_id_type=MESH,
        ).wait_recv()

    def left(self, copies):
        for copy in copies:
            copy.wait_send()
        self.sent = [kept for kept in self.sent if all(kept is not copy for copy in copies)]

    def finish(self):
        for copy in self.sent:
            copy.wait_send()
        self.sent = []


class Gather:
    def __init__(self, wires, place, own, buf, at, wide, turn=False):
        self.w, self.p, self.own, self.buf, self.cols = wires, place, own, buf, pl.ds(at, wide)
        self.base, self.copies = wires.slots(10), []
        self.near, self.far = place.routes(turn)

    def send(self, src, dst, slot, device):
        self.copies.append(self.w.start(src, dst, self.base + slot, device))

    def mine(self):
        p = self.p
        return self.buf.at[p.z, p.x, p.c, p.y, :, self.cols]

    def block(self, x, y, c):
        return self.buf.at[:, x, c, y, :, self.cols]

    def begin(self):
        for j, peer in enumerate(self.p.z_peers):
            self.send(self.own.at[:, self.cols], self.mine(), j, peer)

    def after_z(self):
        p = self.p
        for j in range(3):
            self.w.arrived(self.mine(), self.base + j)
        b = self.block(p.x, p.y, p.c)
        self.send(b, b, 3, p.on_chip(self.near))
        self.send(b, b, 4, p.on_chip(self.far))
        self.send(b, b, 6, p.twin)

    def after_near(self):
        p = self.p
        b = self.block(*self.near, p.c)
        self.w.arrived(b, self.base + 3)
        self.send(b, b, 5, p.on_chip(self.far))
        self.send(b, b, 7, p.twin)

    def after_far(self):
        p = self.p
        b = self.block(*self.far, p.c)
        self.w.arrived(b, self.base + 4)
        self.send(b, b, 8, p.twin)
        b = self.block(1 - p.x, 1 - p.y, p.c)
        self.w.arrived(b, self.base + 5)
        self.send(b, b, 9, p.twin)
        for j in range(6, 10):
            self.w.arrived(self.block(p.x, p.y, 1 - p.c), self.base + j)

    def halves_in_place(self):
        self.w.left(self.copies)
        rows = self.buf.shape[-2] // 2

        @pl.loop(0, 16)
        def _(pair):
            z, x, c = pair // 4, (pair // 2) % 2, pair % 2
            v = [self.buf[z, x, c, y, :, self.cols].astype(F32) for y in (0, 1)]
            for h in (0, 1):
                part = slice(h * rows, h * rows + rows)
                self.buf[z, x, c, h, :, self.cols] = jnp.concatenate([v[0][part], v[1][part]], 0).astype(BF16)


class LayerFirst(Gather):
    def begin(self):
        for j, chip in enumerate((self.near, self.far)):
            self.send(self.own.at[:, self.cols], self.mine(), j, self.p.on_chip(chip))

    def shard(self, chip):
        return self.buf.at[self.p.z, chip[0], self.p.c, chip[1], :, self.cols]

    def layer(self, z, c):
        return self.buf.at[z, :, c, :, :, self.cols]

    def forward(self):
        b = self.shard(self.near)
        self.w.arrived(b, self.base)
        self.send(b, b, 2, self.p.on_chip(self.far))

    def along_z(self):
        p = self.p
        self.w.arrived(self.shard(self.far), self.base + 1)
        self.w.arrived(self.shard((1 - p.x, 1 - p.y)), self.base + 2)
        b = self.layer(p.z, p.c)
        for j, peer in enumerate(p.z_peers):
            self.send(b, b, 3 + j, peer)
        self.send(b, b, 6, p.twin)

    def after_z(self):
        p = self.p
        for j in range(3):
            b = self.layer(lax.rem(p.z + 3 - j, Z_CHIPS), p.c)
            self.w.arrived(b, self.base + 3 + j)
            self.send(b, b, 7 + j, p.twin)
        for j in range(6, 10):
            self.w.arrived(self.layer(p.z, 1 - p.c), self.base + j)


class Scatter:
    def __init__(self, wires, place, rows, cols, keep, s1, r1, s2, r2, sz, rz, out, out_cols, turn=False):
        self.w, self.p, self.rows, self.cols, self.out_cols = wires, place, rows, cols, out_cols
        self.keep, self.s1, self.r1, self.s2, self.r2, self.sz, self.rz, self.out = keep, s1, r1, s2, r2, sz, rz, out
        self.base, self.quarter, self.packed = wires.slots(5), Z_CHIPS * rows, rows % 16 != 0
        wide = cols.size // 2 if self.packed else cols.size
        self.z_cols = pl.ds(cols.start // 2 if self.packed else cols.start, wide)
        near, far = place.routes(turn)
        self.near, self.far = place.on_chip(near), place.on_chip(far)
        swapped = (1 - place.c) if turn else 0
        self.roles = (0, 1 + swapped, 2 - swapped, 3)

    def begin(self, left, right):
        q = self.quarter
        for i, role in enumerate(self.roles):
            total = contract(left(0, role), right[0], (1,), (0,)) + contract(left(1, role), right[1], (1,), (0,))
            at = pl.ds((i % 2) * q, q)
            if i < 2:
                self.keep[at, self.cols] = total
            else:
                self.s1[at, self.cols] = total.astype(BF16)
    def launch(self):
        both = pl.ds(0, 2 * self.quarter)
        self.w.start(self.s1.at[both, self.cols], self.r1.at[both, self.cols], self.base, self.far)

    def after_far(self):
        q = self.quarter
        self.w.arrived(self.r1.at[pl.ds(0, 2 * q), self.cols], self.base)
        at = pl.ds(q, q)
        self.s2[:, self.cols] = (self.keep[at, self.cols] + self.r1[at, self.cols].astype(F32)).astype(BF16)
        self.w.start(self.s2.at[:, self.cols], self.r2.at[:, self.cols], self.base + 1, self.near)

    def after_near(self):
        q, n = self.quarter, self.rows
        self.w.arrived(self.r2.at[:, self.cols], self.base + 1)
        at = pl.ds(0, q)
        total = self.keep[at, self.cols] + self.r1[at, self.cols].astype(F32) + self.r2[:, self.cols].astype(F32)
        for z in range(Z_CHIPS):
            piece = total[z * n:z * n + n]

            @pl.when(z == self.p.z)
            def _():
                self.out[:, self.out_cols] = piece

            if self.packed:
                half = self.z_cols.size
                piece = jnp.concatenate([piece[:, :half], piece[:, half:]], 0)
            self.sz[z, :, self.z_cols] = piece.astype(BF16)
        for j, (z, peer) in enumerate(zip(self.p.z_slots, self.p.z_peers)):
            self.w.start(self.sz.at[z, :, self.z_cols], self.rz.at[j, :, self.z_cols], self.base + 2 + j, peer)

    def after_z(self):
        total = 0.0
        for j in range(3):
            self.w.arrived(self.rz.at[j, :, self.z_cols], self.base + 2 + j)
            total = total + self.rz[j, :, self.z_cols].astype(F32)
        if self.packed:
            total = jnp.concatenate([total[:self.rows], total[self.rows:]], 1)
        self.out[:, self.out_cols] = self.out[:, self.out_cols] + total


class AlongZFirst(Scatter):
    def __init__(self, *args, zs, zr):
        super().__init__(*args)
        self.zs, self.zr = zs, zr

    def begin(self, left, right):
        n = self.rows
        for role in range(4):
            total = contract(left(0, role), right[0], (1,), (0,)) + contract(left(1, role), right[1], (1,), (0,))
            for z in range(Z_CHIPS):
                piece = total[z * n:z * n + n]
                self.zs[z, role] = piece.astype(BF16)

                @pl.when(z == self.p.z)
                def _():
                    self.keep[pl.ds(role * n, n), self.cols] = piece

        for j, (z, peer) in enumerate(zip(self.p.z_slots, self.p.z_peers)):
            self.w.start(self.zs.at[z], self.zr.at[j], self.base + 2 + j, peer)

    def after_z(self):
        n = self.rows
        for j in range(3):
            self.w.arrived(self.zr.at[j], self.base + 2 + j)
        for role in range(4):
            at = pl.ds(role * n, n)
            total = self.keep[at, self.cols]
            for j in range(3):
                total = total + self.zr[j, role].astype(F32)
            if role < 2:
                self.keep[at, self.cols] = total
            else:
                self.s1[pl.ds((role - 2) * n, n), self.cols] = total.astype(BF16)
        both = pl.ds(0, 2 * n)
        self.w.start(self.s1.at[both, self.cols], self.r1.at[both, self.cols], self.base, self.far)

    def after_far(self):
        n = self.rows
        self.w.arrived(self.r1.at[pl.ds(0, 2 * n), self.cols], self.base)
        at, first = pl.ds(n, n), pl.ds(0, n)
        self.s2[first, self.cols] = (self.keep[at, self.cols] + self.r1[at, self.cols].astype(F32)).astype(BF16)
        self.w.start(self.s2.at[first, self.cols], self.r2.at[first, self.cols], self.base + 1, self.near)

    def after_near(self):
        at = pl.ds(0, self.rows)
        self.w.arrived(self.r2.at[at, self.cols], self.base + 1)
        self.out[:, self.out_cols] = (
            self.keep[at, self.cols] + self.r1[at, self.cols].astype(F32) + self.r2[at, self.cols].astype(F32))


class SmallScatter:
    def __init__(self, wires, place, slabs, from_twin, s1, r1, s2, r2, sz, rz, out):
        self.w, self.p, self.slabs, self.from_twin = wires, place, slabs, from_twin
        self.s1, self.r1, self.s2, self.r2, self.sz, self.rz, self.out = s1, r1, s2, r2, sz, rz, out
        self.base = wires.slots(6)
        near, far = place.routes(False)
        self.chips = ((place.x, place.y), near, far, (1 - place.x, 1 - place.y))
        self.near, self.far = place.on_chip(near), place.on_chip(far)

    def summed(self, role):
        x, y = self.chips[role]
        return self.slabs[:, x, self.p.c, y] + self.from_twin[:, x, y]

    def to_twin(self):
        self.w.start(self.slabs.at[:, :, 1 - self.p.c], self.from_twin, self.base, self.p.twin)

    def begin(self):
        self.w.arrived(self.from_twin, self.base)
        self.s1[0], self.s1[1] = self.summed(2), self.summed(3)
        self.w.start(self.s1, self.r1, self.base + 1, self.far)

    def after_far(self):
        self.w.arrived(self.r1, self.base + 1)
        self.s2[...] = self.summed(1) + self.r1[1]
        self.w.start(self.s2, self.r2, self.base + 2, self.near)

    def after_near(self):
        self.w.arrived(self.r2, self.base + 2)
        self.sz[...] = self.summed(0) + self.r1[0] + self.r2[...]
        for j, (z, peer) in enumerate(zip(self.p.z_slots, self.p.z_peers)):
            self.w.start(self.sz.at[z], self.rz.at[j], self.base + 3 + j, peer)

    def after_z(self):
        total = self.sz[self.p.z]
        for j in range(3):
            self.w.arrived(self.rz.at[j], self.base + 3 + j)
            total = total + self.rz[j]
        self.out[...] = total


def merged(value):
    return value.reshape(-1, value.shape[-1])


def by_rows(step, body, *carry):
    return lax.fori_loop(0, TOKENS // step, lambda i, kept: body(i, pl.ds(pl.multiple_of(i * step, step), step), *kept), carry)


def folded(value):
    return jnp.sum(value.reshape(value.shape[0] // 8, 8, value.shape[1]), 0)


def column_sums(value):
    return contract(jnp.ones((8, value.shape[0]), BF16), value, (1,), (0,))[0:1]


def token_block(i):
    return i // 4, (i // 2) % 2, pl.ds(pl.multiple_of((i % 2) * 32, 32), 32)


def scratch_table(slots):
    k, w = WIDTH // 2, WIDTH
    return [
        ("par", SMALL, F32), ("sums", SMALL, F32), ("small", (16, 128), BF16), ("bs", (4, 2, 2, 2, 16, 128), BF16),
        ("slabs", (4, 2, 2, 2, 16, 128), F32), ("from_twin", (4, 2, 2, 16, 128), F32), ("s1_s", (2, 4, 16, 128), F32),
        ("r1_s", (2, 4, 16, 128), F32), ("s2_s", (4, 16, 128), F32), ("r2_s", (4, 16, 128), F32),
        ("sz_s", (4, 16, 128), F32), ("rz_s", (3, 16, 128), F32),
        ("w1", (48, 1536), BF16), ("w2", (48, 1536), BF16), ("same", (2, 128, 128), F32), ("time", (2, 1, w), F32),
        ("b1", (4, 2, 2, 2, 48, 1536), BF16), ("b2", (4, 2, 2, 2, 48, 1536), BF16), ("b3", (4, 2, 2, 2, 96, w), BF16),
        ("x0", (2, 2, 64, w), BF16), ("cot", (2, 2, 2, 64, w), BF16),
        ("res_in", (TOKENS, w), F32), ("normed1", (TOKENS, w), BF16), ("qkv", (TOKENS, 3 * w), BF16),
        ("probs", (12, TOKENS, 128), F32), ("att", (TOKENS, w), BF16), ("res_mid", (TOKENS, w), F32),
        ("normed2", (TOKENS, w), BF16), ("slope", (TOKENS, HIDDEN), F32), ("act", (TOKENS, HIDDEN), BF16),
        ("pick", (2, k, w), BF16), ("pick_act", (2, 192, PART), BF16),
        ("t1", (2, k, TOKENS), BF16), ("t1_send", (k, TOKENS), BF16),
        ("to", (2, k, TOKENS), BF16), ("to_send", (k, TOKENS), BF16),
        ("t2", (2, k, TOKENS), BF16), ("t2_send", (k, TOKENS), BF16),
        ("ta", (2, 4, 4, 96, TOKENS), BF16), ("ta_send", (4, 4, 96, TOKENS), BF16),
        ("d_hid", (2, TOKENS, HIDDEN), BF16), ("d_norm", (TOKENS, w), F32),
        ("d_branch", (2, TOKENS, w), BF16), ("d_proj", (2, TOKENS, 3 * w), BF16),
        ("ig", (2, 2, 64, w), F32), ("tg", (2, 8, PART), F32),
        ("keep_d", (768, w), F32), ("s1_d", (768, w), BF16), ("r1_d", (768, w), BF16), ("s2_d", (PART, w), BF16),
        ("r2_d", (PART, w), BF16), ("sz_d", (4, 96, w), BF16), ("rz_d", (3, 96, w), BF16),
        ("zr_d", (3, 4, 96, 256), BF16), ("ig_send", (2, 64, w), BF16),
        ("keep_u", (192, HIDDEN), F32), ("s1_u", (192, HIDDEN), BF16), ("r1_u", (192, HIDDEN), BF16),
        ("s2_u", (96, HIDDEN), BF16), ("r2_u", (96, HIDDEN), BF16), ("sz_u", (4, 48, 1536), BF16), ("rz_u", (3, 48, 1536), BF16),
        ("r1_m", (192, HIDDEN), BF16),
        ("s2_m", (96, HIDDEN), BF16), ("r2_m", (96, HIDDEN), BF16), ("sz_m", (4, 48, 1536), BF16), ("rz_m", (3, 48, 1536), BF16),
        ("send_sem", (slots,), None), ("recv_sem", (slots,), None), ("local_sem", (10,), None),
    ]


SLOTS = 240
AHEAD = 4
TURNED = ()
UPS_TURNED, MIX_TURNED = (), (1, 3)


def iota(shape, dim):
    return lax.broadcasted_iota(jnp.int32, shape, dim)


def piece_place(row, device):
    block = jnp.where(row < 6, device, jnp.where(row < 8, 2 * device + row - 6, 4 * device + row - 8))
    first = jnp.where(row < 6, row, jnp.where(row < 8, 6, 8))
    return jnp.where(row < 12, first + (block >> 5), -1), block & 31


def ones_where(condition):
    return condition.astype(F32).astype(BF16)


def lane_piece(shape):
    return (iota(shape, 1) * 2731) >> 16


def every_piece():
    shape = (128, WIDTH)
    return ones_where(iota(shape, 1) - PIECE * lane_piece(shape) == iota(shape, 0))


def slab_rows(first, count):
    n = iota((SMALL[0], count), 1) + first
    return ones_where(piece_place(n & 15, n >> 4)[0] == iota((SMALL[0], count), 0))


def slab_places(first, count):
    n = iota((count, WIDTH), 0) + first
    return (piece_place(n & 15, n >> 4)[1] == lane_piece((count, WIDTH))).astype(F32)


def whole_of(ref):
    total = 0.0
    for z in range(Z_CHIPS):
        wide = contract(merged(ref[z]), every_piece(), (1,), (0,)) * slab_places(128 * z, 128)
        total = total + contract(slab_rows(128 * z, 128), wide.astype(BF16), (1,), (0,))
    return total


def put_slabs(ref, whole):
    high = whole.astype(BF16)
    parts = (high, (whole - high.astype(F32)).astype(BF16))
    for z in range(Z_CHIPS):
        places, total = slab_places(128 * z, 128), 0.0
        for part in parts:
            wide = contract(slab_rows(128 * z, 128), part, *TOKEN_SUM) * places
            total = total + contract(wide.astype(BF16), every_piece(), *TRANSPOSED)
        ref[z] = total.reshape(ref.shape[1:])


def layer_kernel(names, mix, out, up, w3, gain1, shift1, obias, gain2, shift2, dbias, mbias, ubias, time, ids, xin, cin,
                 o_mix, o_out, o_up, o_down, o_small, lo_out, ig_out, ig_there, tg_out, *scratch):
    m = SimpleNamespace(**dict(zip(names, scratch)))
    p = Place()
    p.greet()
    wires = Wires(m.send_sem, m.recv_sem, p)
    me, twin = p.c, 1 - p.c
    scale = 1.0 / math.sqrt(HEAD_DIM)

    own, bufs = (m.w1, m.w2, w3), (m.b1, m.b2, m.b3)
    for ref, target, at in ((mix, m.w1, 0), (out, m.w1, 3 * PART), (up, m.w2, 0)):
        half = ref.shape[1] // 2
        value = ref[...].astype(F32)
        target[:, at:at + half] = jnp.concatenate([value[:, :half], value[:, half:]], 0).astype(BF16)
    pieces = []
    for ref in (gain1, shift1, obias, gain2, shift2, dbias, mbias, ubias):
        value = ref[...].astype(F32).reshape(1, ref.shape[0])
        pieces += [value[:, at:at + PIECE] for at in range(0, ref.shape[0], PIECE)]
    pieces.append(jnp.zeros((16 - len(pieces), PIECE), F32))
    m.small[...] = jnp.concatenate([jnp.concatenate(pieces, 0), jnp.zeros((16, 128 - PIECE), F32)], 1).astype(BF16)
    p.all_here()
    plan = [(0, PART * i, PART) for i in range(4)] + [(1, PART * i, PART) for i in range(4)] + [(2, 256 * i, 256) for i in range(3)]
    gathers = [Gather(wires, p, own[w], bufs[w], at, wide, k in TURNED) for k, (w, at, wide) in enumerate(plan[:-1])]
    last = LayerFirst(wires, p, own[2], bufs[2], *plan[-1][1:])
    params = Gather(wires, p, m.small, m.bs, 0, 128)
    params.begin()
    for g in gathers[:AHEAD]:
        g.begin()
    locs = [pltpu.make_async_copy(own[i], bufs[i].at[p.z, p.x, p.c, p.y], m.local_sem.at[i]) for i in range(3)]
    rows_own, rows_other = pl.ds(2 * p.y, 2), pl.ds(2 - 2 * p.y, 2)
    locs.append(pltpu.make_async_copy(xin.at[rows_own], m.x0.at[:, p.y], m.local_sem.at[3]))
    locs.append(pltpu.make_async_copy(cin.at[rows_own], m.cot.at[me, :, p.y], m.local_sem.at[4]))
    for copy in locs:
        copy.start()
    swap = wires.slots(3)
    small_copy = pltpu.make_async_copy(m.small, m.bs.at[p.z, p.x, p.c, p.y], m.local_sem.at[8])
    small_copy.start()
    wires.start(xin.at[rows_other], m.x0.at[:, p.y], swap, p.y_peer)
    last.begin()
    wires.start(cin.at[rows_other], m.cot.at[me, :, p.y], swap + 1, p.y_peer)

    def z_step(k):
        gathers[k].after_z()
        if k + AHEAD < len(gathers):
            gathers[k + AHEAD].begin()

    def near_step(k):
        gathers[k].after_near()

    def far_step(k):
        gathers[k].after_far()
        if plan[k][0] < 2:
            gathers[k].halves_in_place()

    lane, row = lax.broadcasted_iota(jnp.int32, (24, WIDTH), 1), lax.broadcasted_iota(jnp.int32, (24, WIDTH), 0)
    lane_a, row_a = lax.broadcasted_iota(jnp.int32, (192, PART), 1), lax.broadcasted_iota(jnp.int32, (192, PART), 0)
    for side, c in ((0, me), (1, twin)):
        pieces = []
        for role in range(4):
            x, y = p.of_role(c, role)
            for z in range(Z_CHIPS):
                first = (((z * 2 + x) * 2 + c) * 2 + y) * 24
                pieces.append((lane == row + first).astype(F32))
        m.pick[side] = jnp.concatenate(pieces, 0).astype(BF16)
        m.pick_act[side] = (lane_a == row_a + c * 192).astype(F32).astype(BF16)

    for r in (0, 1):
        m.time[r] = jnp.where(p.y == 0, time[r:r + 1, :].astype(F32), time[r + 2:r + 3, :].astype(F32))
        along = jnp.where(p.y == 0, ids[r:r + 1, :], ids[r + 2:r + 3, :])
        one_hot = (lax.broadcasted_iota(jnp.int32, (8, 128), 0) == along).astype(F32).astype(BF16)
        m.same[r] = contract(one_hot, one_hot, *TOKEN_SUM)

    twin_base = wires.slots(16)

    def transposed(value, ref, send, slot):
        ref[me] = contract(m.pick[0], value, *TRANSPOSED).astype(BF16)
        send[...] = contract(m.pick[1], value, *TRANSPOSED).astype(BF16)
        wires.start(send, ref.at[me], twin_base + slot, p.twin)

    def left_of(ref, quarter=96):
        return lambda core, role: ref[core, pl.ds(role * quarter, quarter), :]

    def left_act(core, role):
        return merged(m.ta[core, role])

    def normal(h):
        centred = h - jnp.mean(h, -1, keepdims=True)
        inv = lax.rsqrt(jnp.mean(centred * centred, -1, keepdims=True) + EPSILON)
        return centred * inv, inv

    def first_norm():
        m.par[...] = whole_of(m.bs)
        for copy in locs[3:]:
            copy.wait()
        wires.arrived(m.x0.at[:, p.y], swap)

        def body(i, at):
            r, half, pos = token_block(i)
            h = m.x0[r, half, pos, :].astype(F32) + m.time[r]
            m.res_in[at, :] = h
            m.normed1[at, :] = (normal(h)[0] * m.par[0:1, :] + m.par[1:2, :]).astype(BF16)
            return ()

        by_rows(32, body)
        transposed(m.normed1[...], m.t1, m.t1_send, 0)

    def projected(k):
        for h in (0, 1):
            weight = merged(m.b1[:, :, :, h, :, pl.ds(PART * k, PART)])
            group, lanes = (3 * h + k) // 2, PART * ((3 * h + k) % 2)
            total = contract(m.normed1[...], weight, (1,), (0,))
            if group != 1:
                total = total + m.par[6 + group // 2:7 + group // 2, lanes:lanes + PART]
            m.qkv[:, WIDTH * group + lanes:WIDTH * group + lanes + PART] = total.astype(BF16)

    low = (lax.broadcasted_iota(jnp.int32, (1, 128), 1) < HEAD_DIM).astype(F32)
    heads_of = [low.astype(BF16), (1.0 - low).astype(BF16)]

    def two_heads(value):
        return jnp.concatenate([value * h for h in heads_of], 0)

    def side_by_side(value):
        return jnp.concatenate([value[:128], value[128:]], 1)

    def at_pair(i):
        return pl.ds(pl.multiple_of((i // 6) * 128, 128), 128), [
            pl.ds(pl.multiple_of((i % 6) * 128 + WIDTH * part, 128), 128) for part in range(3)]

    def attention(first, last):
        def body(i, _):
            rows, (cq, ck, cv) = at_pair(i)
            q2, k, v = two_heads(m.qkv[rows, cq]), m.qkv[rows, ck], m.qkv[rows, cv]
            scores = contract(q2, k, *TRANSPOSED) * scale
            same = m.same[i // 6] > 0.5
            masked = jnp.where(jnp.concatenate([same, same], 0), scores, NEG_FILL)
            e = jnp.exp(masked - jnp.max(masked, -1, keepdims=True))
            probs = e / jnp.sum(e, -1, keepdims=True)
            m.probs[i] = probs
            m.att[rows, cq] = contract(side_by_side(probs.astype(BF16)), two_heads(v), (1,), (0,)).astype(BF16)
            return 0

        lax.fori_loop(first, last, body, 0)

    def out_half(h):
        return merged(m.b1[:, :, :, h, :, pl.ds(3 * PART, PART)])

    def branch():
        transposed(m.att[...], m.to, m.to_send, 1)
        for h in (0, 1):
            at = slice(PART * h, PART * h + PART)
            total = contract(m.att[...], out_half(h), (1,), (0,)) + m.par[2:3, at]
            m.res_mid[:, at] = m.res_in[:, at] + total

        def body(i, at):
            m.normed2[at, :] = (normal(m.res_mid[at, :])[0] * m.par[3:4, :] + m.par[4:5, :]).astype(BF16)
            return ()

        by_rows(32, body)
        transposed(m.normed2[...], m.t2, m.t2_send, 2)

    def up_part(k):
        for h in (0, 1):
            first = 1536 * h + PART * k
            cols, lanes = slice(first, first + PART), first % WIDTH
            weight = merged(m.b2[:, :, :, h, :, pl.ds(PART * k, PART)])
            bias = m.par[8 + first // WIDTH:9 + first // WIDTH, lanes:lanes + PART]
            m.slope[:, cols] = contract(m.normed2[...], weight, (1,), (0,)) + bias

            def body(i, at):
                v = m.slope[at, cols]
                cdf = 0.5 + 0.5 * lax.erf(v * math.sqrt(0.5))
                m.act[at, cols] = (v * cdf).astype(BF16)
                m.slope[at, cols] = cdf + v * jnp.exp(-0.5 * v * v) * (1.0 / math.sqrt(2 * math.pi))
                return ()

            by_rows(32, body)
            z, x = (first // PART) // 2, (first // PART) % 2
            act = m.act[:, cols]
            for side, c in ((0, me), (1, twin)):
                picked = contract(m.pick_act[side], act, *TRANSPOSED).astype(BF16)
                for y in (0, 1):
                    role = p.role(c, x, y)
                    piece = picked[96 * y:96 * y + 96]
                    if side == 0:
                        m.ta[me, role, z] = piece
                    else:
                        m.ta_send[role, z] = piece

    def cot_whole():
        wires.arrived(m.cot.at[me, :, p.y], swap + 1)
        wires.start(m.cot.at[me], m.cot.at[me], twin_base + 3, p.twin)

    twin_act = []

    def act_out():
        twin_act.append(wires.start(m.ta_send, m.ta.at[me], twin_base + 4, p.twin))

    def scatter_of(kind, first, wide, out, out_first, turn=False):
        cols, out_cols = pl.ds(first, wide), pl.ds(out_first, wide)
        if kind == 0:
            args = wires, p, 96, cols, m.keep_d, m.s1_d, m.r1_d, m.s2_d, m.r2_d, m.sz_d, m.rz_d, out, out_cols
            return Scatter(*args) if first else AlongZFirst(*args, zs=m.ta_send, zr=m.zr_d)
        if kind == 1:
            return Scatter(wires, p, 24, cols, m.keep_u, m.s1_u, m.r1_u, m.s2_u, m.r2_u, m.sz_u, m.rz_u, out, out_cols, turn)
        return Scatter(wires, p, 24, cols, m.slope, m.act, m.r1_m, m.s2_m, m.r2_m, m.sz_m, m.rz_m, out, out_cols, turn)

    down = [scatter_of(0, 256 * i, 256, o_down, 256 * i) for i in range(3)]
    ups = [scatter_of(1, WIDTH * i, WIDTH, o_up, WIDTH * i, i in UPS_TURNED) for i in range(4)]
    mix_plan = [(0, WIDTH), (WIDTH, WIDTH), (2 * WIDTH, 512), (2 * WIDTH + 512, 256)]
    mixes = [scatter_of(2, at, wide, o_mix, at, i in MIX_TURNED) for i, (at, wide) in enumerate(mix_plan)]
    outs = scatter_of(2, 3 * WIDTH, WIDTH, o_out, 0, True)

    def down_grad(i):
        if i == 0:
            wires.arrived(m.cot.at[twin], twin_base + 3)
            wires.arrived(m.ta.at[twin], twin_base + 4)
            wires.left(twin_act)
            m.sums[...] = jnp.zeros(SMALL, F32)
            m.sums[5:6, :] = column_sums(merged(m.cot[me]))
        cols = pl.ds(256 * i, 256)
        down[i].begin(left_act, [merged(m.cot[core, :, :, :, cols]) for core in (0, 1)])

    def hidden_grad(i):
        cot = merged(m.cot[me])
        for part in (2 * i, 2 * i + 1):
            cols = slice(PART * part, PART * part + PART)
            d_act = contract(cot, merged(m.b3[part // 2, part % 2]), *TRANSPOSED)
            grad = (d_act * m.slope[:, cols]).astype(BF16)
            m.d_hid[me, :, cols] = grad
            lanes = PART * (part % 2)
            m.sums[8 + i:9 + i, lanes:lanes + PART] = column_sums(grad)
        at = m.d_hid.at[me, :, pl.ds(WIDTH * i, WIDTH)]
        wires.start(at, at, twin_base + 5 + i, p.twin)

    def up_grad(i):
        if i == 0:
            wires.arrived(m.t2.at[twin], twin_base + 2)
        cols = pl.ds(WIDTH * i, WIDTH)
        wires.arrived(m.d_hid.at[twin, :, cols], twin_base + 5 + i)
        ups[i].begin(left_of(m.t2), [m.d_hid[core, :, cols] for core in (0, 1)])

    def layer_result(*parts):
        for i in parts:
            cols = slice(256 * i, 256 * i + 256)
            total = contract(m.act[...], merged(m.b3[:, :, :, :, :, cols]), (1,), (0,)) + m.par[5:6, cols]
            total = (m.res_mid[:, cols] + total).astype(BF16)
            for r in (0, 1):
                for half in (0, 1):
                    first = r * 128 + half * 64
                    m.x0[r, half, :, cols] = total[first:first + 64]

    back = wires.slots(3)
    lo_copy = pltpu.make_async_copy(m.x0.at[:, p.y], lo_out.at[rows_own], m.local_sem.at[5])
    ig_copy = pltpu.make_async_copy(m.ig.at[:, p.y], ig_out, m.local_sem.at[6])
    tg_copy = pltpu.make_async_copy(m.tg.at[p.y], tg_out.at[p.y], m.local_sem.at[7])

    def result_out():
        lo_copy.start()
        wires.start(m.x0.at[:, 1 - p.y], lo_out.at[rows_own], back, p.y_peer)

    def second_norm_back():
        halves = [merged(m.b2[:, :, :, h]) for h in (0, 1)]
        m.d_norm[...] = contract(m.d_hid[me, :, 0:1536], halves[0], *TRANSPOSED)
        m.d_norm[...] += contract(m.d_hid[me, :, 1536:3072], halves[1], *TRANSPOSED)

        def body(i, at, gain_sum, shift_sum):
            r, half, pos = token_block(i)
            norm, inv = normal(m.res_mid[at, :])
            dn = m.d_norm[at, :]
            dn_norm = dn * norm
            g, gn = dn * m.par[3:4, :], dn_norm * m.par[3:4, :]
            back_in = inv * (g - jnp.mean(g, -1, keepdims=True) - norm * jnp.mean(gn, -1, keepdims=True))
            d_mid = m.cot[me, r, half, pos, :].astype(F32) + back_in
            m.res_mid[at, :] = d_mid
            m.d_branch[me, at, :] = d_mid.astype(BF16)
            return gain_sum + folded(dn_norm), shift_sum + folded(dn)

        zero = jnp.zeros((8, WIDTH), F32)
        gain_sum, shift_sum = by_rows(32, body, zero, zero)
        m.sums[3:4, :] = jnp.sum(gain_sum, 0, keepdims=True)
        m.sums[4:5, :] = jnp.sum(shift_sum, 0, keepdims=True)
        wires.start(m.d_branch.at[me], m.d_branch.at[me], twin_base + 9, p.twin)
        d_branch = m.d_branch[me]
        m.sums[2:3, :] = column_sums(d_branch)
        d_att = contract(d_branch[:, 0:PART], out_half(0), *TRANSPOSED) + contract(d_branch[:, PART:], out_half(1), *TRANSPOSED)
        m.normed2[...] = d_att.astype(BF16)

    def out_grad():
        wires.arrived(m.to.at[twin], twin_base + 1)
        wires.arrived(m.d_branch.at[twin], twin_base + 9)
        outs.begin(left_of(m.to), [m.d_branch[core] for core in (0, 1)])

    def attention_back(first, last):
        def body(i, _):
            rows, (cq, ck, cv) = at_pair(i)
            q2, k, v = two_heads(m.qkv[rows, cq]), m.qkv[rows, ck], m.qkv[rows, cv]
            da2 = two_heads(m.normed2[rows, cq])
            probs = m.probs[i]
            d_probs = contract(da2, v, *TRANSPOSED)
            delta = jnp.sum(probs * d_probs, -1, keepdims=True)
            d_scores = (probs * (d_probs - delta)).astype(BF16)
            m.d_proj[me, rows, cq] = (contract(side_by_side(d_scores), two_heads(k), (1,), (0,)) * scale).astype(BF16)
            m.d_proj[me, rows, ck] = (contract(d_scores, q2, *TOKEN_SUM) * scale).astype(BF16)
            m.d_proj[me, rows, cv] = contract(probs.astype(BF16), da2, *TOKEN_SUM).astype(BF16)
            return 0

        lax.fori_loop(first, last, body, 0)

    def proj_out():
        for i in range(3):
            at = m.d_proj.at[me, :, pl.ds(WIDTH * i, WIDTH)]
            wires.start(at, at, twin_base + 10 + i, p.twin)

    def mix_grad(i):
        if i == 0:
            wires.arrived(m.t1.at[twin], twin_base)
        at, wide = mix_plan[i]
        cols, whole = pl.ds(at, wide), pl.ds(at // WIDTH * WIDTH, WIDTH)
        if i < 3:
            if i != 1:
                m.sums[6 + i // 2:7 + i // 2, :] = column_sums(m.d_proj[me, :, whole])
            wires.arrived(m.d_proj.at[twin, :, whole], twin_base + 10 + i)
        mixes[i].begin(left_of(m.t1), [m.d_proj[core, :, cols] for core in (0, 1)])

    def first_norm_back():
        halves = [merged(m.b1[:, :, :, h, :, 0:3 * PART]) for h in (0, 1)]
        m.d_norm[...] = contract(m.d_proj[me, :, 0:3 * PART], halves[0], *TRANSPOSED)
        m.d_norm[...] += contract(m.d_proj[me, :, 3 * PART:], halves[1], *TRANSPOSED)

        def body(i, at, gain_sum, shift_sum, row_sum):
            r, half, pos = token_block(i)
            norm, inv = normal(m.res_in[at, :])
            dn = m.d_norm[at, :]
            dn_norm = dn * norm
            g, gn = dn * m.par[0:1, :], dn_norm * m.par[0:1, :]
            grad = m.res_mid[at, :] + inv * (g - jnp.mean(g, -1, keepdims=True) - norm * jnp.mean(gn, -1, keepdims=True))
            m.ig[r, half, pos, :] = grad
            sums = folded(grad)
            first = (r == 0).astype(F32)
            return (gain_sum + folded(dn_norm), shift_sum + folded(dn),
                    row_sum + jnp.concatenate([sums * first, sums * (1.0 - first)], 0))

        zero = jnp.zeros((8, WIDTH), F32)
        gain_sum, shift_sum, row_sum = by_rows(32, body, zero, zero, jnp.zeros((16, WIDTH), F32))
        m.sums[0:1, :] = jnp.sum(gain_sum, 0, keepdims=True)
        m.sums[1:2, :] = jnp.sum(shift_sum, 0, keepdims=True)
        for r in (0, 1):
            total = jnp.sum(row_sum[8 * r:8 * r + 8], 0, keepdims=True)
            for half in (0, 1):
                m.tg[half, r:r + 1, :] = total[:, PART * half:PART * half + PART]
        ig_copy.start()
        m.ig_send[...] = m.ig[:, 1 - p.y].astype(BF16)
        wires.start(m.ig_send, ig_there, back + 1, p.y_peer)
        tg_copy.start()
        wires.start(m.tg.at[1 - p.y], tg_out.at[p.y], back + 2, p.y_peer)

    totals = SmallScatter(wires, p, m.slabs, m.from_twin, m.s1_s, m.r1_s, m.s2_s, m.r2_s, m.sz_s, m.rz_s, o_small)

    def small_out():
        put_slabs(m.slabs, m.sums[...])
        totals.to_twin()

    small_copy.wait()
    for copy in locs[:3]:
        copy.wait()
    params.after_z()
    z_step(0)
    params.after_near()
    last.forward()
    z_step(1)
    near_step(0)
    params.after_far()
    z_step(2)
    near_step(1)
    first_norm()
    far_step(0)
    projected(0)
    z_step(3)
    near_step(2)
    far_step(1)
    projected(1)
    cot_whole()
    z_step(4)
    near_step(3)
    far_step(2)
    projected(2)
    attention(0, 4)
    z_step(5)
    near_step(4)
    attention(4, 8)
    far_step(3)
    attention(8, 12)
    z_step(6)
    last.along_z()
    near_step(5)
    branch()
    far_step(4)
    up_part(0)
    z_step(7)
    near_step(6)
    far_step(5)
    up_part(1)
    z_step(8)
    near_step(7)
    far_step(6)
    up_part(2)
    z_step(9)
    near_step(8)
    far_step(7)
    up_part(3)
    act_out()
    down_grad(0)
    near_step(9)
    down_grad(1)
    down[1].launch()
    down_grad(2)
    down[2].launch()
    far_step(8)
    down[1].after_far()
    layer_result(0)
    far_step(9)
    down[2].after_far()
    layer_result(1)
    last.after_z()
    hidden_grad(0)
    hidden_grad(1)
    up_grad(0)
    ups[0].launch()
    down[1].after_near()
    hidden_grad(2)
    up_grad(1)
    ups[1].launch()
    hidden_grad(3)
    up_grad(2)
    ups[2].launch()
    down[2].after_near()
    up_grad(3)
    layer_result(2)
    result_out()
    second_norm_back()
    ups[0].after_far()
    ups[3].launch()
    down[1].after_z()
    attention_back(0, 3)
    out_grad()
    ups[1].after_far()
    outs.launch()
    attention_back(3, 6)
    ups[0].after_near()
    down[2].after_z()
    attention_back(6, 9)
    down[0].after_z()
    ups[2].after_far()
    attention_back(9, 12)
    ups[1].after_near()
    proj_out()
    mix_grad(0)
    mixes[0].launch()
    mix_grad(1)
    ups[3].after_far()
    mixes[1].launch()
    ups[2].after_near()
    ups[0].after_z()
    mix_grad(2)
    mix_grad(3)
    down[0].after_far()
    first_norm_back()
    small_out()
    outs.after_far()
    mixes[2].launch()
    ups[3].after_near()
    ups[1].after_z()
    totals.begin()
    down[0].after_near()
    mixes[0].after_far()
    mixes[3].launch()
    outs.after_near()
    ups[2].after_z()
    mixes[1].after_far()
    mixes[0].after_near()
    ups[3].after_z()
    mixes[2].after_far()
    totals.after_far()
    mixes[1].after_near()
    outs.after_z()
    mixes[3].after_far()
    mixes[2].after_near()
    mixes[0].after_z()
    totals.after_near()
    mixes[3].after_near()
    for s in mixes[1:]:
        s.after_z()
    totals.after_z()
    wires.arrived(lo_out.at[rows_own], back)
    wires.arrived(ig_there, back + 1)
    wires.arrived(tg_out.at[p.y], back + 2)
    for copy in (lo_copy, ig_copy, tg_copy):
        copy.wait()
    wires.finish()


def results_kernel(mix, out, up, down, lo, ig, ig_there, tg, small, lo_out, ig_out, time_out, *rest):
    gain1, shift1, o_mix, mbias, o_out, obias, gain2, shift2, o_up, ubias, o_down, dbias, wide, sem = rest
    y = lax.axis_index(SEQ)
    pairs = [(mix, o_mix), (out, o_out), (up, o_up), (down, o_down), (lo, lo_out), (ig, ig_out.at[pl.ds(2 * y, 2)])]
    copies = [pltpu.make_async_copy(src, dst, sem.at[i]) for i, (src, dst) in enumerate(pairs)]
    wide[...] = ig_there[...].astype(F32)
    copies.append(pltpu.make_async_copy(wide, ig_out.at[pl.ds(2 - 2 * y, 2)], sem.at[len(pairs)]))
    for copy in copies:
        copy.start()
    time_out[...] = jnp.concatenate([tg[0, 0:2], tg[1, 0:2]], 0)
    first = 0
    for ref in (gain1, shift1, obias, gain2, shift2, dbias, mbias, ubias):
        count = ref.shape[0] // PIECE
        ref[...] = jnp.concatenate([small[first + i:first + i + 1, :PIECE] for i in range(count)], 1)[0]
        first += count
    for copy in copies:
        copy.wait()


def in_one_kernel(inputs, time_embed, segment_ids, cotangent, gain1, shift1, mix, mbias, out, obias, gain2, shift2, up, ubias,
                  down, dbias):
    table = scratch_table(SLOTS)
    anywhere, vmem = pl.BlockSpec(memory_space=pl.ANY), pl.BlockSpec(memory_space=pltpu.VMEM)
    shape = jax.ShapeDtypeStruct
    tokens = inputs.shape
    here = (tokens[0] // 2,) + tokens[1:]
    g_mix, g_out, g_up, g_down, small, lo, ig, ig_there, tg = pl.pallas_call(
        partial(layer_kernel, [name for name, _, _ in table]),
        out_shape=[shape(w.shape, F32) for w in (mix, out, up, down)]
        + [shape((16, 128), F32), shape(tokens, BF16), shape(here, F32), shape(here, BF16), shape((2, 8, PART), F32)],
        in_specs=[vmem] * 14 + [anywhere] * 2,
        out_specs=[vmem] * 5 + [anywhere] * 4,
        scratch_shapes=[pltpu.SemaphoreType.DMA(shape) if kind is None else pltpu.VMEM(shape, kind) for _, shape, kind in table],
        compiler_params=pltpu.CompilerParams(collective_id=0, has_side_effects=True, vmem_limit_bytes=60 * 2**20),
    )(mix, out, up, down, gain1, shift1, obias, gain2, shift2, dbias, mbias, ubias, time_embed, segment_ids, inputs, cotangent)
    params = (gain1, shift1, mix, mbias, out, obias, gain2, shift2, up, ubias, down, dbias)
    return tuple(pl.pallas_call(
        results_kernel,
        out_shape=[shape(tokens, BF16), shape(tokens, F32), shape((tokens[0], PART), F32)] + [shape(w.shape, F32) for w in params],
        in_specs=[vmem] * 9,
        out_specs=[anywhere] * 2 + [vmem] + [anywhere if w.ndim == 2 else vmem for w in params],
        scratch_shapes=[pltpu.VMEM(here, F32), pltpu.SemaphoreType.DMA((7,))],
    )(g_mix, g_out, g_up, g_down, lo, ig, ig_there, tg, small))


def solution(mesh):
    fits = mesh.shape[BATCH] == 16 and mesh.shape[SEQ] == 2
    tokens, rows, vector, matrix = P(BATCH, SEQ, None), P(BATCH, None), P(AXES), P(AXES, None)
    params = (vector, vector, matrix, vector, matrix, vector, vector, vector, matrix, vector, matrix, vector)
    return jax.shard_map(
        in_one_kernel if fits else any_mesh,
        mesh=mesh,
        in_specs=(tokens, rows, rows, tokens) + params,
        out_specs=(tokens, tokens, P(BATCH, SEQ)) + params,
        check_vma=False,
    )
```
